32 devices in a mesh: dp: 4 (over y, x), expert: 8 (over z, core).
Axes of the slice: x: 2, y: 2, z: 4, core: 2. Of those that a mesh axis runs over, the one named last changes fastest.
Arguments:
- tokens: bfloat16 [4, 1024, 1280], P('dp', 'expert'), may hold values from -6 to 6
- cotangent: bfloat16 [4, 1024, 1280], P('dp', 'expert'), may hold values from -6 to 6
- attn_gain: bfloat16 [1280], P('expert'), may hold values from 0.099609375 to 1.8984375
- ffn_gain: bfloat16 [1280], P('expert'), may hold values from 0.099609375 to 1.8984375
- w_query: bfloat16 [1280, 1280], P('expert'), may hold values from -0.15625 to 0.15625
- w_key: bfloat16 [1280, 1280], P('expert'), may hold values from -0.15625 to 0.15625
- w_value: bfloat16 [1280, 1280], P('expert'), may hold values from -0.15625 to 0.15625
- w_output: bfloat16 [1280, 1280], P('expert'), may hold values from -2.5 to 2.5
- router: bfloat16 [1280, 16], P('expert'), may hold values from -0.078125 to 0.078125
- shared_gate: bfloat16 [1280, 896], P('expert'), may hold values from -0.15625 to 0.15625
- shared_up: bfloat16 [1280, 896], P('expert'), may hold values from -0.15625 to 0.15625
- shared_down: bfloat16 [896, 1280], P('expert'), may hold values from -0.1875 to 0.1875
- expert_gate: bfloat16 [16, 1280, 896], P('expert'), may hold values from -0.15625 to 0.15625
- expert_up: bfloat16 [16, 1280, 896], P('expert'), may hold values from -0.15625 to 0.15625
- expert_down: bfloat16 [16, 896, 1280], P('expert'), may hold values from -12 to 12
- expert_ids: int32 [32, 128, 6], P(('dp', 'expert')), may hold values from 0 to 15, all different within a row; in each aligned block of 128 rows (0 to 127, 128 to 255, ..., all dimensions but the last counted through in order) at most 96 rows name the same one
Outputs:
- layer_output: bfloat16 [4, 1024, 1280], P('dp', 'expert')
- input_grad: bfloat16 [4, 1024, 1280], P('dp', 'expert')
- attn_gain_grad: float32 [1280], P('expert')
- ffn_gain_grad: float32 [1280], P('expert')
- query_grad: float32 [1280, 1280], P('expert')
- key_grad: float32 [1280, 1280], P('expert')
- value_grad: float32 [1280, 1280], P('expert')
- output_grad: float32 [1280, 1280], P('expert')
- router_grad: float32 [1280, 16], P('expert')
- shared_gate_grad: float32 [1280, 896], P('expert')
- shared_up_grad: float32 [1280, 896], P('expert')
- shared_down_grad: float32 [896, 1280], P('expert')
- expert_gate_grad: float32 [16, 1280, 896], P('expert')
- expert_up_grad: float32 [16, 1280, 896], P('expert')
- expert_down_grad: float32 [16, 896, 1280], P('expert')
The draws below stay inside these ranges and needn't reach their ends.
Inputs may be any that keep to these rules, and one draw needn't show every extreme that they name: `expert_ids`: in each block of 128 rows (one value of the first dimension) no expert is named more than 96 times, a bound that some block reaches; the 6 ids of a token differ.
All inputs are finite; a program needn't handle non-finite values.
Results may differ from the reference program's by a relative error of at most 0.02.
Values may be sent and summed in bfloat16 or wider, within the bound.
A program may use at most 320 MiB of HBM per device.

```python
import math
import jax
import jax.numpy as jnp
import numpy as np
from jax import lax

D = 1280
HEADS = 10
HEAD_DIM = 128
FF = 896
TOP = 6
TOK_DEV = 128
EXPERTS = 16
LENGTH = 1024
SEQS = 1
SEQ_ALL = 4
POS_DEV = 128
CAP = 96
N_DP = 4
N_EXPERT = 8
DEVICES = 32


def shard_levels(stream_key, extent, cuts, low, largest):
    def one(position, shards_of):
        steps = jax.random.uniform(jax.random.fold_in(jax.random.fold_in(stream_key, 6), position), (shards_of,), jnp.float32, low / len(cuts), largest / len(cuts))
        return jnp.repeat(jnp.exp(steps), extent[position] // shards_of).reshape((-1,) + (1,) * (len(extent) - position - 1))

    loudness = one(*cuts[0])
    for cut in cuts[1:]:
        loudness = loudness * one(*cut)
    return loudness


def assign_block(rng, own, number, rows, amount, top, reach, skew):
    order = jax.random.permutation(rng, amount)
    crowded, usual = load_shares(amount, rows * top, reach, skew, True), load_shares(amount, rows * top, reach, skew, False)
    places = jnp.arange(amount)

    def named(sizes, turn):
        used = int((sizes > 0).sum())
        fixed = max(1, used // 4)
        passed = fixed + (places - fixed + turn * (used - fixed)) % max(1, amount - fixed)
        return jnp.zeros((amount,), jnp.int32).at[order[jnp.where(places < fixed, places, passed)]].set(jnp.asarray(sizes, jnp.int32))

    sizes = jnp.where(number % 4 == 0, named(crowded, number // 4), named(usual, number - number // 4 - 1))
    mixed = jax.random.permutation(jax.random.fold_in(own, 3), amount)
    donor, receiver = mixed[0:amount // 2 * 2:2], mixed[1:amount // 2 * 2:2]
    margin = jnp.minimum(sizes[donor] - 1, reach - sizes[receiver]) // 2
    margin = jnp.where((donor == order[0]) | (receiver == order[0]) | (sizes[receiver] == 0), 0, jnp.maximum(margin, 0))
    passed = jax.random.randint(jax.random.fold_in(own, 4), (amount // 2,), 0, 1 << 20) % (margin + 1)
    sizes = sizes.at[donor].add(-passed).at[receiver].add(passed)
    labels = jnp.searchsorted(jnp.cumsum(sizes), jnp.arange(rows * top), side="right").astype(jnp.int32)
    table = labels.reshape(top, rows).T
    table = table[jax.random.permutation(jax.random.fold_in(own, 1), rows)]
    turn = jax.random.randint(jax.random.fold_in(own, 2), (rows, 1), 0, top)
    return jnp.take_along_axis(table, (jnp.arange(top)[None, :] + turn) % top, axis=1)


def load_shares(count, total, limit, lean, full):
    loads = [(1 << 20) // math.isqrt(rank ** lean) + 1 for rank in range(1, count + 1)]
    largest = limit if full else min(limit, max(-(-total // count), total * loads[0] // sum(loads)))
    least = 1 if total - largest >= count - 1 else 0
    holding, rest = [largest] + [least] * (count - 1), total - largest - least * (count - 1)
    while rest > 0:
        candidates = [i for i in range(1, count) if holding[i] < largest] or [i for i in range(1, count) if holding[i] < limit]
        mass, left = sum([loads[i] for i in candidates]), rest
        for i in candidates:
            more = min(limit - holding[i], max(1, left * loads[i] // mass), rest)
            holding[i] = holding[i] + more
            rest = rest - more
    return np.array(holding)


def normal_values(stream_key, shape, width, reach, shards=(), kind=jnp.bfloat16):
    gain = shard_levels(stream_key, shape, shards, -0.22, 0.18) if shards else 1.0
    drawn = jax.random.normal(stream_key, shape, jnp.float32) * width * gain
    return jnp.minimum(jnp.maximum(drawn, -reach), reach).astype(kind)


def setup_inputs(seed: int = 0) -> dict:
    arg_keys = jax.random.split(jax.random.key(seed), 17)
    tokens = normal_values(arg_keys[0], (SEQ_ALL, LENGTH, D), 1.0, 6.0, ((0, 4), (1, 8)))
    cotangent = normal_values(arg_keys[1], (SEQ_ALL, LENGTH, D), 1.0, 6.0, ((0, 4), (1, 8)))
    attn_gain = jnp.clip(1.0 + 0.18 * jax.random.normal(arg_keys[2], (D,), jnp.float32), 0.099609375, 1.8984375).astype(jnp.bfloat16)
    ffn_gain = jnp.clip(1.0 + 0.18 * jax.random.normal(arg_keys[3], (D,), jnp.float32), 0.099609375, 1.8984375).astype(jnp.bfloat16)
    w_query = normal_values(arg_keys[4], (D, D), D ** -0.5, 0.15625, ((0, 8),))
    w_key = normal_values(arg_keys[5], (D, D), D ** -0.5, 0.15625, ((0, 8),))
    w_value = normal_values(arg_keys[6], (D, D), D ** -0.5, 0.15625, ((0, 8),))
    w_output = normal_values(arg_keys[7], (D, D), (max(1, D // 256)) ** -0.5, 2.5, ((0, 8),))
    router = normal_values(arg_keys[8], (D, EXPERTS), (4 * D) ** -0.5, 0.078125, ((0, 8),))
    shared_gate = normal_values(arg_keys[9], (D, FF), D ** -0.5, 0.15625, ((0, 8),))
    shared_up = normal_values(arg_keys[10], (D, FF), D ** -0.5, 0.15625, ((0, 8),))
    shared_down = normal_values(arg_keys[11], (FF, D), FF ** -0.5, 0.1875, ((0, 8),))
    expert_gate = normal_values(arg_keys[12], (EXPERTS, D, FF), D ** -0.5, 0.15625, ((0, 8),))
    expert_up = normal_values(arg_keys[13], (EXPERTS, D, FF), D ** -0.5, 0.15625, ((0, 8),))
    expert_down = normal_values(arg_keys[14], (EXPERTS, FF, D), 2.0, 12.0, ((0, 8),))
    expert_ids_keys = jax.random.split(jax.random.fold_in(arg_keys[15], 1), DEVICES * TOK_DEV // TOK_DEV)
    expert_ids_turns = jax.random.permutation(jax.random.fold_in(arg_keys[15], 3), DEVICES * TOK_DEV // TOK_DEV)
    expert_ids = jax.vmap(lambda own, number: assign_block(jax.random.fold_in(arg_keys[15], 2), own, number, TOK_DEV, EXPERTS, TOP, CAP, 2))(expert_ids_keys, expert_ids_turns).reshape((DEVICES, TOK_DEV, TOP))
    return {"tokens": tokens, "cotangent": cotangent, "attn_gain": attn_gain, "ffn_gain": ffn_gain, "w_query": w_query, "w_key": w_key, "w_value": w_value, "w_output": w_output, "router": router, "shared_gate": shared_gate, "shared_up": shared_up, "shared_down": shared_down, "expert_gate": expert_gate, "expert_up": expert_up, "expert_down": expert_down, "expert_ids": expert_ids}


@jax.custom_vjp
def low(v):
    return lax.optimization_barrier(v.astype(jnp.bfloat16)).astype(jnp.float32)

@jax.custom_vjp
def low_back(v):
    return v

def low_keep(v):
    return (low(v), None)

def low_pass(kept, grad):
    return (grad,)

def back_keep(v):
    return (v, None)

def back_low(kept, grad):
    return (low(grad),)
low.defvjp(low_keep, low_pass)
low_back.defvjp(back_keep, back_low)
norm_eps = 1e-06
masked_score = -1e+30
highest_precision = lax.Precision.HIGHEST

def matmul(left, right):
    return jnp.dot(left, right, precision=highest_precision, preferred_element_type=jnp.float32)

def rotary_tables(positions, head_size):
    half_size = head_size // 2
    inverse_freq = 10000.0 ** (-jnp.arange(half_size, dtype=jnp.float32) * 2.0 / head_size)
    angles = positions.astype(jnp.float32)[:, None] * inverse_freq[None, :]
    cosine = jnp.cos(angles)
    sine_part = jnp.sin(angles)
    return (jnp.concatenate([cosine, cosine], -1)[:, None, :], jnp.concatenate([sine_part, sine_part], -1)[:, None, :])

def rotate(values, cosine, sine_part):
    half_size = values.shape[-1] // 2
    turned = jnp.concatenate([-values[..., half_size:], values[..., :half_size]], -1)
    return values * cosine + turned * sine_part

def to_devices(values):
    last_width = values.shape[-1]
    grouped = values.reshape(N_DP, SEQS, N_EXPERT, POS_DEV, last_width)
    return grouped.transpose(0, 2, 1, 3, 4).reshape(DEVICES, TOK_DEV, last_width)

def from_devices(values):
    last_width = values.shape[-1]
    grouped = values.reshape(N_DP, N_EXPERT, SEQS, POS_DEV, last_width)
    return grouped.transpose(0, 2, 1, 3, 4).reshape(SEQ_ALL, LENGTH, last_width)

def attend(packed):
    queries, keys_in, values_in = packed
    raw = jnp.einsum('qhd,khd->hqk', queries, keys_in, precision=highest_precision)
    scores = low_back(raw * HEAD_DIM ** (-0.5))
    allowed = jnp.arange(LENGTH)[None, :] <= jnp.arange(LENGTH)[:, None]
    scores = jnp.where(allowed[None], scores, masked_score)
    weights = jax.nn.softmax(scores, axis=-1)
    mixed = jnp.einsum('hqk,khd->qhd', low(weights), values_in, precision=highest_precision)
    return low(low_back(mixed))

def experts_block(packed, expert_gate, expert_up, expert_down):
    rows_in, prob_rows, route_ids = packed
    flat_ids = route_ids.reshape(-1)
    flags = (flat_ids[:, None] == jnp.arange(EXPERTS)[None, :]).astype(jnp.int32)
    earlier = jnp.cumsum(flags, 0) - flags
    slots = lax.optimization_barrier(jnp.sum(earlier * flags, 1))
    targets = flat_ids * CAP + slots
    buffer = jnp.zeros((EXPERTS * CAP, D), rows_in.dtype).at[targets].set(jnp.repeat(rows_in, TOP, 0))
    buffer = low_back(buffer).reshape(EXPERTS, CAP, D)
    gate_hidden = low_back(jnp.einsum('ecd,edf->ecf', buffer, expert_gate, precision=highest_precision))
    up_hidden = low_back(jnp.einsum('ecd,edf->ecf', buffer, expert_up, precision=highest_precision))
    activated = low(jax.nn.silu(gate_hidden) * up_hidden)
    produced = low(low_back(jnp.einsum('ecf,efd->ecd', activated, expert_down, precision=highest_precision)))
    picked = produced.reshape(EXPERTS * CAP, D)[targets].reshape(TOK_DEV, TOP, D)
    gate_vals = jnp.take_along_axis(prob_rows, route_ids, 1)
    return lax.optimization_barrier(jnp.sum(gate_vals[..., None] * picked, 1))

def layer(inputs, attn_gain, ffn_gain, w_query, w_key, w_value, w_output, router, shared_gate, shared_up, shared_down, expert_gate, expert_up, expert_down, expert_ids):
    rows_flat = inputs.reshape(SEQ_ALL * LENGTH, D)
    inverse_one = lax.rsqrt(lax.optimization_barrier(jnp.mean(rows_flat * rows_flat, -1, keepdims=True)) + norm_eps)
    normed_one = low(rows_flat * inverse_one * attn_gain)
    shaped = (SEQ_ALL, LENGTH, HEADS, HEAD_DIM)
    query = low_back(matmul(normed_one, w_query)).reshape(shaped)
    keyed = low_back(matmul(normed_one, w_key)).reshape(shaped)
    valued = low_back(matmul(normed_one, w_value)).reshape(shaped)
    cosine, sine_part = rotary_tables(jnp.arange(LENGTH), HEAD_DIM)
    query = low(rotate(query, cosine, sine_part))
    keyed = low(rotate(keyed, cosine, sine_part))
    valued = low(valued)
    mixed = lax.map(jax.checkpoint(attend), (query, keyed, valued))
    attended = low_back(matmul(mixed.reshape(SEQ_ALL * LENGTH, D), w_output))
    resid = rows_flat + attended
    inverse_two = lax.rsqrt(lax.optimization_barrier(jnp.mean(resid * resid, -1, keepdims=True)) + norm_eps)
    normed_two = low(resid * inverse_two * ffn_gain)
    logits = low_back(matmul(normed_two, router))
    probs = jax.nn.softmax(logits, axis=-1)
    gate_shared = low_back(matmul(normed_two, shared_gate))
    up_shared = low_back(matmul(normed_two, shared_up))
    hidden_shared = low(jax.nn.silu(gate_shared) * up_shared)
    shared_out = low_back(matmul(hidden_shared, shared_down))

    def block_fn(packed):
        return experts_block(packed, expert_gate, expert_up, expert_down)
    routed = lax.map(jax.checkpoint(block_fn), (to_devices(normed_two.reshape(SEQ_ALL, LENGTH, D)), to_devices(probs.reshape(SEQ_ALL, LENGTH, EXPERTS)), expert_ids))
    routed = from_devices(routed).reshape(SEQ_ALL * LENGTH, D)
    return (resid + shared_out + routed).reshape(SEQ_ALL, LENGTH, D)

def reference(tokens, cotangent, attn_gain, ffn_gain, w_query, w_key, w_value, w_output, router, shared_gate, shared_up, shared_down, expert_gate, expert_up, expert_down, expert_ids):
    floats = [member.astype(jnp.float32) for member in (tokens, attn_gain, ffn_gain, w_query, w_key, w_value, w_output, router, shared_gate, shared_up, shared_down, expert_gate, expert_up, expert_down)]

    def closed(*values):
        return layer(*values, expert_ids)
    produced, pullback = jax.vjp(closed, *floats)
    grads = pullback(cotangent.astype(jnp.float32))
    return (produced.astype(jnp.bfloat16), grads[0].astype(jnp.bfloat16), grads[1], grads[2], grads[3], grads[4], grads[5], grads[6], grads[7], grads[8], grads[9], grads[10], grads[11], grads[12], grads[13])
```

```python
import functools

import jax
import jax.numpy as jnp
from jax import lax
from jax.experimental import pallas as pl
from jax.experimental.pallas import tpu as pltpu
from jax.sharding import PartitionSpec as P

HEAD_DIM = 128
LANES = 128
EPS = 1e-06
MASKED = -1e30
VMEM_LIMIT = 60 * 2**20
BF = jnp.bfloat16
F32 = jnp.float32


def dot(a, b):
    return jnp.dot(a, b, preferred_element_type=F32)


def dot_nt(a, b):
    return lax.dot_general(a, b, (((1,), (1,)), ((), ())), preferred_element_type=F32)


def dot_tn(a, b):
    return lax.dot_general(a, b, (((0,), (0,)), ((), ())), preferred_element_type=F32)


def silu(v):
    return v / (1.0 + jnp.exp(-v))


def swiglu_back(d_hidden, gates, ups):
    sigma = 1.0 / (1.0 + jnp.exp(-gates))
    d_gate = d_hidden * ups * sigma * (1.0 + gates * (1.0 - sigma))
    d_up = d_hidden * (gates * sigma)
    return d_gate.astype(BF), d_up.astype(BF)


def rotary_tables(length):
    half = HEAD_DIM // 2
    inverse_freq = 10000.0 ** (-jnp.arange(half, dtype=F32) * 2.0 / HEAD_DIM)
    angles = jnp.arange(length).astype(F32)[:, None] * inverse_freq[None, :]
    cosine, sine = jnp.cos(angles), jnp.sin(angles)
    return jnp.concatenate([cosine, cosine], -1), jnp.concatenate([-sine, sine], -1)


def vmem_call(kernel, outs, *args, remote_id=None, **kwargs):
    spec = pl.BlockSpec(memory_space=pltpu.VMEM)
    params = {} if remote_id is None else {"collective_id": remote_id, "has_side_effects": True}
    return pl.pallas_call(
        kernel,
        out_shape=outs,
        in_specs=[spec] * len(args),
        out_specs=[spec] * len(outs),
        compiler_params=pltpu.CompilerParams(vmem_limit_bytes=VMEM_LIMIT, **params),
        **kwargs,
    )(*args)


def row_block(length):
    return 256 if length % 256 == 0 else length


def remote(src, dst, send, recv, **device):
    return pltpu.make_async_remote_copy(
        src_ref=src, dst_ref=dst, send_sem=send, recv_sem=recv, device_id=device, device_id_type=pl.DeviceIdType.MESH
    )


def meet(peers):
    barrier = pltpu.get_barrier_semaphore()
    for peer in peers:
        pl.semaphore_signal(barrier, inc=1, device_id=peer, device_id_type=pl.DeviceIdType.MESH)
    pl.semaphore_wait(barrier, len(peers))


def meet_near(chips, z, me, peers=()):
    barrier = pltpu.get_barrier_semaphore()
    near = [(True, {"expert": me + 1 - 2 * lax.rem(me, 2)}), (z > 0, {"expert": me - 2}), (z < chips - 1, {"expert": me + 2})]
    near += [(True, {"dp": t}) for t in peers]

    def signal(t):
        pl.semaphore_signal(barrier, inc=1, device_id=t, device_id_type=pl.DeviceIdType.MESH)

    for ok, t in near:
        guarded(ok, functools.partial(signal, t))
    ends = jnp.where(z > 0, 1, 0) + jnp.where(z < chips - 1, 1, 0)
    pl.semaphore_wait(barrier, 1 + len(peers) + ends)


def both(*conditions):
    held = [c for c in conditions if c is not True]
    if not held:
        return True
    out = held[0]
    for c in held[1:]:
        out = jnp.logical_and(out, c)
    return out


def guarded(condition, action):
    if condition is True:
        action()
    else:
        pl.when(condition)(action)


class LineGather:
    def __init__(self, ranks, own, block, send, recv, base=0, valid=lambda i: True, twins=True):
        self.me = lax.axis_index("expert")
        self.chips = ranks // 2
        self.z = self.me // 2
        self.twin = self.me + 1 - 2 * lax.rem(self.me, 2)
        self.own, self.block, self.send, self.recv, self.base, self.valid = own, block, send, recv, base, valid
        self.twins = twins

    @staticmethod
    def semaphores(ranks):
        return 4 * (ranks // 2 - 1) + 1

    def copy(self, src, i, k, to):
        return remote(src, self.block(i), self.send.at[self.base + k], self.recv.at[self.base + k], expert=to)

    def sources(self, s):
        hops = self.chips - 1
        return (
            (self.me - 2 * s, self.z - s >= 0, self.z < hops, self.me + 2, 0, 2 * hops, -2 * s),
            (self.me + 2 * s, self.z + s <= hops, self.z > 0, self.me - 2, hops, 3 * hops, 2 * s),
        )

    def start(self):
        hops = self.chips - 1
        mine = self.valid(self.me)
        if hops:
            guarded(both(self.z < hops, mine), lambda: self.copy(self.own, self.me, 0, self.me + 2).start())
            guarded(both(self.z > 0, mine), lambda: self.copy(self.own, self.me, hops, self.me - 2).start())
        if self.twins:
            guarded(mine, lambda: self.copy(self.own, self.me, 2 * hops, self.twin).start())

    def step(self, s):
        for i, there, more, to, k, pair, _ in self.sources(s):
            known = both(there, self.valid(i))
            src = self.block(i)
            guarded(known, lambda: self.copy(src, i, k + s - 1, self.twin).wait_recv())
            if s < self.chips - 1:
                guarded(both(known, more), lambda: self.copy(src, i, k + s, to).start())
            if self.twins:
                guarded(known, lambda: self.copy(src, i, pair + s, self.twin).start())

    def finish(self):
        hops = self.chips - 1
        mine = self.valid(self.me)
        theirs = self.valid(self.twin)
        if self.twins:
            guarded(mine, lambda: self.copy(self.own, self.me, 2 * hops, self.twin).wait_send())
            guarded(theirs, lambda: self.copy(self.own, self.twin, 2 * hops, self.twin).wait_recv())
        if hops:
            guarded(both(self.z < hops, mine), lambda: self.copy(self.own, self.me, 0, self.twin).wait_send())
            guarded(both(self.z > 0, mine), lambda: self.copy(self.own, self.me, hops, self.twin).wait_send())
        for s in range(1, self.chips):
            for i, there, more, to, k, pair, shift in self.sources(s):
                known = both(there, self.valid(i))
                src = self.block(i)
                if s < hops:
                    guarded(both(known, more), lambda: self.copy(src, i, k + s, self.twin).wait_send())
                if not self.twins:
                    continue
                guarded(known, lambda: self.copy(src, i, pair + s, self.twin).wait_send())
                j = self.twin + shift
                got = both(there, self.valid(j))
                guarded(got, lambda: self.copy(self.block(j), j, pair + s, self.twin).wait_recv())


class Across:
    SEMAPHORES = 12

    def __init__(self, source, dst, send, recv):
        self.me, self.g = lax.axis_index("expert"), lax.axis_index("dp")
        self.twin = self.me + 1 - 2 * lax.rem(self.me, 2)
        self.by_x = self.g + 1 - 2 * lax.rem(self.g, 2)
        self.by_y = lax.rem(self.g + 2, 4)
        self.source, self.dst, self.send, self.recv = source, dst, send, recv
        self.half = dst.shape[1]
        self.part = self.half // 2

    def peers(self):
        return [{"dp": self.by_x}, {"dp": self.by_y}, {"expert": self.twin}]

    def piece(self, slot, j):
        return self.dst.at[slot, pl.ds(j * self.part, self.part)]

    def mine(self, j):
        first = lax.rem(self.me, 2) * self.half + j * self.part
        return self.source(pl.ds(pl.multiple_of(first, self.part), self.part))

    def copy(self, k, src, dst, **to):
        return remote(src, dst, self.send.at[k], self.recv.at[k], **to)

    def direct(self, k):
        slot, j, to = ((0, 0, self.by_x), (1, 1, self.by_y), (0, 1, self.by_x), (1, 0, self.by_y))[k]
        return self.copy(k, self.mine(j), self.piece(slot, j), dp=to)

    def relayed(self, j):
        if j == 0:
            return self.copy(4, self.piece(0, 0), self.piece(2, 0), dp=self.by_y)
        return self.copy(5, self.piece(1, 1), self.piece(2, 1), dp=self.by_x)

    def shared(self, slot, j):
        return self.copy(6 + 2 * slot + j, self.piece(slot, j), self.piece(slot + 3, j), expert=self.twin)

    def start(self):
        for k in range(4):
            self.direct(k).start()

    def relay(self):
        self.direct(0).wait_recv()
        self.relayed(0).start()
        self.direct(1).wait_recv()
        self.relayed(1).start()
        self.shared(0, 0).start()
        self.shared(1, 1).start()

    def hand_over(self):
        self.direct(2).wait_recv()
        self.shared(0, 1).start()
        self.direct(3).wait_recv()
        self.shared(1, 0).start()

    def finish(self):
        for j in range(2):
            self.relayed(j).wait_recv()
            self.shared(2, j).start()
        for k in range(4):
            self.direct(k).wait_send()
        for j in range(2):
            self.relayed(j).wait_send()
            for slot in range(3):
                self.shared(slot, j).wait()


class SameExperts:
    SEMAPHORES = 6

    def __init__(self, source, dst, send, recv):
        self.me, self.g = lax.axis_index("expert"), lax.axis_index("dp")
        self.near = [self.g + 1 - 2 * lax.rem(self.g, 2), lax.rem(self.g + 2, 4)]
        self.near.append(self.near[1] + 1 - 2 * lax.rem(self.near[1], 2))
        self.source, self.dst, self.send, self.recv = source, dst, send, recv
        self.half = dst.shape[1]

    def peers(self):
        return [{"dp": self.near[2]}]

    def copy(self, k, h):
        slot = k + 3 * lax.rem(lax.rem(self.me, 2) + h, 2)
        i = 2 * k + h
        src = self.source.at[pl.ds(h * self.half, self.half)]
        return remote(src, self.dst.at[slot], self.send.at[i], self.recv.at[i], dp=self.near[k])

    def start(self):
        for k in range(3):
            for h in range(2):
                self.copy(k, h).start()

    def relay(self):
        pass

    hand_over = relay

    def finish(self):
        for k in range(3):
            for h in range(2):
                self.copy(k, h).wait()


def aligned(i, size):
    return pl.ds(pl.multiple_of(i * size, size), size)


def front_kernel(
    ranks, groups, heads, slots, x_ref, wq_ref, wk_ref, wv_ref, pack_ref,
    gx_ref, w_ref, stage_ref, land_ref,
    x_send, x_recv, w_send, w_recv, d_send, d_recv,
):
    me, g = lax.axis_index("expert"), lax.axis_index("dp")
    rows = wq_ref.shape[0]
    peers = [lax.rem(g + d, groups) for d in range(1, groups)]
    others = [lax.rem(me + d, ranks) for d in range(1, ranks)]
    meet([{"expert": t} for t in others] + [{"dp": t} for t in peers])

    tokens = LineGather(ranks, x_ref, lambda i: gx_ref.at[i], x_send, x_recv)
    tokens.start()

    def stage_heads(w):
        for u in range(heads):
            stage_ref[u] = w[:, u * LANES : (u + 1) * LANES]

    for which, w in enumerate((wq_ref, wk_ref, wv_ref)):
        pl.when(g == which)(functools.partial(stage_heads, w))

    def stage_pack():
        for s in range(slots):
            stage_ref[pl.ds(s * ranks, ranks)] = pack_ref[:, :, s * LANES : (s + 1) * LANES]

    pl.when(g == groups - 1)(stage_pack)

    def known(s, t, group=None):
        return jnp.logical_or((g if group is None else group) == groups - 1, s * ranks + t < heads)

    def weight_copy(s, d, unit, i, to):
        return remote(
            stage_ref.at[unit], land_ref.at[g, s, i], w_send.at[s, d], w_recv.at[s, d], expert=to
        )

    for d in range(1, ranks):
        t = others[d - 1]
        for s in range(slots):
            guarded(known(s, t), lambda: weight_copy(s, d, s * ranks + t, me, t).start())
    for s in range(slots):
        def keep(s=s):
            land_ref[g, s, me] = stage_ref[s * ranks + me]

        pl.when(known(s, me))(keep)
        for which in range(groups - 1):
            def clear(s=s, which=which):
                land_ref[which, s] = jnp.zeros(land_ref.shape[2:], BF)

            pl.when(s * ranks + me >= heads)(clear)

    gx_ref[me] = x_ref[...]

    def share(s, part, d, to):
        return remote(part, part, d_send.at[s, d], d_recv.at[s, d], dp=to)

    def pass_on(i):
        for s in range(slots):
            part = land_ref.at[g, s, i]
            for d in range(1, groups):
                pl.when(known(s, me))(lambda: share(s, part, d, peers[d - 1]).start())

    pass_on(me)
    steps = ranks // 2 - 1
    taken = 1
    for step in range(1, steps + 1):
        tokens.step(step)
        until = ranks if step == steps else min(ranks, taken + 2)
        for d in range(taken, until):
            i = lax.rem(me + ranks - d, ranks)
            for s in range(slots):
                pl.when(known(s, me))(lambda: weight_copy(s, d, 0, i, others[0]).wait_recv())
            pass_on(i)
        taken = until
    tokens.finish()
    for d in range(1, ranks):
        t = others[d - 1]
        for s in range(slots):
            pl.when(known(s, t))(lambda: weight_copy(s, d, 0, me, t).wait_send())
    for d in range(1, groups):
        there = lax.rem(g + groups - d, groups)
        for s in range(slots):
            pl.when(known(s, me))(lambda: share(s, land_ref.at[g, s], d, peers[d - 1]).wait_send())
            pl.when(known(s, me, there))(lambda: share(s, land_ref.at[there, s], d, peers[d - 1]).wait_recv())
    for which in range(groups):
        for s in range(slots):
            for r in range(ranks):
                w_ref[which, r * rows : (r + 1) * rows, s * LANES : (s + 1) * LANES] = land_ref[which, s, r]


def front(ranks, groups, heads, slots, x, w_query, w_key, w_value, pack):
    own, width = x.shape
    rows = w_query.shape[0]
    line = LineGather.semaphores(ranks)
    dma = pltpu.SemaphoreType.DMA
    spec = pl.BlockSpec(memory_space=pltpu.VMEM)
    shape = jax.ShapeDtypeStruct
    return pl.pallas_call(
        functools.partial(front_kernel, ranks, groups, heads, slots),
        out_shape=[
            shape((ranks, own, width), BF),
            shape((groups, width, slots * LANES), BF),
        ],
        in_specs=[spec] * 5,
        out_specs=[spec] * 2,
        scratch_shapes=[
            pltpu.VMEM((slots * ranks, rows, LANES), BF),
            pltpu.VMEM((groups, slots, ranks, rows, LANES), BF),
            dma((line,)), dma((line,)),
            dma((slots, ranks)), dma((slots, ranks)),
            dma((slots, groups)), dma((slots, groups)),
        ],
        compiler_params=pltpu.CompilerParams(
            collective_id=0, has_side_effects=True, vmem_limit_bytes=VMEM_LIMIT
        ),
        name="front",
    )(x, w_query, w_key, w_value, pack)


def project_kernel(
    ranks, heads, slots, x_ref, mixed_ref, half_ref, gain_ref, c_ref,
    resid_ref, n_ref, all_ref, wo_ref, c_all_ref, other_ref, send, recv, t_send, t_recv, a_send, a_recv,
):
    me = lax.axis_index("expert")
    chips = ranks // 2
    z = me // 2
    share = c_all_ref.shape[-1]
    across = Across(lambda r: c_ref.at[r, pl.ds(0, share)], c_all_ref, a_send, a_recv)
    meet_near(chips, z, me, [across.by_x, across.by_y])
    twin = me + 1 - 2 * lax.rem(me, 2)
    halves = remote(half_ref, other_ref, t_send, t_recv, expert=twin)
    halves.start()
    across.start()
    line = LineGather.semaphores(ranks)
    parts = []
    for s in range(slots):
        def head(i, s=s):
            return aligned(jnp.clip(s * ranks + i, 0, heads - 1), LANES)

        cols = slice(s * LANES, (s + 1) * LANES)
        ok = (lambda i: True) if (s + 1) * ranks <= heads else (lambda i, s=s: s * ranks + i < heads)
        gather = LineGather(
            ranks, mixed_ref.at[:, cols], lambda i, head=head: all_ref.at[:, head(i)], send, recv, s * line, ok
        )
        gather.start()
        parts.append(gather)

        def keep(cols=cols, head=head):
            all_ref[:, head(me)] = mixed_ref[:, cols]

        guarded(ok(me), keep)
    for step in range(1, chips):
        for gather in parts:
            gather.step(step)
    for gather in parts:
        gather.finish()
    across.relay()
    halves.wait()
    groups, per, _, part, _ = half_ref.shape

    def lay_out(even, odd):
        for which in range(groups):
            for k in range(per):
                u = which * per + k
                if u < wo_ref.shape[1] // LANES:
                    cols = slice(u * LANES, (u + 1) * LANES)
                    for c in range(chips):
                        wo_ref[2 * c * part : (2 * c + 1) * part, cols] = even[which, k, c]
                        wo_ref[(2 * c + 1) * part : (2 * c + 2) * part, cols] = odd[which, k, c]

    pl.when(me == 2 * z)(lambda: lay_out(half_ref, other_ref))
    pl.when(me != 2 * z)(lambda: lay_out(other_ref, half_ref))
    blocks, own, width = x_ref.shape
    gain = gain_ref[...]
    tile = 2 if own <= 128 and blocks % 2 == 0 else 1

    def rows_of(b):
        rows = aligned(b, tile * own)
        x = x_ref[pl.ds(b * tile, tile)].reshape(tile * own, width).astype(F32)
        resid = x + dot(all_ref[rows, :], wo_ref[...])
        inverse = lax.rsqrt(jnp.mean(resid * resid, -1, keepdims=True) + EPS)
        n_ref[rows, :] = (resid * inverse * gain).astype(BF)
        for t in range(tile):
            def keep(t=t):
                resid_ref[...] = resid[t * own : (t + 1) * own]

            pl.when(b * tile + t == me)(keep)

    lax.fori_loop(0, blocks // tile, lambda b, c: (rows_of(b), c)[1], 0)
    across.hand_over()
    across.finish()


def project(ranks, heads, slots, x, mixed, half, gain, cot):
    blocks, own, width = x.shape
    total = blocks * own
    line = LineGather.semaphores(ranks)
    dma = pltpu.SemaphoreType.DMA
    spec = pl.BlockSpec(memory_space=pltpu.VMEM)
    anywhere = pl.BlockSpec(memory_space=pl.ANY)
    shape = jax.ShapeDtypeStruct
    return pl.pallas_call(
        functools.partial(project_kernel, ranks, heads, slots),
        out_shape=[
            shape((own, width), F32),
            shape((total, width), BF),
            shape((total, width), BF),
            shape((width, width), BF),
            shape((6, total // 2, width // 2), BF),
        ],
        in_specs=[spec] * 4 + [anywhere],
        out_specs=[spec] * 4 + [anywhere],
        scratch_shapes=[
            pltpu.VMEM(half.shape, BF), dma((slots * line,)), dma((slots * line,)), dma(()), dma(()),
            dma((Across.SEMAPHORES,)), dma((Across.SEMAPHORES,)),
        ],
        compiler_params=pltpu.CompilerParams(
            collective_id=2, has_side_effects=True, vmem_limit_bytes=VMEM_LIMIT
        ),
        name="project",
    )(x, mixed, half, gain, cot)


def attend_kernel(
    ranks, groups, seqs, slots, x_ref, gain_ref, wq_ref, wk_ref, wv_ref, cos_ref, sin_ref, wo_ref,
    inv_ref, q_ref, k_ref, v_ref, mixed_ref, lse_ref, half_ref,
    stage_ref, o_send, o_recv, p_send, p_recv,
):
    total, width = x_ref.shape
    length = total // seqs
    block = row_block(length)
    scale = HEAD_DIM ** (-0.5)

    me, g = lax.axis_index("expert"), lax.axis_index("dp")
    chips, per = half_ref.shape[2], half_ref.shape[1]
    z = me // 2
    peers = [lax.rem(g + d, groups) for d in range(1, groups)]
    meet_near(chips, z, me, peers)
    for which in range(groups):

        def stage(which=which):
            for k in range(per):
                u = which * per + k
                if u < width // LANES:
                    stage_ref[k] = wo_ref[:, u * LANES : (u + 1) * LANES]

        pl.when(g == which)(stage)
    out_rows = LineGather(
        ranks, stage_ref, lambda i: half_ref.at[g, :, i // 2], o_send, o_recv, twins=False
    )
    out_rows.start()
    half_ref[g, :, z] = stage_ref[...]

    def out_share(d, group, to):
        part = half_ref.at[group]
        return remote(part, part, p_send.at[d], p_recv.at[d], dp=to)

    pending = list(range(1, chips))

    def progress():
        if pending:
            out_rows.step(pending.pop(0))
            if not pending:
                out_rows.finish()
                for d in range(1, groups):
                    out_share(d, g, peers[d - 1]).start()

    for s in range(seqs):
        for i in range(length // block):
            rows = pl.ds(s * length + i * block, block)
            x = x_ref[rows, :].astype(F32)
            inv = lax.rsqrt(jnp.mean(x * x, -1, keepdims=True) + EPS)
            normed = (x * inv * gain_ref[...].astype(F32)).astype(BF)
            inv_ref[rows, :] = inv
            cosine = cos_ref[pl.ds(i * block, block), :]
            sine = sin_ref[pl.ds(i * block, block), :]
            queries, keyed, valued = dot(normed, wq_ref[...]), dot(normed, wk_ref[...]), dot(normed, wv_ref[...])
            for h in range(slots):
                cols = slice(h * HEAD_DIM, (h + 1) * HEAD_DIM)
                q, k = queries[:, cols], keyed[:, cols]
                q_ref[rows, cols] = (q * cosine + pltpu.roll(q, HEAD_DIM // 2, 1) * sine).astype(BF)
                k_ref[rows, cols] = (k * cosine + pltpu.roll(k, HEAD_DIM // 2, 1) * sine).astype(BF)
            v_ref[rows, :] = valued.astype(BF)
    progress()
    for s in range(seqs):
        for i in range(length // block):
            if i:
                progress()
            rows = pl.ds(s * length + i * block, block)
            keys = pl.ds(s * length, (i + 1) * block)
            shape = (block, (i + 1) * block)
            seen = (
                lax.broadcasted_iota(jnp.int32, shape, 1)
                <= lax.broadcasted_iota(jnp.int32, shape, 0) + i * block
            )
            for h in range(slots):
                cols = slice(h * HEAD_DIM, (h + 1) * HEAD_DIM)
                scores = dot_nt(q_ref[rows, cols], k_ref[keys, cols]) * scale
                scores = jnp.where(seen, scores, MASKED)
                top = jnp.max(scores, -1, keepdims=True)
                raised = jnp.exp(scores - top)
                totals = jnp.sum(raised, -1, keepdims=True)
                probs = (raised / totals).astype(BF)
                mixed_ref[rows, cols] = dot(probs, v_ref[keys, cols]).astype(BF)
                lse_ref[rows, h : h + 1] = top + jnp.log(totals)
    while pending:
        progress()
    for d in range(1, groups):
        out_share(d, g, peers[d - 1]).wait_send()
        out_share(d, lax.rem(g + groups - d, groups), peers[d - 1]).wait_recv()


def attend(ranks, groups, seqs, slots, x, gain, w_q, w_k, w_v, cosine, sine, w_output):
    total, width = x.shape
    span = slots * HEAD_DIM
    rows = w_output.shape[0]
    per = -(-(width // LANES) // groups)
    line = LineGather.semaphores(ranks)
    dma = pltpu.SemaphoreType.DMA
    shape = jax.ShapeDtypeStruct
    return vmem_call(
        functools.partial(attend_kernel, ranks, groups, seqs, slots),
        [
            shape((total, 1), F32),
            shape((total, span), BF),
            shape((total, span), BF),
            shape((total, span), BF),
            shape((total, span), BF),
            shape((total, slots), F32),
            shape((groups, per, ranks // 2, rows, LANES), BF),
        ],
        x, gain, w_q, w_k, w_v, cosine, sine, w_output,
        scratch_shapes=[
            pltpu.VMEM((per, rows, LANES), BF),
            dma((line,)), dma((line,)),
            dma((groups,)), dma((groups,)),
        ],
        remote_id=1,
        name="attend",
    )


def attend_back_kernel(
    seqs, slots, da_ref, x_ref, inv_ref, g_ref, wq_ref, wk_ref, wv_ref, wo_ref, cos_ref, sin_ref,
    q_ref, k_ref, v_ref, lse_ref,
    dn_ref, dwq_ref, dwk_ref, dwv_ref, gain_ref, dmix_ref, dqkv_ref, dk_ref, dv_ref,
):
    total, width = da_ref.shape
    length = total // seqs
    block = row_block(length)
    count = length // block
    scale = HEAD_DIM ** (-0.5)
    span = slots * HEAD_DIM
    for s in range(seqs):
        for i in range(count):
            rows = pl.ds(s * length + i * block, block)
            dmix_ref[rows, :] = dot_nt(da_ref[rows, :], wo_ref[...]).astype(BF)
        for h in range(slots):
            cols = slice(h * HEAD_DIM, (h + 1) * HEAD_DIM)
            dk_ref[...] = jnp.zeros_like(dk_ref)
            dv_ref[...] = jnp.zeros_like(dv_ref)
            for i in range(count):
                rows = pl.ds(s * length + i * block, block)
                reach = (i + 1) * block
                keys = pl.ds(s * length, reach)
                shape = (block, reach)
                seen = (
                    lax.broadcasted_iota(jnp.int32, shape, 1)
                    <= lax.broadcasted_iota(jnp.int32, shape, 0) + i * block
                )
                q = q_ref[rows, cols]
                k = k_ref[keys, cols]
                dmix = dmix_ref[rows, cols]
                scores = jnp.where(seen, dot_nt(q, k) * scale, MASKED)
                probs = jnp.exp(scores - lse_ref[rows, h : h + 1])
                dp = dot_nt(dmix, v_ref[keys, cols])
                delta = jnp.sum(probs * dp, -1, keepdims=True)
                ds = (probs * (dp - delta)).astype(BF)
                dq = dot(ds, k) * scale
                cosine = cos_ref[pl.ds(i * block, block), :]
                sine = sin_ref[pl.ds(i * block, block), :]
                dqkv_ref[rows, h * HEAD_DIM : (h + 1) * HEAD_DIM] = (
                    dq * cosine - pltpu.roll(dq, HEAD_DIM // 2, 1) * sine
                ).astype(BF)
                dk_ref[pl.ds(0, reach), :] += dot_tn(ds, q)
                dv_ref[pl.ds(0, reach), :] += dot_tn(probs.astype(BF), dmix)
            for i in range(count):
                rows = pl.ds(s * length + i * block, block)
                here = pl.ds(i * block, block)
                dk = dk_ref[here, :] * scale
                dk = dk * cos_ref[here, :] - pltpu.roll(dk, HEAD_DIM // 2, 1) * sin_ref[here, :]
                dqkv_ref[rows, span + h * HEAD_DIM : span + (h + 1) * HEAD_DIM] = dk.astype(BF)
                dqkv_ref[rows, 2 * span + h * HEAD_DIM : 2 * span + (h + 1) * HEAD_DIM] = dv_ref[here, :].astype(BF)
    gain = jnp.zeros((1, width), F32)
    for i in range(total // block):
        rows = pl.ds(i * block, block)
        d_normed = dot_nt(dqkv_ref[rows, :span], wq_ref[...])
        d_normed += dot_nt(dqkv_ref[rows, span : 2 * span], wk_ref[...])
        d_normed += dot_nt(dqkv_ref[rows, 2 * span :], wv_ref[...])
        dn_ref[rows, :] = d_normed.astype(BF)
        gain += jnp.sum(d_normed * x_ref[rows, :].astype(F32) * inv_ref[rows, :], 0, keepdims=True)
    gain_ref[...] = gain
    step = LANES * 2
    for i in range(width // step):
        cols = slice(i * step, (i + 1) * step)
        normed = (x_ref[:, cols].astype(F32) * inv_ref[...] * g_ref[:, cols].astype(F32)).astype(BF)
        grads = dot_tn(normed, dqkv_ref[...]).astype(BF)
        dwq_ref[cols, :] = grads[:, :span]
        dwk_ref[cols, :] = grads[:, span : 2 * span]
        dwv_ref[cols, :] = grads[:, 2 * span :]


def attend_back(seqs, slots, d_att, x, inverse, gain, w_slices, w_out, cosine, sine, q, k, v, lse):
    total, width = d_att.shape
    span = slots * HEAD_DIM
    shape = jax.ShapeDtypeStruct
    return vmem_call(
        functools.partial(attend_back_kernel, seqs, slots),
        [shape((total, width), BF)] + [shape((width, span), BF)] * 3 + [shape((1, width), F32)],
        d_att, x, inverse, gain, *w_slices, w_out, cosine, sine, q, k, v, lse,
        scratch_shapes=[
            pltpu.VMEM((total, span), BF),
            pltpu.VMEM((total, 3 * span), BF),
            pltpu.VMEM((total // seqs, HEAD_DIM), F32),
            pltpu.VMEM((total // seqs, HEAD_DIM), F32),
        ],
        name="attend_back",
    )


def experts_kernel(
    experts, steps, n_ref, c_ref, prob_ref, weight_ref, eye_ref, wg_ref, wu_ref, wd_ref, sg_ref, su_ref, sd_ref,
    router_ref, n_group, c_group, w_group,
    out_ref, dx_ref, dlog_ref, dsg_ref, dsu_ref, dsd_ref, n_all, c_all, w_all, send, recv,
):
    step = pl.program_id(0)
    part = c_all.shape[-1]
    moves = [
        Across(lambda r: n_group.at[r], n_all, send.at[0], recv.at[0]),
        SameExperts(w_group, w_all, send.at[1], recv.at[1]),
        Across(lambda r: c_group.at[r, pl.ds(part, part)], c_all, send.at[2], recv.at[2]),
    ]

    @pl.when(step == 0)
    def _():
        meet(moves[0].peers() + moves[1].peers())
        for move in moves:
            move.start()

    @pl.when(step == steps // 3)
    def _():
        for move in moves:
            move.relay()

    @pl.when(step == 2 * steps // 3)
    def _():
        for move in moves:
            move.hand_over()

    n = n_ref[...]
    c_b = c_ref[...]
    c = c_b.astype(F32)
    gate = dot(n, sg_ref[...])
    up = dot(n, su_ref[...])
    hidden = (silu(gate) * up).astype(BF)
    out = dot(hidden, sd_ref[...])
    d_gate, d_up = swiglu_back(dot_nt(c_b, sd_ref[...]), gate, up)
    dx = dot_nt(d_gate, sg_ref[...]) + dot_nt(d_up, su_ref[...])

    @pl.when(step == 0)
    def _():
        dsg_ref[...] = jnp.zeros_like(dsg_ref)
        dsu_ref[...] = jnp.zeros_like(dsu_ref)
        dsd_ref[...] = jnp.zeros_like(dsd_ref)

    dsg_ref[...] += dot_tn(n, d_gate)
    dsu_ref[...] += dot_tn(n, d_up)
    dsd_ref[...] += dot_tn(hidden, c_b)
    probs = prob_ref[...]
    d_log = jnp.zeros_like(probs)
    inner = jnp.zeros((n.shape[0], 1), F32)
    for j in range(experts):
        weight = weight_ref[:, j : j + 1]
        gate = dot(n, wg_ref[j])
        up = dot(n, wu_ref[j])
        hidden = (silu(gate) * up).astype(BF)
        y = dot(hidden, wd_ref[j]).astype(BF).astype(F32)
        out += weight * y
        d_weight = weight * jnp.sum(c * y, -1, keepdims=True)
        d_log += eye_ref[j : j + 1, :] * d_weight
        inner += d_weight
        d_gate, d_up = swiglu_back(dot_nt((weight * c).astype(BF), wd_ref[j]), gate, up)
        dx += dot_nt(d_gate, wg_ref[j]) + dot_nt(d_up, wu_ref[j])
    d_log = (d_log - probs * inner).astype(BF)
    dlog_ref[...] = d_log
    dx += dot_nt(d_log, router_ref[...])
    out_ref[...] = out.astype(BF)
    dx_ref[...] = dx.astype(BF)

    @pl.when(step == steps - 1)
    def _():
        for move in moves:
            move.finish()


def experts(normed, cot, probs, weight, packed, eye, w_gate, w_up, w_down, s_gate, s_up, s_down, router):
    total, width = normed.shape
    count, _, hidden = w_gate.shape
    tile = 256 if total % 256 == 0 else total
    steps = total // tile
    anywhere = pl.BlockSpec(memory_space=pl.ANY)
    dma = pltpu.SemaphoreType.DMA
    names = probs.shape[1]
    share = s_gate.shape[1]

    def rows(cols):
        return pl.BlockSpec((tile, cols), lambda i: (i, 0))

    def whole(a):
        zeros = (0,) * a.ndim
        return pl.BlockSpec(a.shape, lambda i: zeros, pipeline_mode=pl.Buffered(1))

    shape = jax.ShapeDtypeStruct
    fixed = (eye, w_gate, w_up, w_down, s_gate, s_up, s_down, router)
    flops = total * width * hidden * count * 12
    return pl.pallas_call(
        functools.partial(experts_kernel, count, steps),
        grid=(steps,),
        in_specs=[rows(width), rows(width), rows(names), rows(count)] + [whole(a) for a in fixed] + [anywhere] * 3,
        out_specs=[
            rows(width),
            rows(width),
            rows(names),
            pl.BlockSpec((width, share), lambda i: (0, 0)),
            pl.BlockSpec((width, share), lambda i: (0, 0)),
            pl.BlockSpec((share, width), lambda i: (0, 0)),
            anywhere, anywhere, anywhere,
        ],
        out_shape=[
            shape((total, width), BF),
            shape((total, width), BF),
            shape((total, names), BF),
            shape((width, share), F32),
            shape((width, share), F32),
            shape((share, width), F32),
            shape((6, total // 2, width), BF),
            shape((6, total // 2, width // 2), BF),
            shape((6, total // 2, LANES), BF),
        ],
        scratch_shapes=[dma((3, Across.SEMAPHORES)), dma((3, Across.SEMAPHORES))],
        compiler_params=pltpu.CompilerParams(
            vmem_limit_bytes=VMEM_LIMIT, collective_id=3, has_side_effects=True
        ),
        cost_estimate=pl.CostEstimate(flops=flops, bytes_accessed=30 * 2**20, transcendentals=0),
        name="experts",
    )(normed, cot, probs, weight, *fixed, normed, cot, packed)


def routed_tile(j, count, n, c1, c2, packed, w_gate, w_up, w_down, acc_gate, acc_up, acc_down):
    part = c1.shape[-1]
    weight = packed[:, j : j + 1].astype(F32) + packed[:, count + j : count + j + 1].astype(F32)
    d_y = jnp.concatenate(
        [(weight * c1.astype(F32)).astype(BF), (weight * c2.astype(F32)).astype(BF)], -1
    )
    gate, up = dot(n, w_gate), dot(n, w_up)
    d_gate, d_up = swiglu_back(dot_nt(d_y, w_down), gate, up)
    hidden = (silu(gate) * up).astype(BF)
    acc_gate[...] += dot_tn(n, d_gate)
    acc_up[...] += dot_tn(n, d_up)
    acc_down[...] += dot_tn(hidden, d_y)


def weights_kernel(
    j, count, first, size, own_steps, n_own, c_own, packed_own, n_ref, c1_ref, c2_ref, packed_ref,
    wg_ref, wu_ref, wd_ref, *refs,
):
    dg_ref, du_ref, dd_ref, wg, wu, wd, acc_gate, acc_up, acc_down, load, store = refs[-11:]
    step = pl.program_id(0)
    cols = pl.ds(first, size)

    @pl.when(step == 0)
    def _():
        copies = [
            pltpu.make_async_copy(wg_ref.at[j, :, cols], wg, load.at[0]),
            pltpu.make_async_copy(wu_ref.at[j, :, cols], wu, load.at[1]),
            pltpu.make_async_copy(wd_ref.at[j, cols], wd, load.at[2]),
        ]
        for copy in copies:
            copy.start()
        for acc in (acc_gate, acc_up, acc_down):
            acc[...] = jnp.zeros_like(acc)
        for copy in copies:
            copy.wait()

    ours = step < own_steps
    part = c1_ref.shape[-1]
    routed_tile(
        j, count,
        jnp.where(ours, n_own[...], n_ref[0]),
        jnp.where(ours, c_own[:, :part], c1_ref[0]),
        jnp.where(ours, c_own[:, part : 2 * part], c2_ref[0]),
        jnp.where(ours, packed_own[...], packed_ref[0]),
        wg[...], wu[...], wd[...], acc_gate, acc_up, acc_down,
    )

    @pl.when(step == pl.num_programs(0) - 1)
    def _():
        copies = [
            pltpu.make_async_copy(acc_gate, dg_ref.at[j, :, cols], store.at[0]),
            pltpu.make_async_copy(acc_up, du_ref.at[j, :, cols], store.at[1]),
            pltpu.make_async_copy(acc_down, dd_ref.at[j, cols], store.at[2]),
        ]
        for copy in copies:
            copy.start()
        for copy in copies:
            copy.wait()


def expert_weights(j, first, size, tokens, weights, grads=None):
    own, others = tokens
    slots, half, width = others[0].shape
    count = weights[0].shape[0]
    tile = min(512, half)
    per = half // tile
    own_steps = 2 * per

    def own_rows(a):
        return pl.BlockSpec((tile, a.shape[-1]), lambda i: (jnp.minimum(i, own_steps - 1), 0))

    def rows(a):
        def place(i):
            k = jnp.maximum(i - own_steps, 0)
            return k // per, k % per, 0

        return pl.BlockSpec((1, tile, a.shape[-1]), place)

    anywhere = pl.BlockSpec(memory_space=pl.ANY)
    dma = pltpu.SemaphoreType.DMA
    before = [] if grads is None else list(grads)
    return pl.pallas_call(
        functools.partial(weights_kernel, j, count, first, size, own_steps),
        grid=(own_steps + slots * per,),
        in_specs=[own_rows(a) for a in own] + [rows(a) for a in others]
        + [anywhere] * (3 + len(before)),
        out_specs=[anywhere] * 3,
        out_shape=[jax.ShapeDtypeStruct(w.shape, F32) for w in weights],
        scratch_shapes=[
            pltpu.VMEM((width, size), BF), pltpu.VMEM((width, size), BF), pltpu.VMEM((size, width), BF),
            pltpu.VMEM((width, size), F32), pltpu.VMEM((width, size), F32), pltpu.VMEM((size, width), F32),
            dma((3,)), dma((3,)),
        ],
        input_output_aliases={} if grads is None else {10: 0, 11: 1, 12: 2},
        compiler_params=pltpu.CompilerParams(vmem_limit_bytes=VMEM_LIMIT),
        cost_estimate=pl.CostEstimate(
            flops=slots * half * width * size * 12, bytes_accessed=40 * 2**20, transcendentals=0
        ),
        name="expert_weights",
    )(*own, *others, *weights, *before)


def norm_back(grad, values, inverse, gain):
    scaled = grad * gain
    inner = jnp.mean(scaled * values, -1, keepdims=True)
    return inverse * scaled - values * inverse**3 * inner


def body(
    tokens, cotangent, attn_gain, ffn_gain, w_query, w_key, w_value, w_output, router,
    shared_gate, shared_up, shared_down, expert_gate, expert_up, expert_down, expert_ids,
):
    ranks = lax.axis_size("expert")
    me = lax.axis_index("expert")
    seqs, own_pos, width = tokens.shape
    length = own_pos * ranks
    total = seqs * length
    own = seqs * own_pos
    rows = w_query.shape[0]
    heads = width // HEAD_DIM
    slots = -(-heads // ranks)
    span = slots * HEAD_DIM
    share = shared_gate.shape[1] // ranks
    names = router.shape[1]
    count = expert_gate.shape[0]

    groups = lax.axis_size("dp")

    def in_order(a):
        return a.reshape(ranks, seqs, own_pos, -1).transpose(1, 0, 2, 3).reshape(total, -1)

    def by_rank(a):
        return a.reshape(seqs, ranks, own_pos, -1).transpose(1, 0, 2, 3).reshape(total, -1)

    def by_share(w):
        return w.reshape(rows, ranks, share).transpose(1, 0, 2)

    def to_all(w):
        return jnp.broadcast_to(w[None], (ranks,) + w.shape)

    pieces = [
        by_share(shared_gate), by_share(shared_up), to_all(router), to_all(attn_gain[:, None]), to_all(ffn_gain[:, None]),
    ]
    edges = [0]
    for p in pieces:
        edges.append(edges[-1] + p.shape[-1])
    pack = jnp.concatenate(pieces, -1)
    pack = jnp.pad(pack, ((0, 0), (0, 0), (0, span - edges[-1])))
    group_x, w_slices = front(
        ranks, groups, heads, slots, tokens.reshape(own, width), w_query, w_key, w_value, pack
    )
    landed = w_slices[3]
    s_gate = landed[:, edges[0] : edges[1]]
    s_up = landed[:, edges[1] : edges[2]]
    full_router = landed[:, edges[2] : edges[3]]
    gain_one = landed[:, edges[3]][None, :]
    gain_two = landed[:, edges[4]][None, :].astype(F32)
    cosine, sine = rotary_tables(length)
    inverse_one, q, k, v, mixed, lse, half_out = attend(
        ranks, groups, seqs, slots, in_order(group_x), gain_one, w_slices[0], w_slices[1], w_slices[2],
        cosine, sine, w_output,
    )

    top = expert_ids.shape[-1]
    extended = jnp.concatenate(
        [
            cotangent.reshape(own, width),
            expert_ids.reshape(own, top).astype(BF),
            jnp.zeros((own, -top % LANES), BF),
        ],
        -1,
    )
    group_c = lax.all_gather(extended, "expert", axis=0, tiled=True)
    group_ids = group_c[:, width : width + top].astype(jnp.int32)

    inputs = tokens.reshape(own, width).astype(F32)
    resid, normed_two, all_mixed, all_out, all_c1 = project(
        ranks, heads, slots, group_x, by_rank(mixed), half_out, gain_two, group_c
    )
    padded_out = jnp.pad(all_out, ((0, slots * ranks * HEAD_DIM - width), (0, 0)))
    w_out = lax.dynamic_index_in_dim(
        padded_out.reshape(slots, ranks, HEAD_DIM, width), me, 1, keepdims=False
    ).reshape(span, width)

    probs = jax.nn.softmax(dot(normed_two, full_router), axis=-1)
    mine = me * count + jnp.arange(count)
    chosen = jnp.any(group_ids[:, :, None] == mine[None, None, :], axis=1).astype(F32)
    weight = chosen * lax.dynamic_slice_in_dim(probs, me * count, count, 1)
    high = weight.astype(BF)
    low = (weight - high.astype(F32)).astype(BF)
    packed = jnp.concatenate([high, low, jnp.zeros((total, LANES - 2 * count), BF)], -1)
    eye = (jnp.arange(names)[None, :] == mine[:, None]).astype(F32)
    layer_part, d_normed_part, d_log, d_s_gate, d_s_up, d_s_down, all_n, all_c2, all_w = experts(
        normed_two, group_c, probs, weight, packed, eye, expert_gate, expert_up, expert_down,
        s_gate, s_up, shared_down, full_router,
    )
    router_part = dot_tn(normed_two, d_log)
    every = ((normed_two, group_c, packed), (all_n, all_c1, all_c2, all_w))
    banks = (expert_gate, expert_up, expert_down)
    hidden = expert_gate.shape[-1]
    cut = hidden * 4 // 7 if hidden % (7 * LANES) == 0 else hidden // 2

    def after(late, *earlier):
        return lax.optimization_barrier((late, earlier))[0]

    def scatter(partial):
        return lax.psum_scatter(partial, "expert", scatter_dimension=0, tiled=True)

    grads = expert_weights(0, 0, cut, every, banks)
    d_normed_two, grads = lax.optimization_barrier((scatter(d_normed_part), grads))
    d_normed_two = d_normed_two.astype(F32)
    inverse_two = lax.rsqrt(jnp.mean(resid * resid, -1, keepdims=True) + EPS)
    ffn_gain_part = jnp.sum(d_normed_two * resid * inverse_two, 0)
    d_out = cotangent.reshape(own, width).astype(F32)
    d_resid = d_out + norm_back(d_normed_two, resid, inverse_two, gain_two)
    own_att = d_resid.astype(BF)
    d_att = lax.all_gather(own_att, "expert", axis=0, tiled=True)
    grads = expert_weights(0, cut, hidden - cut, after(every, own_att), banks, grads)
    d_att, grads = lax.optimization_barrier((d_att, grads))

    d_normed_part, d_wq, d_wk, d_wv, attn_gain_part = attend_back(
        seqs, slots, in_order(d_att), in_order(group_x), inverse_one, gain_one, w_slices[:3], w_out,
        cosine, sine, q, k, v, lse
    )
    d_qkv = jnp.concatenate([d_wq, d_wk, d_wv], -1)
    grads = expert_weights(1, 0, hidden, after(every, attn_gain_part), banks, grads)
    g_gate, g_up, g_down = grads
    d_normed_one = scatter(by_rank(d_normed_part)).astype(F32)
    own_inverse = lax.rsqrt(jnp.mean(inputs * inputs, -1, keepdims=True) + EPS)
    input_grad = d_resid + norm_back(d_normed_one, inputs, own_inverse, gain_one.astype(F32))
    layer_output = resid + scatter(layer_part).astype(F32)
    own_mixed = lax.dynamic_slice_in_dim(all_mixed, me * rows, rows, 1)
    d_wo_rows = dot_tn(own_mixed, d_att).astype(BF)

    def to_rows(g):
        return g.reshape(ranks, rows, -1)

    pieces = [
        to_rows(d_qkv), to_rows(d_s_gate.astype(BF)), to_rows(d_s_up.astype(BF)), to_rows(router_part.astype(BF)),
        to_rows(attn_gain_part.astype(BF)), to_rows(ffn_gain_part.astype(BF)),
    ]
    used = sum(p.shape[-1] for p in pieces)
    packed = jnp.pad(jnp.concatenate(pieces, -1), ((0, 0), (0, 0), (0, -used % LANES)))
    landed = lax.all_to_all(packed, "expert", 0, 0, tiled=True)
    edges = [0]
    for p in pieces:
        edges.append(edges[-1] + p.shape[-1])

    def heads_back(part):
        part = part.reshape(ranks, rows, slots, HEAD_DIM).transpose(1, 2, 0, 3)
        return part.reshape(rows, slots * ranks * HEAD_DIM)[:, :width]

    def shares_back(part):
        return part.transpose(1, 0, 2).reshape(rows, ranks * share)

    def summed(part):
        return jnp.sum(part.astype(F32), 0).astype(BF)

    sums = lax.psum(
        (
            heads_back(landed[:, :, :span]),
            heads_back(landed[:, :, span : 2 * span]),
            heads_back(landed[:, :, 2 * span : 3 * span]),
            d_wo_rows,
            shares_back(landed[:, :, edges[1] : edges[2]]),
            shares_back(landed[:, :, edges[2] : edges[3]]),
            summed(landed[:, :, edges[3] : edges[4]]),
            summed(landed[:, :, edges[4]]),
            summed(landed[:, :, edges[5]]),
            d_s_down.astype(BF),
        ),
        "dp",
    )
    g_q, g_k, g_v, g_o, g_sg, g_su, g_r, g_one, g_two, g_sd = [s.astype(F32) for s in sums]
    return (
        layer_output.astype(BF).reshape(tokens.shape),
        input_grad.astype(BF).reshape(tokens.shape),
        g_one, g_two, g_q, g_k, g_v, g_o, g_r, g_sg, g_su, g_sd, g_gate, g_up, g_down,
    )


def solution(mesh):
    row = P("expert", None)
    experts_spec = P("expert", None, None)
    tokens_spec = P("dp", "expert", None)
    return jax.shard_map(
        body,
        mesh=mesh,
        in_specs=(tokens_spec, tokens_spec, P("expert"), P("expert"))
        + (row,) * 8
        + (experts_spec,) * 3
        + (P(("dp", "expert"), None, None),),
        out_specs=(tokens_spec, tokens_spec, P("expert"), P("expert")) + (row,) * 8 + (experts_spec,) * 3,
        check_vma=False,
    )
```

```python
import functools

import jax
import jax.numpy as jnp
from jax import lax
from jax.experimental import pallas as pl
from jax.experimental.pallas import tpu as pltpu
from jax.sharding import PartitionSpec as P

HEAD_DIM = 128
LANES = 128
EPS = 1e-06
MASKED = -1e30
VMEM_LIMIT = 60 * 2**20
BF = jnp.bfloat16
F32 = jnp.float32


def dot(a, b):
    return jnp.dot(a, b, preferred_element_type=F32)


def dot_nt(a, b):
    return lax.dot_general(a, b, (((1,), (1,)), ((), ())), preferred_element_type=F32)


def dot_tn(a, b):
    return lax.dot_general(a, b, (((0,), (0,)), ((), ())), preferred_element_type=F32)


def silu(v):
    return v / (1.0 + jnp.exp(-v))


def swiglu_back(d_hidden, gates, ups):
    sigma = 1.0 / (1.0 + jnp.exp(-gates))
    d_gate = d_hidden * ups * sigma * (1.0 + gates * (1.0 - sigma))
    d_up = d_hidden * (gates * sigma)
    return d_gate.astype(BF), d_up.astype(BF)


def rotary_tables(length):
    half = HEAD_DIM // 2
    inverse_freq = 10000.0 ** (-jnp.arange(half, dtype=F32) * 2.0 / HEAD_DIM)
    angles = jnp.arange(length).astype(F32)[:, None] * inverse_freq[None, :]
    cosine, sine = jnp.cos(angles), jnp.sin(angles)
    return jnp.concatenate([cosine, cosine], -1), jnp.concatenate([-sine, sine], -1)


def vmem_call(kernel, outs, *args, remote_id=None, **kwargs):
    spec = pl.BlockSpec(memory_space=pltpu.VMEM)
    params = {} if remote_id is None else {"collective_id": remote_id, "has_side_effects": True}
    return pl.pallas_call(
        kernel,
        out_shape=outs,
        in_specs=[spec] * len(args),
        out_specs=[spec] * len(outs),
        compiler_params=pltpu.CompilerParams(vmem_limit_bytes=VMEM_LIMIT, **params),
        **kwargs,
    )(*args)


def row_block(length):
    return 256 if length % 256 == 0 else length


def remote(src, dst, send, recv, **device):
    return pltpu.make_async_remote_copy(
        src_ref=src, dst_ref=dst, send_sem=send, recv_sem=recv, device_id=device, device_id_type=pl.DeviceIdType.MESH
    )


def meet(peers):
    barrier = pltpu.get_barrier_semaphore()
    for peer in peers:
        pl.semaphore_signal(barrier, inc=1, device_id=peer, device_id_type=pl.DeviceIdType.MESH)
    pl.semaphore_wait(barrier, len(peers))


def meet_near(chips, z, me, peers=()):
    barrier = pltpu.get_barrier_semaphore()
    near = [(True, {"expert": me + 1 - 2 * lax.rem(me, 2)}), (z > 0, {"expert": me - 2}), (z < chips - 1, {"expert": me + 2})]
    near += [(True, {"dp": t}) for t in peers]

    def signal(t):
        pl.semaphore_signal(barrier, inc=1, device_id=t, device_id_type=pl.DeviceIdType.MESH)

    for ok, t in near:
        guarded(ok, functools.partial(signal, t))
    ends = jnp.where(z > 0, 1, 0) + jnp.where(z < chips - 1, 1, 0)
    pl.semaphore_wait(barrier, 1 + len(peers) + ends)


def both(*conditions):
    held = [c for c in conditions if c is not True]
    if not held:
        return True
    out = held[0]
    for c in held[1:]:
        out = jnp.logical_and(out, c)
    return out


def guarded(condition, action):
    if condition is True:
        action()
    else:
        pl.when(condition)(action)


class LineGather:
    def __init__(self, ranks, own, block, send, recv, base=0, valid=lambda i: True, twins=True):
        self.me = lax.axis_index("expert")
        self.chips = ranks // 2
        self.z = self.me // 2
        self.twin = self.me + 1 - 2 * lax.rem(self.me, 2)
        self.own, self.block, self.send, self.recv, self.base, self.valid = own, block, send, recv, base, valid
        self.twins = twins

    @staticmethod
    def semaphores(ranks):
        return 4 * (ranks // 2 - 1) + 1

    def copy(self, src, i, k, to):
        return remote(src, self.block(i), self.send.at[self.base + k], self.recv.at[self.base + k], expert=to)

    def sources(self, s):
        hops = self.chips - 1
        return (
            (self.me - 2 * s, self.z - s >= 0, self.z < hops, self.me + 2, 0, 2 * hops, -2 * s),
            (self.me + 2 * s, self.z + s <= hops, self.z > 0, self.me - 2, hops, 3 * hops, 2 * s),
        )

    def start(self):
        hops = self.chips - 1
        mine = self.valid(self.me)
        if hops:
            guarded(both(self.z < hops, mine), lambda: self.copy(self.own, self.me, 0, self.me + 2).start())
            guarded(both(self.z > 0, mine), lambda: self.copy(self.own, self.me, hops, self.me - 2).start())
        if self.twins:
            guarded(mine, lambda: self.copy(self.own, self.me, 2 * hops, self.twin).start())

    def step(self, s):
        for i, there, more, to, k, pair, _ in self.sources(s):
            known = both(there, self.valid(i))
            src = self.block(i)
            guarded(known, lambda: self.copy(src, i, k + s - 1, self.twin).wait_recv())
            if s < self.chips - 1:
                guarded(both(known, more), lambda: self.copy(src, i, k + s, to).start())
            if self.twins:
                guarded(known, lambda: self.copy(src, i, pair + s, self.twin).start())

    def finish(self):
        hops = self.chips - 1
        mine = self.valid(self.me)
        theirs = self.valid(self.twin)
        if self.twins:
            guarded(mine, lambda: self.copy(self.own, self.me, 2 * hops, self.twin).wait_send())
            guarded(theirs, lambda: self.copy(self.own, self.twin, 2 * hops, self.twin).wait_recv())
        if hops:
            guarded(both(self.z < hops, mine), lambda: self.copy(self.own, self.me, 0, self.twin).wait_send())
            guarded(both(self.z > 0, mine), lambda: self.copy(self.own, self.me, hops, self.twin).wait_send())
        for s in range(1, self.chips):
            for i, there, more, to, k, pair, shift in self.sources(s):
                known = both(there, self.valid(i))
                src = self.block(i)
                if s < hops:
                    guarded(both(known, more), lambda: self.copy(src, i, k + s, self.twin).wait_send())
                if not self.twins:
                    continue
                guarded(known, lambda: self.copy(src, i, pair + s, self.twin).wait_send())
                j = self.twin + shift
                got = both(there, self.valid(j))
                guarded(got, lambda: self.copy(self.block(j), j, pair + s, self.twin).wait_recv())


class Across:
    SEMAPHORES = 12

    def __init__(self, source, dst, send, recv):
        self.me, self.g = lax.axis_index("expert"), lax.axis_index("dp")
        self.twin = self.me + 1 - 2 * lax.rem(self.me, 2)
        self.by_x = self.g + 1 - 2 * lax.rem(self.g, 2)
        self.by_y = lax.rem(self.g + 2, 4)
        self.source, self.dst, self.send, self.recv = source, dst, send, recv
        self.half = dst.shape[1]
        self.part = self.half // 2

    def peers(self):
        return [{"dp": self.by_x}, {"dp": self.by_y}, {"expert": self.twin}]

    def piece(self, slot, j):
        return self.dst.at[slot, pl.ds(j * self.part, self.part)]

    def mine(self, j):
        first = lax.rem(self.me, 2) * self.half + j * self.part
        return self.source(pl.ds(pl.multiple_of(first, self.part), self.part))

    def copy(self, k, src, dst, **to):
        return remote(src, dst, self.send.at[k], self.recv.at[k], **to)

    def direct(self, k):
        slot, j, to = ((0, 0, self.by_x), (1, 1, self.by_y), (0, 1, self.by_x), (1, 0, self.by_y))[k]
        return self.copy(k, self.mine(j), self.piece(slot, j), dp=to)

    def relayed(self, j):
        if j == 0:
            return self.copy(4, self.piece(0, 0), self.piece(2, 0), dp=self.by_y)
        return self.copy(5, self.piece(1, 1), self.piece(2, 1), dp=self.by_x)

    def shared(self, slot, j):
        return self.copy(6 + 2 * slot + j, self.piece(slot, j), self.piece(slot + 3, j), expert=self.twin)

    def start(self):
        for k in range(2):
            self.direct(k).start()

    def more(self):
        for k in range(2, 4):
            self.direct(k).start()

    def relay(self):
        self.direct(0).wait_recv()
        self.relayed(0).start()
        self.direct(1).wait_recv()
        self.relayed(1).start()
        self.shared(0, 0).start()
        self.shared(1, 1).start()

    def hand_over(self):
        self.direct(2).wait_recv()
        self.shared(0, 1).start()
        self.direct(3).wait_recv()
        self.shared(1, 0).start()

    def finish(self):
        for j in range(2):
            self.relayed(j).wait_recv()
            self.shared(2, j).start()
        for k in range(4):
            self.direct(k).wait_send()
        for j in range(2):
            self.relayed(j).wait_send()
            for slot in range(3):
                self.shared(slot, j).wait()


class SameExperts:
    SEMAPHORES = 6

    def __init__(self, source, dst, send, recv):
        self.me, self.g = lax.axis_index("expert"), lax.axis_index("dp")
        self.near = [self.g + 1 - 2 * lax.rem(self.g, 2), lax.rem(self.g + 2, 4)]
        self.near.append(self.near[1] + 1 - 2 * lax.rem(self.near[1], 2))
        self.source, self.dst, self.send, self.recv = source, dst, send, recv
        self.half = dst.shape[1]

    def peers(self):
        return [{"dp": self.near[2]}]

    def copy(self, k, h):
        slot = k + 3 * lax.rem(lax.rem(self.me, 2) + h, 2)
        i = 2 * k + h
        src = self.source.at[pl.ds(h * self.half, self.half)]
        return remote(src, self.dst.at[slot], self.send.at[i], self.recv.at[i], dp=self.near[k])

    def start(self):
        for k in range(3):
            for h in range(2):
                self.copy(k, h).start()

    def relay(self):
        pass

    hand_over = more = relay

    def finish(self):
        for k in range(3):
            for h in range(2):
                self.copy(k, h).wait()


def head_of(s, i, ranks):
    return i if s == 0 else s * ranks + i // 2 + (i % 2) * (ranks // 2)


def aligned(i, size):
    return pl.ds(pl.multiple_of(i * size, size), size)


def front_kernel(
    ranks, groups, heads, slots, x_ref, c_ref, wq_ref, wk_ref, wv_ref, pack_ref, wo_ref,
    gx_ref, gc_ref, wqs_ref, wks_ref, wvs_ref, wps_ref, small_ref, half_ref, stage_ref, land_ref, ostage_ref,
    x_send, x_recv, c_send, c_recv, w_send, w_recv, d_send, d_recv, o_send, o_recv, p_send, p_recv,
):
    me, g = lax.axis_index("expert"), lax.axis_index("dp")
    rows, width = wq_ref.shape
    units = width // LANES
    per = ostage_ref.shape[0]
    peers = [lax.rem(g + d, groups) for d in range(1, groups)]
    others = [lax.rem(me + d, ranks) for d in range(1, ranks)]
    meet([{"expert": t} for t in others] + [{"dp": t} for t in peers])

    def stage_heads(w):
        for u in range(heads):
            stage_ref[u] = w[:, u * LANES : (u + 1) * LANES]

    for which, w in enumerate((wq_ref, wk_ref, wv_ref)):
        pl.when(g == which)(functools.partial(stage_heads, w))

    def stage_pack():
        for s in range(slots):
            for t in range(ranks):
                stage_ref[head_of(s, t, ranks)] = pack_ref[t, :, s * LANES : (s + 1) * LANES]

    pl.when(g == groups - 1)(stage_pack)

    def known(s, t, group=None):
        return jnp.logical_or((g if group is None else group) == groups - 1, head_of(s, t, ranks) < heads)

    def weight_copy(s, d, unit, i, to):
        return remote(
            stage_ref.at[unit], land_ref.at[g, s, i], w_send.at[s, d], w_recv.at[s, d], expert=to
        )

    for d in range(1, ranks):
        t = others[d - 1]
        for s in range(slots):
            guarded(known(s, t), lambda: weight_copy(s, d, head_of(s, t, ranks), me, t).start())

    def stage_out(which):
        for k in range(per):
            u = which * per + k
            if u < units:
                ostage_ref[k] = wo_ref[:, u * LANES : (u + 1) * LANES]

    for which in range(groups):
        pl.when(g == which)(functools.partial(stage_out, which))
    out_rows = LineGather(
        ranks, ostage_ref, lambda i: half_ref.at[g, :, i // 2], o_send, o_recv, twins=False
    )
    out_rows.start()
    tokens = LineGather(ranks, x_ref, lambda i: gx_ref.at[i], x_send, x_recv)
    tokens.start()
    half_ref[g, :, me // 2] = ostage_ref[...]
    for s in range(slots):
        def keep(s=s):
            land_ref[g, s, me] = stage_ref[head_of(s, me, ranks)]

        pl.when(known(s, me))(keep)
        for which in range(groups - 1):
            def clear(s=s, which=which):
                land_ref[which, s] = jnp.zeros(land_ref.shape[2:], BF)

            pl.when(head_of(s, me, ranks) >= heads)(clear)
    gx_ref[me] = x_ref[...]
    gc_ref[me] = c_ref[...]

    def share(s, part, d, to):
        return remote(part, part, d_send.at[s, d], d_recv.at[s, d], dp=to)

    def pass_on(i):
        for s in range(slots):
            part = land_ref.at[g, s, i]
            for d in range(1, groups):
                pl.when(known(s, me))(lambda: share(s, part, d, peers[d - 1]).start())

    def out_share(d, k, group):
        part = half_ref.at[group, k]
        return remote(part, part, p_send.at[d, k], p_recv.at[d, k], dp=peers[d - 1])

    def held(group, k):
        return True if (groups - 1) * per + k < units else group * per + k < units

    pass_on(me)
    for d in range(1, ranks):
        i = lax.rem(me + ranks - d, ranks)
        for s in range(slots):
            pl.when(known(s, me))(lambda: weight_copy(s, d, 0, i, others[0]).wait_recv())
        pass_on(i)
    steps = ranks // 2 - 1
    for step in range(1, steps + 1):
        out_rows.step(step)
        if step == 1:
            tokens.step(1)
    out_rows.finish()
    for d in range(1, groups):
        for k in range(per):
            guarded(held(g, k), out_share(d, k, g).start)
    cots = LineGather(ranks, c_ref, lambda i: gc_ref.at[i], c_send, c_recv)
    for step in range(2, steps + 1):
        tokens.step(step)
        if step == steps - 1:
            cots.start()
    if steps < 3:
        cots.start()
    for step in range(1, steps + 1):
        cots.step(step)
    tokens.finish()
    cots.finish()
    for d in range(1, ranks):
        t = others[d - 1]
        for s in range(slots):
            pl.when(known(s, t))(lambda: weight_copy(s, d, 0, me, t).wait_send())
    for d in range(1, groups):
        there = lax.rem(g + groups - d, groups)
        for s in range(slots):
            pl.when(known(s, me))(lambda: share(s, land_ref.at[g, s], d, peers[d - 1]).wait_send())
            pl.when(known(s, me, there))(lambda: share(s, land_ref.at[there, s], d, peers[d - 1]).wait_recv())
        for k in range(per):
            guarded(held(g, k), out_share(d, k, g).wait_send)
            guarded(held(there, k), out_share(d, k, there).wait_recv)
    for which, ref in enumerate((wqs_ref, wks_ref, wvs_ref, wps_ref)):
        for s in range(slots):
            for r in range(ranks):
                ref[r * rows : (r + 1) * rows, s * LANES : (s + 1) * LANES] = land_ref[which, s, r]
    small_ref[...] = jnp.transpose(wps_ref[:, (slots - 1) * LANES :].astype(F32))


def front(ranks, groups, heads, slots, x, cot, w_query, w_key, w_value, pack, w_output):
    own, width = x.shape
    rows = w_query.shape[0]
    per = -(-(width // LANES) // groups)
    line = LineGather.semaphores(ranks)
    dma = pltpu.SemaphoreType.DMA
    spec = pl.BlockSpec(memory_space=pltpu.VMEM)
    shape = jax.ShapeDtypeStruct
    return pl.pallas_call(
        functools.partial(front_kernel, ranks, groups, heads, slots),
        out_shape=[shape((ranks, own, width), BF), shape((ranks,) + cot.shape, BF)]
        + [shape((width, slots * LANES), BF)] * 4
        + [shape((LANES, width), F32), shape((groups, per, ranks // 2, rows, LANES), BF)],
        in_specs=[spec] * 7,
        out_specs=[spec] * 8,
        scratch_shapes=[
            pltpu.VMEM((slots * ranks, rows, LANES), BF),
            pltpu.VMEM((groups, slots, ranks, rows, LANES), BF),
            pltpu.VMEM((per, rows, LANES), BF),
            dma((line,)), dma((line,)),
            dma((line,)), dma((line,)),
            dma((slots, ranks)), dma((slots, ranks)),
            dma((slots, groups)), dma((slots, groups)),
            dma((line,)), dma((line,)),
            dma((groups, per)), dma((groups, per)),
        ],
        compiler_params=pltpu.CompilerParams(
            collective_id=0, has_side_effects=True, vmem_limit_bytes=VMEM_LIMIT
        ),
        name="front",
    )(x, cot, w_query, w_key, w_value, pack, w_output)


def project_kernel(
    ranks, groups, heads, slots, count, top, route_at,
    first, x_ref, mixed_ref, half_ref, small_ref, pack_ref, c_ref,
    resid_ref, n_ref, all_ref, wo_ref, packed_ref, c_all_ref, other_ref, id_ref,
    send, recv, t_send, t_recv, a_send, a_recv, load,
):
    me, g = lax.axis_index("expert"), lax.axis_index("dp")
    chips = ranks // 2
    z = me // 2
    twin = me + 1 - 2 * lax.rem(me, 2)
    per, part = half_ref.shape[1], half_ref.shape[3]
    units = wo_ref.shape[1] // LANES
    peers = [lax.rem(g + d, groups) for d in range(1, groups)]
    lanes = c_all_ref.shape[-1]
    across = Across(lambda r: c_ref.at[r, pl.ds(first, lanes)], c_all_ref, a_send, a_recv)
    meet_near(chips, z, me, peers)
    ids = pltpu.make_async_copy(c_ref.at[:, pl.ds(wo_ref.shape[1], LANES)], id_ref, load)
    ids.start()
    line = LineGather.semaphores(ranks)
    parts = []
    for s in range(slots):
        def head(i, s=s):
            return aligned(jnp.clip(head_of(s, i, ranks), 0, heads - 1), LANES)

        cols = slice(s * LANES, (s + 1) * LANES)
        ok = (lambda i: True) if (s + 1) * ranks <= heads else (lambda i, s=s: head_of(s, i, ranks) < heads)
        gather = LineGather(
            ranks, mixed_ref.at[:, cols], lambda i, head=head: all_ref.at[:, head(i)], send, recv, s * line, ok
        )
        gather.start()
        parts.append(gather)

    across.start()
    across.more()
    for s, gather in enumerate(parts):
        def keep(s=s):
            cols = slice(s * LANES, (s + 1) * LANES)
            all_ref[:, aligned(jnp.clip(head_of(s, me, ranks), 0, heads - 1), LANES)] = mixed_ref[:, cols]

        guarded(gather.valid(me), keep)

    def share_twin(group, k):
        src = half_ref.at[group, k]
        return remote(src, other_ref.at[group, k], t_send.at[group, k], t_recv.at[group, k], expert=twin)

    def each_unit(action):
        for group in range(groups):
            for k in range(per):
                if group * per + k < units:
                    action(share_twin(group, k))

    each_unit(lambda copy: copy.start())
    middle = (chips + 1) // 2
    for step in range(1, chips):
        for gather in parts:
            gather.step(step)
        if step == middle:
            across.relay()
    for gather in parts:
        gather.finish()
    each_unit(lambda copy: copy.wait())
    ids.wait()

    def lay_out(even, odd):
        for u in range(units):
            cols = slice(u * LANES, (u + 1) * LANES)
            for c in range(chips):
                wo_ref[2 * c * part : (2 * c + 1) * part, cols] = even[u // per, u % per, c]
                wo_ref[(2 * c + 1) * part : (2 * c + 2) * part, cols] = odd[u // per, u % per, c]

    pl.when(me == 2 * z)(lambda: lay_out(half_ref, other_ref))
    pl.when(me != 2 * z)(lambda: lay_out(other_ref, half_ref))
    blocks, own, width = x_ref.shape
    names = ranks * count
    gain_at = route_at + names + 1 - (slots - 1) * LANES
    gain = small_ref[gain_at : gain_at + 1, :]
    tile = 2 if own <= 128 and blocks % 2 == 0 else 1

    def rows_of(b):
        rows = aligned(b, tile * own)
        x = x_ref[pl.ds(b * tile, tile)].reshape(tile * own, width).astype(F32)
        resid = x + dot(all_ref[rows, :], wo_ref[...])
        inverse = lax.rsqrt(jnp.mean(resid * resid, -1, keepdims=True) + EPS)
        normed = (resid * inverse * gain).astype(BF)
        n_ref[rows, :] = normed
        for t in range(tile):
            def keep(t=t):
                resid_ref[...] = resid[t * own : (t + 1) * own]

            pl.when(b * tile + t == me)(keep)
        probs = route_probs(dot(normed, pack_ref[...]), route_at, names)
        routes = id_ref[rows, :].astype(jnp.int32)
        lane = lax.broadcasted_iota(jnp.int32, routes.shape, 1)
        out = jnp.zeros((tile * own, LANES), F32)
        for j in range(count):
            mine = me * count + j
            chosen = jnp.max(jnp.where((routes == mine) & (lane < top), 1.0, 0.0), -1, keepdims=True)
            names_at = lax.broadcasted_iota(jnp.int32, probs.shape, 1)
            weight = chosen * jnp.sum(jnp.where(names_at == mine, probs, 0.0), -1, keepdims=True)
            high = weight.astype(BF).astype(F32)
            out = jnp.where(lane == j, high, out)
            out = jnp.where(lane == count + j, weight - high, out)
        packed_ref[rows, :] = out.astype(BF)

    half = blocks // tile // 2
    lax.fori_loop(0, half, lambda b, c: (rows_of(b), c)[1], 0)
    across.hand_over()
    lax.fori_loop(half, blocks // tile, lambda b, c: (rows_of(b), c)[1], 0)
    across.finish()


def route_probs(products, first, names):
    logits = products[:, first : first + names]
    raised = jnp.exp(logits - jnp.max(logits, -1, keepdims=True))
    return raised / jnp.sum(raised, -1, keepdims=True)


def project(ranks, groups, heads, slots, count, top, route_at, first, lanes, x, mixed, half, small, pack, cot):
    blocks, own, width = x.shape
    total = blocks * own
    line = LineGather.semaphores(ranks)
    per = half.shape[1]
    dma = pltpu.SemaphoreType.DMA
    spec = pl.BlockSpec(memory_space=pltpu.VMEM)
    anywhere = pl.BlockSpec(memory_space=pl.ANY)
    shape = jax.ShapeDtypeStruct
    return pl.pallas_call(
        functools.partial(project_kernel, ranks, groups, heads, slots, count, top, route_at, first),
        out_shape=[
            shape((own, width), F32),
            shape((total, width), BF),
            shape((total, width), BF),
            shape((width, width), BF),
            shape((total, LANES), BF),
            shape((6, total // 2, lanes), BF),
        ],
        in_specs=[spec] * 5 + [anywhere],
        out_specs=[spec] * 5 + [anywhere],
        scratch_shapes=[
            pltpu.VMEM(half.shape, BF), pltpu.VMEM((total, LANES), BF),
            dma((slots * line,)), dma((slots * line,)),
            dma((groups, per)), dma((groups, per)),
            dma((Across.SEMAPHORES,)), dma((Across.SEMAPHORES,)), dma(()),
        ],
        compiler_params=pltpu.CompilerParams(
            collective_id=1, has_side_effects=True, vmem_limit_bytes=VMEM_LIMIT
        ),
        name="project",
    )(x, mixed, half, small, pack, cot)


def attend_kernel(
    seqs, slots, gain_at, x_ref, small_ref, wq_ref, wk_ref, wv_ref, cos_ref, sin_ref, c_ref,
    inv_ref, q_ref, k_ref, v_ref, mixed_ref, lse_ref, c_all_ref, a_send, a_recv,
):
    total, width = x_ref.shape
    length = total // seqs
    block = row_block(length)
    scale = HEAD_DIM ** (-0.5)
    gain = small_ref[gain_at : gain_at + 1, :]
    across = Across(lambda r: c_ref.at[r, pl.ds(0, c_all_ref.shape[-1])], c_all_ref, a_send, a_recv)
    meet(across.peers())
    across.start()
    across.more()
    for s in range(seqs):
        for i in range(length // block):
            rows = pl.ds(s * length + i * block, block)
            x = x_ref[rows, :].astype(F32)
            inv = lax.rsqrt(jnp.mean(x * x, -1, keepdims=True) + EPS)
            normed = (x * inv * gain).astype(BF)
            inv_ref[rows, :] = inv
            cosine = cos_ref[pl.ds(i * block, block), :]
            sine = sin_ref[pl.ds(i * block, block), :]
            queries, keyed, valued = dot(normed, wq_ref[...]), dot(normed, wk_ref[...]), dot(normed, wv_ref[...])
            for h in range(slots):
                cols = slice(h * HEAD_DIM, (h + 1) * HEAD_DIM)
                q, k = queries[:, cols], keyed[:, cols]
                q_ref[rows, cols] = (q * cosine + pltpu.roll(q, HEAD_DIM // 2, 1) * sine).astype(BF)
                k_ref[rows, cols] = (k * cosine + pltpu.roll(k, HEAD_DIM // 2, 1) * sine).astype(BF)
            v_ref[rows, :] = valued.astype(BF)
    across.relay()
    for s in range(seqs):
        for i in range(length // block):
            if s == 0 and i == length // block - 1:
                across.hand_over()
            rows = pl.ds(s * length + i * block, block)
            keys = pl.ds(s * length, (i + 1) * block)
            shape = (block, (i + 1) * block)
            seen = (
                lax.broadcasted_iota(jnp.int32, shape, 1)
                <= lax.broadcasted_iota(jnp.int32, shape, 0) + i * block
            )
            for h in range(slots):
                cols = slice(h * HEAD_DIM, (h + 1) * HEAD_DIM)
                scores = dot_nt(q_ref[rows, cols], k_ref[keys, cols]) * scale
                scores = jnp.where(seen, scores, MASKED)
                top = jnp.max(scores, -1, keepdims=True)
                raised = jnp.exp(scores - top)
                totals = jnp.sum(raised, -1, keepdims=True)
                probs = (raised / totals).astype(BF)
                mixed_ref[rows, cols] = dot(probs, v_ref[keys, cols]).astype(BF)
                lse_ref[rows, h : h + 1] = top + jnp.log(totals)
    across.finish()


def attend(seqs, slots, gain_at, lanes, x, small, w_q, w_k, w_v, cosine, sine, cot):
    total, width = x.shape
    span = slots * HEAD_DIM
    shape = jax.ShapeDtypeStruct
    dma = pltpu.SemaphoreType.DMA
    vmem, anywhere = pl.BlockSpec(memory_space=pltpu.VMEM), pl.BlockSpec(memory_space=pl.ANY)
    return pl.pallas_call(
        functools.partial(attend_kernel, seqs, slots, gain_at),
        out_shape=[
            shape((total, 1), F32),
            shape((total, span), BF),
            shape((total, span), BF),
            shape((total, span), BF),
            shape((total, span), BF),
            shape((total, slots), F32),
            shape((6, total // 2, lanes), BF),
        ],
        in_specs=[vmem] * 7 + [anywhere],
        out_specs=[vmem] * 6 + [anywhere],
        scratch_shapes=[dma((Across.SEMAPHORES,)), dma((Across.SEMAPHORES,))],
        compiler_params=pltpu.CompilerParams(
            collective_id=2, has_side_effects=True, vmem_limit_bytes=VMEM_LIMIT
        ),
        name="attend",
    )(x, small, w_q, w_k, w_v, cosine, sine, cot)


def attend_back_kernel(
    ranks, heads, seqs, slots, gain_at, da_ref, x_ref, inv_ref, small_ref, wq_ref, wk_ref, wv_ref, wall_ref,
    cos_ref, sin_ref,
    q_ref, k_ref, v_ref, lse_ref,
    dn_ref, dwq_ref, dwk_ref, dwv_ref, gain_ref, dmix_ref, dqkv_ref, dk_ref, dv_ref, wo_ref,
):
    total, width = da_ref.shape
    length = total // seqs
    block = row_block(length)
    count = length // block
    scale = HEAD_DIM ** (-0.5)
    span = slots * HEAD_DIM
    me = lax.axis_index("expert")
    for h in range(slots):
        cols = slice(h * HEAD_DIM, (h + 1) * HEAD_DIM)
        head = head_of(h, me, ranks)
        rows_here = wall_ref[aligned(jnp.minimum(head, heads - 1), HEAD_DIM), :]
        wo_ref[cols, :] = jnp.where(head < heads, rows_here, jnp.zeros_like(rows_here))
    for s in range(seqs):
        for i in range(count):
            rows = pl.ds(s * length + i * block, block)
            dmix_ref[rows, :] = dot_nt(da_ref[rows, :], wo_ref[...]).astype(BF)
        for h in range(slots):
            cols = slice(h * HEAD_DIM, (h + 1) * HEAD_DIM)
            dk_ref[...] = jnp.zeros_like(dk_ref)
            dv_ref[...] = jnp.zeros_like(dv_ref)
            for i in range(count):
                rows = pl.ds(s * length + i * block, block)
                reach = (i + 1) * block
                keys = pl.ds(s * length, reach)
                shape = (block, reach)
                seen = (
                    lax.broadcasted_iota(jnp.int32, shape, 1)
                    <= lax.broadcasted_iota(jnp.int32, shape, 0) + i * block
                )
                q = q_ref[rows, cols]
                k = k_ref[keys, cols]
                dmix = dmix_ref[rows, cols]
                scores = jnp.where(seen, dot_nt(q, k) * scale, MASKED)
                probs = jnp.exp(scores - lse_ref[rows, h : h + 1])
                dp = dot_nt(dmix, v_ref[keys, cols])
                delta = jnp.sum(probs * dp, -1, keepdims=True)
                ds = (probs * (dp - delta)).astype(BF)
                dq = dot(ds, k) * scale
                cosine = cos_ref[pl.ds(i * block, block), :]
                sine = sin_ref[pl.ds(i * block, block), :]
                dqkv_ref[rows, h * HEAD_DIM : (h + 1) * HEAD_DIM] = (
                    dq * cosine - pltpu.roll(dq, HEAD_DIM // 2, 1) * sine
                ).astype(BF)
                dk_ref[pl.ds(0, reach), :] += dot_tn(ds, q)
                dv_ref[pl.ds(0, reach), :] += dot_tn(probs.astype(BF), dmix)
            for i in range(count):
                rows = pl.ds(s * length + i * block, block)
                here = pl.ds(i * block, block)
                dk = dk_ref[here, :] * scale
                dk = dk * cos_ref[here, :] - pltpu.roll(dk, HEAD_DIM // 2, 1) * sin_ref[here, :]
                dqkv_ref[rows, span + h * HEAD_DIM : span + (h + 1) * HEAD_DIM] = dk.astype(BF)
                dqkv_ref[rows, 2 * span + h * HEAD_DIM : 2 * span + (h + 1) * HEAD_DIM] = dv_ref[here, :].astype(BF)
    gain = jnp.zeros((1, width), F32)
    for i in range(total // block):
        rows = pl.ds(i * block, block)
        d_normed = dot_nt(dqkv_ref[rows, :span], wq_ref[...])
        d_normed += dot_nt(dqkv_ref[rows, span : 2 * span], wk_ref[...])
        d_normed += dot_nt(dqkv_ref[rows, 2 * span :], wv_ref[...])
        dn_ref[rows, :] = d_normed.astype(BF)
        gain += jnp.sum(d_normed * x_ref[rows, :].astype(F32) * inv_ref[rows, :], 0, keepdims=True)
    gain_ref[...] = gain
    step = LANES * 2
    for i in range(width // step):
        cols = slice(i * step, (i + 1) * step)
        normed = (x_ref[:, cols].astype(F32) * inv_ref[...] * small_ref[gain_at : gain_at + 1, cols]).astype(BF)
        grads = dot_tn(normed, dqkv_ref[...]).astype(BF)
        dwq_ref[cols, :] = grads[:, :span]
        dwk_ref[cols, :] = grads[:, span : 2 * span]
        dwv_ref[cols, :] = grads[:, 2 * span :]


def attend_back(ranks, heads, seqs, slots, gain_at, d_att, x, inverse, small, w_slices, w_all, cosine, sine, q, k, v, lse):
    total, width = d_att.shape
    span = slots * HEAD_DIM
    shape = jax.ShapeDtypeStruct
    return vmem_call(
        functools.partial(attend_back_kernel, ranks, heads, seqs, slots, gain_at),
        [shape((total, width), BF)] + [shape((width, span), BF)] * 3 + [shape((1, width), F32)],
        d_att, x, inverse, small, *w_slices, w_all, cosine, sine, q, k, v, lse,
        scratch_shapes=[
            pltpu.VMEM((total, span), BF),
            pltpu.VMEM((total, 3 * span), BF),
            pltpu.VMEM((total // seqs, HEAD_DIM), F32),
            pltpu.VMEM((total // seqs, HEAD_DIM), F32),
            pltpu.VMEM((span, width), BF),
        ],
        name="attend_back",
    )


def experts_kernel(
    ranks, count, steps, share, n_ref, c_ref, packed_ref, wg_ref, wu_ref, wd_ref, pack_ref, sd_ref,
    n_group, c_group, w_group,
    out_ref, dx_ref, dpack_ref, dsd_ref, n_all, c_all, w_all, send, recv,
):
    step = pl.program_id(0)
    me = lax.axis_index("expert")
    names = ranks * count
    part = c_all.shape[-1]
    moves = [
        SameExperts(w_group, w_all, send.at[1], recv.at[1]),
        Across(lambda r: n_group.at[r], n_all, send.at[0], recv.at[0]),
        Across(lambda r: c_group.at[r, pl.ds(n_ref.shape[1] - part, part)], c_all, send.at[2], recv.at[2]),
    ]

    @pl.when(step == 0)
    def _():
        meet(moves[0].peers() + moves[1].peers())
        for move in moves:
            move.start()

    @pl.when(step == min(1, steps - 1))
    def _():
        for move in moves:
            move.more()

    @pl.when(step == steps // 2)
    def _():
        for move in moves:
            move.relay()

    @pl.when(step == steps - 1)
    def _():
        for move in moves:
            move.hand_over()

    n = n_ref[...]
    c_b = c_ref[...]
    c = c_b.astype(F32)
    products = dot(n, pack_ref[...])
    gate, up = products[:, :share], products[:, share : 2 * share]
    hidden = (silu(gate) * up).astype(BF)
    out = dot(hidden, sd_ref[...])
    d_gate_s, d_up_s = swiglu_back(dot_nt(c_b, sd_ref[...]), gate, up)

    @pl.when(step == 0)
    def _():
        dpack_ref[...] = jnp.zeros_like(dpack_ref)
        dsd_ref[...] = jnp.zeros_like(dsd_ref)

    dsd_ref[...] += dot_tn(hidden, c_b)
    probs = route_probs(products, 2 * share, names)
    name = lax.broadcasted_iota(jnp.int32, probs.shape, 1)
    d_log = jnp.zeros_like(probs)
    inner = jnp.zeros((n.shape[0], 1), F32)
    dx = jnp.zeros(c.shape, F32)
    for j in range(count):
        weight = packed_ref[:, j : j + 1].astype(F32) + packed_ref[:, count + j : count + j + 1].astype(F32)
        gate = dot(n, wg_ref[j])
        up = dot(n, wu_ref[j])
        hidden = (silu(gate) * up).astype(BF)
        y = dot(hidden, wd_ref[j]).astype(BF).astype(F32)
        out += weight * y
        d_weight = weight * jnp.sum(c * y, -1, keepdims=True)
        d_log += jnp.where(name == me * count + j, d_weight, 0.0)
        inner += d_weight
        d_gate, d_up = swiglu_back(dot_nt((weight * c).astype(BF), wd_ref[j]), gate, up)
        dx += dot_nt(d_gate, wg_ref[j]) + dot_nt(d_up, wu_ref[j])
    d_log = (d_log - probs * inner).astype(BF)
    rest = jnp.zeros((n.shape[0], pack_ref.shape[1] - 2 * share - names), BF)
    d_products = jnp.concatenate([d_gate_s, d_up_s, d_log, rest], -1)
    dx += dot_nt(d_products, pack_ref[...])
    dpack_ref[...] += dot_tn(n, d_products)
    out_ref[...] = out.astype(BF)
    dx_ref[...] = dx.astype(BF)

    @pl.when(step == steps - 1)
    def _():
        for move in moves:
            move.finish()


def experts(ranks, lanes, normed, cot, packed, w_gate, w_up, w_down, pack, s_down):
    total, width = normed.shape
    count, _, hidden = w_gate.shape
    tile = 256 if total % 256 == 0 else total
    steps = total // tile
    share = s_down.shape[0]
    anywhere = pl.BlockSpec(memory_space=pl.ANY)
    dma = pltpu.SemaphoreType.DMA

    def rows(cols):
        return pl.BlockSpec((tile, cols), lambda i: (i, 0))

    def whole(a):
        zeros = (0,) * a.ndim
        return pl.BlockSpec(a.shape, lambda i: zeros, pipeline_mode=pl.Buffered(1))

    shape = jax.ShapeDtypeStruct
    fixed = (w_gate, w_up, w_down, pack, s_down)
    flops = total * width * hidden * count * 12
    return pl.pallas_call(
        functools.partial(experts_kernel, ranks, count, steps, share),
        grid=(steps,),
        in_specs=[rows(width), rows(width), rows(LANES)] + [whole(a) for a in fixed] + [anywhere] * 3,
        out_specs=[
            rows(width),
            rows(width),
            pl.BlockSpec(pack.shape, lambda i: (0, 0)),
            pl.BlockSpec((share, width), lambda i: (0, 0)),
            anywhere, anywhere, anywhere,
        ],
        out_shape=[
            shape((total, width), BF),
            shape((total, width), BF),
            shape(pack.shape, F32),
            shape((share, width), F32),
            shape((6, total // 2, width), BF),
            shape((6, total // 2, lanes), BF),
            shape((6, total // 2, LANES), BF),
        ],
        scratch_shapes=[dma((3, Across.SEMAPHORES)), dma((3, Across.SEMAPHORES))],
        compiler_params=pltpu.CompilerParams(
            vmem_limit_bytes=VMEM_LIMIT, collective_id=3, has_side_effects=True
        ),
        cost_estimate=pl.CostEstimate(flops=flops, bytes_accessed=30 * 2**20, transcendentals=0),
        name="experts",
    )(normed, cot, packed, *fixed, normed, cot, packed)


def routed_tile(j, count, n, c, packed, w_gate, w_up, w_down, acc_gate, acc_up, acc_down):
    weight = packed[:, j : j + 1].astype(F32) + packed[:, count + j : count + j + 1].astype(F32)
    d_y = jnp.concatenate([(weight * part.astype(F32)).astype(BF) for part in c], -1)
    gate, up = dot(n, w_gate), dot(n, w_up)
    d_gate, d_up = swiglu_back(dot_nt(d_y, w_down), gate, up)
    hidden = (silu(gate) * up).astype(BF)
    acc_gate[...] += dot_tn(n, d_gate)
    acc_up[...] += dot_tn(n, d_up)
    acc_down[...] += dot_tn(hidden, d_y)


def weights_kernel(
    j, count, first, size, own_steps, n_own, c_own, packed_own, n_ref, ca_ref, cb_ref, cc_ref, packed_ref,
    wg_ref, wu_ref, wd_ref, *refs,
):
    dg_ref, du_ref, dd_ref, wg, wu, wd, acc_gate, acc_up, acc_down, load, store = refs[-11:]
    step = pl.program_id(0)
    cols = pl.ds(first, size)

    @pl.when(step == 0)
    def _():
        copies = [
            pltpu.make_async_copy(wg_ref.at[j, :, cols], wg, load.at[0]),
            pltpu.make_async_copy(wu_ref.at[j, :, cols], wu, load.at[1]),
            pltpu.make_async_copy(wd_ref.at[j, cols], wd, load.at[2]),
        ]
        for copy in copies:
            copy.start()
        for acc in (acc_gate, acc_up, acc_down):
            acc[...] = jnp.zeros_like(acc)
        for copy in copies:
            copy.wait()

    ours = step < own_steps
    parts, at = [], 0
    for ref in (ca_ref, cb_ref, cc_ref):
        lanes = ref.shape[-1]
        parts.append(jnp.where(ours, c_own[:, at : at + lanes], ref[0]))
        at += lanes
    routed_tile(
        j, count,
        jnp.where(ours, n_own[...], n_ref[0]),
        parts,
        jnp.where(ours, packed_own[...], packed_ref[0]),
        wg[...], wu[...], wd[...], acc_gate, acc_up, acc_down,
    )

    @pl.when(step == pl.num_programs(0) - 1)
    def _():
        copies = [
            pltpu.make_async_copy(acc_gate, dg_ref.at[j, :, cols], store.at[0]),
            pltpu.make_async_copy(acc_up, du_ref.at[j, :, cols], store.at[1]),
            pltpu.make_async_copy(acc_down, dd_ref.at[j, cols], store.at[2]),
        ]
        for copy in copies:
            copy.start()
        for copy in copies:
            copy.wait()


def expert_weights(j, first, size, tokens, weights, grads=None):
    own, others = tokens
    slots, half, width = others[0].shape
    count = weights[0].shape[0]
    tile = min(512, half)
    per = half // tile
    own_steps = 2 * per

    def own_rows(a):
        return pl.BlockSpec((tile, a.shape[-1]), lambda i: (jnp.minimum(i, own_steps - 1), 0))

    def rows(a):
        def place(i):
            k = jnp.maximum(i - own_steps, 0)
            return k // per, k % per, 0

        return pl.BlockSpec((1, tile, a.shape[-1]), place)

    anywhere = pl.BlockSpec(memory_space=pl.ANY)
    dma = pltpu.SemaphoreType.DMA
    before = [] if grads is None else list(grads)
    return pl.pallas_call(
        functools.partial(weights_kernel, j, count, first, size, own_steps),
        grid=(own_steps + slots * per,),
        in_specs=[own_rows(a) for a in own] + [rows(a) for a in others]
        + [anywhere] * (3 + len(before)),
        out_specs=[anywhere] * 3,
        out_shape=[jax.ShapeDtypeStruct(w.shape, F32) for w in weights],
        scratch_shapes=[
            pltpu.VMEM((width, size), BF), pltpu.VMEM((width, size), BF), pltpu.VMEM((size, width), BF),
            pltpu.VMEM((width, size), F32), pltpu.VMEM((width, size), F32), pltpu.VMEM((size, width), F32),
            dma((3,)), dma((3,)),
        ],
        input_output_aliases={} if grads is None else {11: 0, 12: 1, 13: 2},
        compiler_params=pltpu.CompilerParams(vmem_limit_bytes=VMEM_LIMIT),
        cost_estimate=pl.CostEstimate(
            flops=slots * half * width * size * 12, bytes_accessed=40 * 2**20, transcendentals=0
        ),
        name="expert_weights",
    )(*own, *others, *weights, *before)


class Scatter:
    def __init__(self, part, pair, far, stage, mine, theirs, sems):
        self.me = lax.axis_index("expert")
        self.chips = part.shape[0]
        self.z, self.c = self.me // 2, lax.rem(self.me, 2)
        self.part, self.pair, self.far = part, pair, far
        self.stage, self.mine, self.theirs = stage, mine, theirs
        self.send, self.recv, self.local = sems
        self.near = mine is None

    def swap(self):
        twin = self.me + 1 - 2 * self.c
        return remote(self.part.at[:, 1 - self.c], self.pair, self.send.at[0], self.recv.at[0], expert=twin)

    def own(self):
        return pltpu.make_async_copy(self.part.at[:, self.c], self.stage, self.local.at[0])

    def start(self):
        self.swap().start()
        if self.near:
            self.own().start()

    def hop(self, d):
        to, source = lax.rem(self.z + d, self.chips), lax.rem(self.z + self.chips - d, self.chips)
        out = remote(
            self.stage.at[to], self.far.at[self.z], self.send.at[d], self.recv.at[d], expert=2 * to + self.c
        )
        back = remote(
            self.stage.at[to], self.far.at[source], self.send.at[d], self.recv.at[d], expert=2 * to + self.c
        )
        return out, back

    def load(self, src, dst, k):
        copy = pltpu.make_async_copy(src, dst, self.local.at[k])
        copy.start()
        return copy

    def add_pairs(self):
        if self.near:
            self.own().wait()
        self.swap().wait_recv()

        def one(i, carry):
            if self.near:
                self.stage[i] = (self.stage[i].astype(F32) + self.pair[i].astype(F32)).astype(BF)
                return carry
            copies = [self.load(self.part.at[i, self.c], self.mine, 0), self.load(self.pair.at[i], self.theirs, 1)]
            for copy in copies:
                copy.wait()
            self.stage[i] = (self.mine[...].astype(F32) + self.theirs[...].astype(F32)).astype(BF)
            return carry

        lax.fori_loop(0, self.chips, one, 0)
        for d in range(1, self.chips):
            self.hop(d)[0].start()

    def total(self):
        acc = self.stage[self.z].astype(F32)
        for d in range(1, self.chips):
            self.hop(d)[1].wait_recv()
            source = lax.rem(self.z + self.chips - d, self.chips)
            if self.near:
                acc += self.far[source].astype(F32)
            else:
                self.load(self.far.at[source], self.mine, 0).wait()
                acc += self.mine[...].astype(F32)
        return acc

    def finish(self):
        self.swap().wait_send()
        for d in range(1, self.chips):
            self.hop(d)[0].wait_send()


def tail_kernel(
    ranks, groups, heads, slots, j, count,
    dn_ref, dwq_ref, dwk_ref, dwv_ref, dpack_ref,
    n_own, c_own, packed_own, n_all, ca_all, cb_all, cc_all, packed_all, wg_ref, wu_ref, wd_ref,
    dn_sum, all_ref, dg_ref, du_ref, dd_ref, *refs,
):
    if dn_ref.shape[0] > 4:
        pair, far, mine, theirs = refs[:2] + refs[-2:]
        refs = refs[2:-2]
    else:
        pair, far = refs[-2:]
        mine = theirs = None
        refs = refs[:-2]
    (
        n_buf, c_buf, p_buf, wg, wu, wd, acc_gate, acc_up, acc_down, got_ref, sum_ref, stage,
        a_send, a_recv, a_local, r_send, r_recv, t_send, t_recv, g_send, g_recv,
        e_send, e_recv, load, fetched,
    ) = refs
    me, g = lax.axis_index("expert"), lax.axis_index("dp")
    width = n_own.shape[1]
    rows = width // ranks
    tile = n_buf.shape[1]
    half = n_all.shape[1]
    per = half // tile
    own_steps = 2 * per
    steps = own_steps + n_all.shape[0] * per
    parts, at = [], 0
    for ref in (ca_all, cb_all, cc_all):
        parts.append(pl.ds(at, ref.shape[-1]))
        at += ref.shape[-1]
    peers = [lax.rem(g + d, groups) for d in range(1, groups)]
    others = [lax.rem(me + d, ranks) for d in range(1, ranks)]
    banks = (dwq_ref, dwk_ref, dwv_ref, dpack_ref)

    meet([{"expert": t} for t in others] + [{"dp": t} for t in peers])
    first = Scatter(dn_ref, pair, far, stage, mine, theirs, (a_send, a_recv, a_local))
    first.start()

    def slot(s):
        return slice(s * LANES, (s + 1) * LANES)

    def has(s, i, group):
        return jnp.logical_or(group == groups - 1, head_of(s, i, ranks) < heads)

    def reduce_copy(d, s, which):
        return remote(
            banks[which].at[:, slot(s)], got_ref.at[d - 1, :, slot(s)], r_send.at[d, s], r_recv.at[d, s], dp=peers[d - 1]
        )

    for d in range(1, groups):
        for s in range(slots):
            for which in range(groups):
                ok = jnp.logical_and(peers[d - 1] == which, has(s, me, which))
                pl.when(ok)(lambda: reduce_copy(d, s, which).start())

    def fetch(t, into):
        def ours():
            r = aligned(t, tile)
            return n_own.at[r], packed_own.at[r], *(c_own.at[r, part] for part in parts)

        def theirs_():
            k = t - own_steps
            r = aligned(lax.rem(k, per), tile)
            return tuple(ref.at[k // per, r] for ref in (n_all, packed_all, ca_all, cb_all, cc_all))

        def go(sources):
            for k, copy in enumerate(tile_copies(sources, into)):
                copy.start()

        pl.when(t < own_steps)(lambda: go(ours()))
        pl.when(t >= own_steps)(lambda: go(theirs_()))

    def tile_copies(sources, into):
        targets = (n_buf.at[into], p_buf.at[into], *(c_buf.at[into, :, part] for part in parts))
        return [
            pltpu.make_async_copy(src, dst, fetched.at[into, k]) for k, (src, dst) in enumerate(zip(sources, targets))
        ]

    fetch(0, 0)
    copies = [
        pltpu.make_async_copy(wg_ref.at[j], wg, load.at[0]),
        pltpu.make_async_copy(wu_ref.at[j], wu, load.at[1]),
        pltpu.make_async_copy(wd_ref.at[j], wd, load.at[2]),
    ]
    for copy in copies:
        copy.start()
    for acc in (acc_gate, acc_up, acc_down):
        acc[...] = jnp.zeros_like(acc)
    for copy in copies:
        copy.wait()

    def turn_copy(d, s, i, to):
        return remote(
            sum_ref.at[to, :, slot(s)], all_ref.at[g, i, :, slot(s)], t_send.at[d, s], t_recv.at[d, s], expert=to
        )

    def add_groups():
        for s in range(slots):
            def one(s=s):
                for d in range(1, groups):
                    reduce_copy(d, s, 0).wait_recv()
                for which in range(groups):
                    def add(which=which):
                        for r in range(ranks):
                            here = slice(r * rows, (r + 1) * rows)
                            acc = banks[which][here, slot(s)].astype(F32)
                            for d in range(1, groups):
                                acc += got_ref[d - 1, here, slot(s)].astype(F32)
                            sum_ref[r, :, slot(s)] = acc.astype(BF)

                    pl.when(g == which)(add)
                all_ref[g, me, :, slot(s)] = sum_ref[me, :, slot(s)]
                for d in range(1, ranks):
                    turn_copy(d, s, me, others[d - 1]).start()

            pl.when(has(s, me, g))(one)

    def spread(d, s, group, to):
        if (s + 1) * ranks <= heads:
            part = all_ref.at[group, :, :, slot(s)]
            return [(True, remote(part, part, g_send.at[d, s], g_recv.at[d, s], dp=to))]
        whole = all_ref.at[group, :, :, slot(s)]
        found = [(group == groups - 1, remote(whole, whole, g_send.at[d, s], g_recv.at[d, s], dp=to))]
        for k, i in enumerate(i for i in range(ranks) if head_of(s, i, ranks) < heads):
            part = all_ref.at[group, i, :, slot(s)]
            found.append((group != groups - 1, remote(part, part, e_send.at[d, k], e_recv.at[d, k], dp=to)))
        return found

    def spread_out():
        for d in range(1, ranks):
            i = lax.rem(me + ranks - d, ranks)
            for s in range(slots):
                pl.when(has(s, i, g))(lambda: turn_copy(d, s, i, others[0]).wait_recv())
        for d in range(1, groups):
            for s in range(slots):
                for ok, copy in spread(d, s, g, peers[d - 1]):
                    guarded(ok, copy.start)

    def keep_first():
        dn_sum[...] = first.total()

    hooks = [None, first.add_pairs, None, add_groups, None, spread_out, None, keep_first]

    def step(t, carry):
        now = lax.rem(t, 2)
        pl.when(t + 1 < steps)(lambda: fetch(t + 1, 1 - now))
        r = pl.ds(0, tile)
        for copy in tile_copies((n_own.at[r], packed_own.at[r], *(c_own.at[r, part] for part in parts)), now):
            copy.wait()
        routed_tile(
            j, count, n_buf[now], [c_buf[now]], p_buf[now],
            wg[...], wu[...], wd[...], acc_gate, acc_up, acc_down,
        )
        for k, hook in enumerate(hooks):
            if hook is not None:
                pl.when(t == k * steps // len(hooks))(hook)
        return carry

    lax.fori_loop(0, steps, step, 0)
    stores = [
        pltpu.make_async_copy(acc_gate, dg_ref, load.at[0]),
        pltpu.make_async_copy(acc_up, du_ref, load.at[1]),
        pltpu.make_async_copy(acc_down, dd_ref, load.at[2]),
    ]
    for copy in stores:
        copy.start()
    first.finish()
    for d in range(1, groups):
        source = lax.rem(g + groups - d, groups)
        for s in range(slots):
            pl.when(has(s, me, peers[d - 1]))(lambda: reduce_copy(d, s, 0).wait_send())
            for ok, copy in spread(d, s, source, peers[d - 1]):
                guarded(ok, copy.wait_recv)
            for ok, copy in spread(d, s, g, peers[d - 1]):
                guarded(ok, copy.wait_send)
    for d in range(1, ranks):
        for s in range(slots):
            pl.when(has(s, me, g))(lambda: turn_copy(d, s, me, others[d - 1]).wait_send())
    for copy in stores:
        copy.wait()


def tail(ranks, groups, heads, slots, j, d_normed, d_weights, tokens, weights):
    own_tokens, others = tokens
    half, width = others[0].shape[1:]
    count, _, hidden = weights[0].shape
    chips = ranks // 2
    total = d_normed.shape[0]
    own = total // ranks
    rows = width // ranks
    span = slots * LANES
    tile = min(512, half)
    dma = pltpu.SemaphoreType.DMA
    shape = jax.ShapeDtypeStruct
    vmem, anywhere = pl.BlockSpec(memory_space=pltpu.VMEM), pl.BlockSpec(memory_space=pl.ANY)
    block = shape((chips, own, width), BF)
    near = chips <= 4
    return pl.pallas_call(
        functools.partial(tail_kernel, ranks, groups, heads, slots, j, count),
        out_shape=[
            shape((own, width), F32), shape((groups, ranks, rows, span), BF),
            shape((width, hidden), F32), shape((width, hidden), F32), shape((hidden, width), F32),
        ]
        + [block] * (0 if near else 2),
        in_specs=[anywhere] + [vmem] * 4 + [anywhere] * 11,
        out_specs=[vmem] * 2 + [anywhere] * (3 if near else 5),
        scratch_shapes=[
            pltpu.VMEM((2, tile, width), BF), pltpu.VMEM((2, tile, width), BF), pltpu.VMEM((2, tile, LANES), BF),
            pltpu.VMEM((width, hidden), BF), pltpu.VMEM((width, hidden), BF), pltpu.VMEM((hidden, width), BF),
            pltpu.VMEM((width, hidden), F32), pltpu.VMEM((width, hidden), F32), pltpu.VMEM((hidden, width), F32),
            pltpu.VMEM((groups - 1, width, span), BF), pltpu.VMEM((ranks, rows, span), BF),
            pltpu.VMEM((chips, own, width), BF),
            dma((chips,)), dma((chips,)), dma((2,)),
            dma((groups, slots)), dma((groups, slots)),
            dma((ranks, slots)), dma((ranks, slots)),
            dma((groups, slots)), dma((groups, slots)),
            dma((groups, ranks)), dma((groups, ranks)),
            dma((3,)), dma((2, 5)),
        ]
        + ([pltpu.VMEM((chips, own, width), BF)] * 2 if near else [pltpu.VMEM((own, width), BF)] * 2),
        compiler_params=pltpu.CompilerParams(
            vmem_limit_bytes=VMEM_LIMIT, collective_id=4, has_side_effects=True
        ),
        cost_estimate=pl.CostEstimate(flops=total * groups * width * hidden * 12, bytes_accessed=2**26, transcendentals=0),
        name="tail",
    )(
        d_normed.reshape(chips, 2, own, width), *d_weights,
        *own_tokens, *others, *weights,
    )[:5]


def outputs_kernel(
    heads, slots, j, gain_at, dn_ref, out_ref, resid_ref, dres_ref, x_ref, gain_ref, all_ref, wo_ref, sd_ref,
    eg_ref, eu_ref, ed_ref, bg_ref, bu_ref, bd_ref,
    layer_ref, dx_ref, q_ref, k_ref, v_ref, o_ref, sg_ref, su_ref, dsd_ref, small_ref, dg_ref, du_ref, dd_ref, store,
):
    copies = [
        pltpu.make_async_copy(src, dst.at[j], store.at[k])
        for k, (src, dst) in enumerate(((eg_ref, dg_ref), (eu_ref, du_ref), (ed_ref, dd_ref)))
    ]
    for copy in copies:
        copy.start()
    layer_ref[...] = (resid_ref[...] + out_ref[...].astype(F32)).astype(BF)
    x = x_ref[...].astype(F32)
    inverse = lax.rsqrt(jnp.mean(x * x, -1, keepdims=True) + EPS)
    dx_ref[...] = (dres_ref[...] + norm_back(dn_ref[...], x, inverse, gain_ref[gain_at : gain_at + 1, :])).astype(BF)
    ranks = all_ref.shape[1]
    share = sg_ref.shape[1] // ranks
    for which, ref in enumerate((q_ref, k_ref, v_ref)):
        for h in range(heads):
            s, i = next((s, i) for s in range(slots) for i in range(ranks) if head_of(s, i, ranks) == h)
            ref[:, h * LANES : (h + 1) * LANES] = all_ref[which, i, :, s * LANES : (s + 1) * LANES].astype(F32)
    last = all_ref.shape[0] - 1
    small = jnp.zeros(small_ref.shape, F32)
    for i in range(ranks):
        here = all_ref[last, i].astype(F32)
        sg_ref[:, i * share : (i + 1) * share] = here[:, :share]
        su_ref[:, i * share : (i + 1) * share] = here[:, share : 2 * share]
        small += here
    small_ref[...] = small
    o_ref[...] = wo_ref[...].astype(F32)
    dsd_ref[...] = sd_ref[...].astype(F32)
    for copy in copies:
        copy.wait()


def outputs(heads, slots, j, gain_at, share_width, arrays, last_grads, grads):
    dn, out, resid, d_resid, x, gain, everything, d_wo, d_sd = arrays
    rows, span = everything.shape[2:]
    own, width = x.shape
    shape = jax.ShapeDtypeStruct
    vmem, anywhere = pl.BlockSpec(memory_space=pltpu.VMEM), pl.BlockSpec(memory_space=pl.ANY)
    return pl.pallas_call(
        functools.partial(outputs_kernel, heads, slots, j, gain_at),
        out_shape=[shape((own, width), BF)] * 2
        + [shape((rows, width), F32)] * 4
        + [shape((rows, share_width), F32)] * 2
        + [shape(d_sd.shape, F32), shape((rows, span), F32)]
        + [shape(a.shape, F32) for a in grads],
        in_specs=[vmem] * 12 + [anywhere] * 3,
        out_specs=[vmem] * 10 + [anywhere] * 3,
        scratch_shapes=[pltpu.SemaphoreType.DMA((3,))],
        input_output_aliases={12: 10, 13: 11, 14: 12},
        compiler_params=pltpu.CompilerParams(vmem_limit_bytes=VMEM_LIMIT),
        name="outputs",
    )(*arrays, *last_grads, *grads)


def norm_back(grad, values, inverse, gain):
    scaled = grad * gain
    inner = jnp.mean(scaled * values, -1, keepdims=True)
    return inverse * scaled - values * inverse**3 * inner


def body(
    tokens, cotangent, attn_gain, ffn_gain, w_query, w_key, w_value, w_output, router,
    shared_gate, shared_up, shared_down, expert_gate, expert_up, expert_down, expert_ids,
):
    ranks = lax.axis_size("expert")
    me = lax.axis_index("expert")
    seqs, own_pos, width = tokens.shape
    length = own_pos * ranks
    total = seqs * length
    own = seqs * own_pos
    rows = w_query.shape[0]
    heads = width // HEAD_DIM
    slots = -(-heads // ranks)
    span = slots * HEAD_DIM
    share = shared_gate.shape[1] // ranks
    names = router.shape[1]
    count = expert_gate.shape[0]

    groups = lax.axis_size("dp")

    def in_order(a):
        return a.reshape(ranks, seqs, own_pos, -1).transpose(1, 0, 2, 3).reshape(total, -1)

    def by_rank(a):
        return a.reshape(seqs, ranks, own_pos, -1).transpose(1, 0, 2, 3).reshape(total, -1)

    def by_share(w):
        return w.reshape(rows, ranks, share).transpose(1, 0, 2)

    def to_all(w):
        return jnp.broadcast_to(w[None], (ranks,) + w.shape)

    pieces = [
        by_share(shared_gate), by_share(shared_up), to_all(router), to_all(attn_gain[:, None]), to_all(ffn_gain[:, None]),
    ]
    edges = [0]
    for p in pieces:
        edges.append(edges[-1] + p.shape[-1])
    pack = jnp.concatenate(pieces, -1)
    pack = jnp.pad(pack, ((0, 0), (0, 0), (0, span - edges[-1])))
    gain_at = edges[3] - (slots - 1) * LANES
    top = expert_ids.shape[-1]
    extended = jnp.concatenate(
        [
            cotangent.reshape(own, width),
            expert_ids.reshape(own, top).astype(BF),
            jnp.zeros((own, -top % LANES), BF),
        ],
        -1,
    )
    group_x, group_c, w_q, w_k, w_v, w_pack, small, half_out = front(
        ranks, groups, heads, slots, tokens.reshape(own, width), extended, w_query, w_key, w_value, pack, w_output
    )
    group_c = group_c.reshape(total, -1)
    gain_two = small[gain_at + 1 : gain_at + 2]
    cosine, sine = rotary_tables(length)
    units = width // LANES
    c_first, c_last = max(units // 5, 1) * LANES, max(3 * units // 10, 1) * LANES
    c_middle = width - c_first - c_last
    inverse_one, q, k, v, mixed, lse, all_ca = attend(
        seqs, slots, gain_at, c_first, in_order(group_x), small, w_q, w_k, w_v, cosine, sine, group_c
    )

    resid, normed_two, all_mixed, all_out, packed, all_cb = project(
        ranks, groups, heads, slots, count, top, edges[2], c_first, c_middle, group_x, by_rank(mixed), half_out, small, w_pack, group_c
    )
    layer_part, d_normed_part, d_pack, d_s_down, all_n, all_cc, all_w = experts(
        ranks, c_last, normed_two, group_c, packed, expert_gate, expert_up, expert_down, w_pack, shared_down
    )
    every = ((normed_two, group_c, packed), (all_n, all_ca, all_cb, all_cc, all_w))
    banks = (expert_gate, expert_up, expert_down)
    hidden = expert_gate.shape[-1]
    cut = hidden * 4 // 7 if hidden % (7 * LANES) == 0 else hidden // 2

    def after(late, *earlier):
        return lax.optimization_barrier((late, earlier))[0]

    def scatter(partial):
        return lax.psum_scatter(partial, "expert", scatter_dimension=0, tiled=True)

    grads = expert_weights(0, 0, cut, every, banks)
    d_normed_two, grads = lax.optimization_barrier((scatter(d_normed_part), grads))
    d_normed_two = d_normed_two.astype(F32)
    inverse_two = lax.rsqrt(jnp.mean(resid * resid, -1, keepdims=True) + EPS)
    ffn_gain_part = jnp.sum(d_normed_two * resid * inverse_two, 0)
    d_out = cotangent.reshape(own, width).astype(F32)
    d_resid = d_out + norm_back(d_normed_two, resid, inverse_two, gain_two)
    own_att = d_resid.astype(BF)
    d_att = lax.all_gather(own_att, "expert", axis=0, tiled=True)
    grads = expert_weights(0, cut, hidden - cut, after(every, own_att), banks, grads)
    d_att, grads = lax.optimization_barrier((d_att, grads))

    d_normed_part, d_wq, d_wk, d_wv, attn_gain_part = attend_back(
        ranks, heads, seqs, slots, gain_at, in_order(d_att), in_order(group_x), inverse_one, small,
        (w_q, w_k, w_v), all_out, cosine, sine, q, k, v, lse
    )
    column = jnp.arange(span)[None, :]
    d_pack = jnp.where(column == edges[3], attn_gain_part.reshape(width, 1), d_pack)
    d_pack = jnp.where(column == edges[4], ffn_gain_part[:, None], d_pack).astype(BF)
    own_mixed = lax.dynamic_slice_in_dim(all_mixed, me * rows, rows, 1)
    d_wo_rows = dot_tn(own_mixed, d_att).astype(BF)
    d_wo_rows, d_sd_rows = lax.psum((d_wo_rows, d_s_down.astype(BF)), "dp")
    dn_sum, all_grads, *last_grads = tail(
        ranks, groups, heads, slots, 1, by_rank(d_normed_part), (d_wq, d_wk, d_wv, d_pack), every, banks
    )
    layer_output, input_grad, g_q, g_k, g_v, g_o, g_sg, g_su, g_sd, small, g_gate, g_up, g_down = outputs(
        heads, slots, 1, gain_at, ranks * share,
        (dn_sum, scatter(after(layer_part, d_att)), resid, d_resid, tokens.reshape(own, width), small, all_grads, d_wo_rows, d_sd_rows),
        last_grads, grads,
    )
    g_r = small[:, edges[2] : edges[3]]
    g_one = small[:, edges[3]]
    g_two = small[:, edges[4]]
    return (
        layer_output.reshape(tokens.shape), input_grad.reshape(tokens.shape),
        g_one, g_two, g_q, g_k, g_v, g_o, g_r, g_sg, g_su, g_sd, g_gate, g_up, g_down,
    )


def solution(mesh):
    row = P("expert", None)
    experts_spec = P("expert", None, None)
    tokens_spec = P("dp", "expert", None)
    return jax.shard_map(
        body,
        mesh=mesh,
        in_specs=(tokens_spec, tokens_spec, P("expert"), P("expert"))
        + (row,) * 8
        + (experts_spec,) * 3
        + (P(("dp", "expert"), None, None),),
        out_specs=(tokens_spec, tokens_spec, P("expert"), P("expert")) + (row,) * 8 + (experts_spec,) * 3,
        check_vma=False,
    )
```

```python
import functools

import jax
import jax.numpy as jnp
from jax import lax
from jax.experimental import pallas as pl
from jax.experimental.pallas import tpu as pltpu
from jax.sharding import PartitionSpec as P

HEAD_DIM = 128
LANES = 128
TURNED = 16
EPS = 1e-06
MASKED = -1e30
VMEM_LIMIT = 60 * 2**20
BF = jnp.bfloat16
F32 = jnp.float32


def dot(a, b):
    return jnp.dot(a, b, preferred_element_type=F32)


def dot_nt(a, b):
    return lax.dot_general(a, b, (((1,), (1,)), ((), ())), preferred_element_type=F32)


def dot_tn(a, b):
    return lax.dot_general(a, b, (((0,), (0,)), ((), ())), preferred_element_type=F32)


def silu(v):
    return v / (1.0 + jnp.exp(-v))


def swiglu_back(d_hidden, gates, ups):
    sigma = 1.0 / (1.0 + jnp.exp(-gates))
    d_gate = d_hidden * ups * sigma * (1.0 + gates * (1.0 - sigma))
    d_up = d_hidden * (gates * sigma)
    return d_gate.astype(BF), d_up.astype(BF)


def rotary_tables(length):
    half = HEAD_DIM // 2
    inverse_freq = 10000.0 ** (-jnp.arange(half, dtype=F32) * 2.0 / HEAD_DIM)
    angles = jnp.arange(length).astype(F32)[:, None] * inverse_freq[None, :]
    cosine, sine = jnp.cos(angles), jnp.sin(angles)
    return jnp.concatenate([cosine, cosine], -1), jnp.concatenate([-sine, sine], -1)


def vmem_call(kernel, outs, *args, **kwargs):
    spec = pl.BlockSpec(memory_space=pltpu.VMEM)
    return pl.pallas_call(
        kernel,
        out_shape=outs,
        in_specs=[spec] * len(args),
        out_specs=[spec] * len(outs),
        compiler_params=pltpu.CompilerParams(vmem_limit_bytes=VMEM_LIMIT),
        **kwargs,
    )(*args)


def row_block(length):
    return 256 if length % 256 == 0 else length


def remote(src, dst, send, recv, **device):
    return pltpu.make_async_remote_copy(
        src_ref=src, dst_ref=dst, send_sem=send, recv_sem=recv, device_id=device, device_id_type=pl.DeviceIdType.MESH
    )


def meet(peers):
    barrier = pltpu.get_barrier_semaphore()
    for peer in peers:
        pl.semaphore_signal(barrier, inc=1, device_id=peer, device_id_type=pl.DeviceIdType.MESH)
    pl.semaphore_wait(barrier, len(peers))


def meet_near(chips, z, me, peers=()):
    barrier = pltpu.get_barrier_semaphore()
    near = [(True, {"expert": me + 1 - 2 * lax.rem(me, 2)}), (z > 0, {"expert": me - 2}), (z < chips - 1, {"expert": me + 2})]
    near += [(True, {"dp": t}) for t in peers]

    def signal(t):
        pl.semaphore_signal(barrier, inc=1, device_id=t, device_id_type=pl.DeviceIdType.MESH)

    for ok, t in near:
        guarded(ok, functools.partial(signal, t))
    ends = jnp.where(z > 0, 1, 0) + jnp.where(z < chips - 1, 1, 0)
    pl.semaphore_wait(barrier, 1 + len(peers) + ends)


def both(*conditions):
    held = [c for c in conditions if c is not True]
    if not held:
        return True
    out = held[0]
    for c in held[1:]:
        out = jnp.logical_and(out, c)
    return out


def guarded(condition, action):
    if condition is True:
        action()
    else:
        pl.when(condition)(action)


class LineGather:
    def __init__(self, ranks, own, block, send, recv, base=0, valid=lambda i: True, twins=True):
        self.me = lax.axis_index("expert")
        self.chips = ranks // 2
        self.z = self.me // 2
        self.twin = self.me + 1 - 2 * lax.rem(self.me, 2)
        self.own, self.block, self.send, self.recv, self.base, self.valid = own, block, send, recv, base, valid
        self.twins = twins

    @staticmethod
    def semaphores(ranks):
        return 4 * (ranks // 2 - 1) + 1

    def copy(self, src, i, k, to):
        return remote(src, self.block(i), self.send.at[self.base + k], self.recv.at[self.base + k], expert=to)

    def sources(self, s):
        hops = self.chips - 1
        return (
            (self.me - 2 * s, self.z - s >= 0, self.z < hops, self.me + 2, 0, 2 * hops, -2 * s),
            (self.me + 2 * s, self.z + s <= hops, self.z > 0, self.me - 2, hops, 3 * hops, 2 * s),
        )

    def start(self):
        hops = self.chips - 1
        mine = self.valid(self.me)
        if hops:
            guarded(both(self.z < hops, mine), lambda: self.copy(self.own, self.me, 0, self.me + 2).start())
            guarded(both(self.z > 0, mine), lambda: self.copy(self.own, self.me, hops, self.me - 2).start())
        if self.twins:
            guarded(mine, lambda: self.copy(self.own, self.me, 2 * hops, self.twin).start())

    def step(self, s):
        for i, there, more, to, k, pair, _ in self.sources(s):
            known = both(there, self.valid(i))
            src = self.block(i)
            guarded(known, lambda: self.copy(src, i, k + s - 1, self.twin).wait_recv())
            if s < self.chips - 1:
                guarded(both(known, more), lambda: self.copy(src, i, k + s, to).start())
            if self.twins:
                guarded(known, lambda: self.copy(src, i, pair + s, self.twin).start())

    def finish(self):
        hops = self.chips - 1
        mine = self.valid(self.me)
        theirs = self.valid(self.twin)
        if self.twins:
            guarded(mine, lambda: self.copy(self.own, self.me, 2 * hops, self.twin).wait_send())
            guarded(theirs, lambda: self.copy(self.own, self.twin, 2 * hops, self.twin).wait_recv())
        if hops:
            guarded(both(self.z < hops, mine), lambda: self.copy(self.own, self.me, 0, self.twin).wait_send())
            guarded(both(self.z > 0, mine), lambda: self.copy(self.own, self.me, hops, self.twin).wait_send())
        for s in range(1, self.chips):
            for i, there, more, to, k, pair, shift in self.sources(s):
                known = both(there, self.valid(i))
                src = self.block(i)
                if s < hops:
                    guarded(both(known, more), lambda: self.copy(src, i, k + s, self.twin).wait_send())
                if not self.twins:
                    continue
                guarded(known, lambda: self.copy(src, i, pair + s, self.twin).wait_send())
                j = self.twin + shift
                got = both(there, self.valid(j))
                guarded(got, lambda: self.copy(self.block(j), j, pair + s, self.twin).wait_recv())


class Across:
    SEMAPHORES = 12

    def __init__(self, source, dst, send, recv):
        self.me, self.g = lax.axis_index("expert"), lax.axis_index("dp")
        self.twin = self.me + 1 - 2 * lax.rem(self.me, 2)
        self.by_x = self.g + 1 - 2 * lax.rem(self.g, 2)
        self.by_y = lax.rem(self.g + 2, 4)
        self.source, self.dst, self.send, self.recv = source, dst, send, recv
        self.half = dst.shape[1]
        self.part = self.half // 2

    def peers(self):
        return [{"dp": self.by_x}, {"dp": self.by_y}, {"expert": self.twin}]

    def piece(self, slot, j):
        return self.dst.at[slot, pl.ds(j * self.part, self.part)]

    def mine(self, j):
        first = lax.rem(self.me, 2) * self.half + j * self.part
        return self.source(pl.ds(pl.multiple_of(first, self.part), self.part))

    def copy(self, k, src, dst, **to):
        return remote(src, dst, self.send.at[k], self.recv.at[k], **to)

    def direct(self, k):
        slot, j, to = ((0, 0, self.by_x), (1, 1, self.by_y), (0, 1, self.by_x), (1, 0, self.by_y))[k]
        return self.copy(k, self.mine(j), self.piece(slot, j), dp=to)

    def relayed(self, j):
        if j == 0:
            return self.copy(4, self.piece(0, 0), self.piece(2, 0), dp=self.by_y)
        return self.copy(5, self.piece(1, 1), self.piece(2, 1), dp=self.by_x)

    def shared(self, slot, j):
        return self.copy(6 + 2 * slot + j, self.piece(slot, j), self.piece(slot + 3, j), expert=self.twin)

    def start(self):
        for k in range(2):
            self.direct(k).start()

    def more(self):
        for k in range(2, 4):
            self.direct(k).start()

    def relay(self):
        self.direct(0).wait_recv()
        self.relayed(0).start()
        self.direct(1).wait_recv()
        self.relayed(1).start()
        self.shared(0, 0).start()
        self.shared(1, 1).start()

    def hand_over(self):
        self.direct(2).wait_recv()
        self.shared(0, 1).start()
        self.direct(3).wait_recv()
        self.shared(1, 0).start()

    def finish(self):
        for j in range(2):
            self.relayed(j).wait_recv()
            self.shared(2, j).start()
        for k in range(4):
            self.direct(k).wait_send()
        for j in range(2):
            self.relayed(j).wait_send()
            for slot in range(3):
                self.shared(slot, j).wait()


class SameExperts:
    SEMAPHORES = 6

    def __init__(self, source, dst, send, recv):
        self.me, self.g = lax.axis_index("expert"), lax.axis_index("dp")
        self.near = [self.g + 1 - 2 * lax.rem(self.g, 2), lax.rem(self.g + 2, 4)]
        self.near.append(self.near[1] + 1 - 2 * lax.rem(self.near[1], 2))
        self.source, self.dst, self.send, self.recv = source, dst, send, recv
        self.half = dst.shape[2]

    def peers(self):
        return [{"dp": self.near[2]}]

    def copy(self, k, h):
        slot = k + 3 * lax.rem(lax.rem(self.me, 2) + h, 2)
        i = 2 * k + h
        src = self.source.at[:, pl.ds(h * self.half, self.half)]
        return remote(src, self.dst.at[slot], self.send.at[i], self.recv.at[i], dp=self.near[k])

    def start(self):
        for k in range(3):
            for h in range(2):
                self.copy(k, h).start()

    def relay(self):
        pass

    hand_over = more = relay

    def finish(self):
        for k in range(3):
            for h in range(2):
                self.copy(k, h).wait()


def head_of(s, i, ranks):
    return i if s == 0 else s * ranks + i // 2 + (i % 2) * (ranks // 2)


def aligned(i, size):
    return pl.ds(pl.multiple_of(i * size, size), size)


def front_kernel(
    ranks, groups, heads, seqs, slots, gain_at,
    x_ref, c_ref, id_ref, wq_ref, wk_ref, wv_ref, sg_ref, su_ref, rest_ref, wo_ref, cos_ref, sin_ref,
    gx_ref, gc_ref, wqs_ref, wks_ref, wvs_ref, wps_ref, small_ref, half_ref,
    inv_ref, q_ref, k_ref, v_ref, mixed_ref, lse_ref, stage_ref, land_ref, ostage_ref,
    x_send, x_recv, c_send, c_recv, w_send, w_recv, d_send, d_recv, o_send, o_recv, p_send, p_recv,
):
    me, g = lax.axis_index("expert"), lax.axis_index("dp")
    rows, width = wq_ref.shape
    units = width // LANES
    per = ostage_ref.shape[0]
    peers = [lax.rem(g + d, groups) for d in range(1, groups)]
    others = [lax.rem(me + d, ranks) for d in range(1, ranks)]
    meet([{"expert": t} for t in others] + [{"dp": t} for t in peers])

    def stage_heads(w):
        for u in range(heads):
            stage_ref[u] = w[:, u * LANES : (u + 1) * LANES]

    for which, w in enumerate((wq_ref, wk_ref, wv_ref)):
        pl.when(g == which)(functools.partial(stage_heads, w))

    def stage_pack():
        share = sg_ref.shape[1] // ranks
        spare = slots * LANES - 2 * share - rest_ref.shape[1]
        for t in range(ranks):
            cols = slice(t * share, (t + 1) * share)
            pieces = [sg_ref[:, cols], su_ref[:, cols], rest_ref[...]]
            if spare:
                pieces.append(jnp.zeros((rows, spare), BF))
            packed = jnp.concatenate(pieces, -1)
            for s in range(slots):
                stage_ref[head_of(s, t, ranks)] = packed[:, s * LANES : (s + 1) * LANES]

    pl.when(g == groups - 1)(stage_pack)

    def known(s, t, group=None):
        return jnp.logical_or((g if group is None else group) == groups - 1, head_of(s, t, ranks) < heads)

    def weight_copy(s, d, unit, i, to):
        return remote(
            stage_ref.at[unit], land_ref.at[g, s, i], w_send.at[s, d], w_recv.at[s, d], expert=to
        )

    for d in range(1, ranks):
        t = others[d - 1]
        for s in range(slots):
            guarded(known(s, t), lambda: weight_copy(s, d, head_of(s, t, ranks), me, t).start())

    def stage_out(which):
        for k in range(per):
            u = which * per + k
            if u < units:
                ostage_ref[k] = wo_ref[:, u * LANES : (u + 1) * LANES]

    for which in range(groups):
        pl.when(g == which)(functools.partial(stage_out, which))
    out_rows = LineGather(
        ranks, ostage_ref, lambda i: half_ref.at[g, :, i // 2], o_send, o_recv, twins=False
    )
    out_rows.start()
    tokens = LineGather(ranks, x_ref, lambda i: gx_ref.at[i], x_send, x_recv)
    tokens.start()
    half_ref[g, :, me // 2] = ostage_ref[...]
    for s in range(slots):
        def keep(s=s):
            land_ref[g, s, me] = stage_ref[head_of(s, me, ranks)]

        pl.when(known(s, me))(keep)
        for which in range(groups - 1):
            def clear(s=s, which=which):
                land_ref[which, s] = jnp.zeros(land_ref.shape[2:], BF)

            pl.when(head_of(s, me, ranks) >= heads)(clear)
    gx_ref[me] = x_ref[...]
    gc_ref[me, :, :width] = c_ref[...]
    routes = id_ref[...].astype(F32).astype(BF)
    blank = jnp.zeros((routes.shape[0], LANES - routes.shape[1]), BF)
    gc_ref[me, :, width:] = jnp.concatenate([routes, blank], -1)

    def share(s, part, d, to):
        return remote(part, part, d_send.at[s, d], d_recv.at[s, d], dp=to)

    def pass_on(i):
        for s in range(slots):
            part = land_ref.at[g, s, i]
            for d in range(1, groups):
                pl.when(known(s, me))(lambda: share(s, part, d, peers[d - 1]).start())

    def out_share(d, k, group):
        part = half_ref.at[group, k]
        return remote(part, part, p_send.at[d, k], p_recv.at[d, k], dp=peers[d - 1])

    def held(group, k):
        return True if (groups - 1) * per + k < units else group * per + k < units

    pass_on(me)
    for d in range(1, ranks):
        i = lax.rem(me + ranks - d, ranks)
        for s in range(slots):
            pl.when(known(s, me))(lambda: weight_copy(s, d, 0, i, others[0]).wait_recv())
        pass_on(i)
    steps = ranks // 2 - 1
    for step in range(1, steps + 1):
        out_rows.step(step)
        if step == 1:
            tokens.step(1)
    out_rows.finish()
    for d in range(1, groups):
        for k in range(per):
            guarded(held(g, k), out_share(d, k, g).start)
    cots = LineGather(ranks, gc_ref.at[me], lambda i: gc_ref.at[i], c_send, c_recv)
    for step in range(2, steps + 1):
        tokens.step(step)
        if step == steps - 1:
            cots.start()
    if steps < 3:
        cots.start()
    tokens.finish()
    for d in range(1, groups):
        there = lax.rem(g + groups - d, groups)
        for s in range(slots):
            pl.when(known(s, me, there))(lambda: share(s, land_ref.at[there, s], d, peers[d - 1]).wait_recv())
    for which, ref in enumerate((wqs_ref, wks_ref, wvs_ref, wps_ref)):
        for s in range(slots):
            for r in range(ranks):
                ref[r * rows : (r + 1) * rows, s * LANES : (s + 1) * LANES] = land_ref[which, s, r]
    small_ref[...] = jnp.transpose(wps_ref[:, (slots - 1) * LANES :].astype(F32))
    attend(
        seqs, slots, gain_at, gx_ref, small_ref, wqs_ref, wks_ref, wvs_ref, cos_ref, sin_ref,
        inv_ref, q_ref, k_ref, v_ref, mixed_ref, lse_ref,
        [functools.partial(cots.step, step) for step in range(1, steps + 1)],
    )
    cots.finish()
    for d in range(1, ranks):
        t = others[d - 1]
        for s in range(slots):
            pl.when(known(s, t))(lambda: weight_copy(s, d, 0, me, t).wait_send())
    for d in range(1, groups):
        there = lax.rem(g + groups - d, groups)
        for s in range(slots):
            pl.when(known(s, me))(lambda: share(s, land_ref.at[g, s], d, peers[d - 1]).wait_send())
        for k in range(per):
            guarded(held(g, k), out_share(d, k, g).wait_send)
            guarded(held(there, k), out_share(d, k, there).wait_recv)


def front(
    ranks, groups, heads, seqs, slots, gain_at, x, cot, ids, w_query, w_key, w_value, s_gate, s_up, rest, w_output,
    cosine, sine,
):
    own, width = x.shape
    total, span = ranks * own, slots * LANES
    rows = w_query.shape[0]
    per = -(-(width // LANES) // groups)
    line = LineGather.semaphores(ranks)
    dma = pltpu.SemaphoreType.DMA
    spec = pl.BlockSpec(memory_space=pltpu.VMEM)
    shape = jax.ShapeDtypeStruct
    return pl.pallas_call(
        functools.partial(front_kernel, ranks, groups, heads, seqs, slots, gain_at),
        out_shape=[shape((ranks, own, width), BF), shape((ranks, own, width + LANES), BF)]
        + [shape((width, slots * LANES), BF)] * 4
        + [shape((LANES, width), F32), shape((groups, per, ranks // 2, rows, LANES), BF)]
        + [shape((total, 1), F32)]
        + [shape((total, span), BF)] * 4
        + [shape((total, slots), F32)],
        in_specs=[spec] * 12,
        out_specs=[spec] * 14,
        scratch_shapes=[
            pltpu.VMEM((slots * ranks, rows, LANES), BF),
            pltpu.VMEM((groups, slots, ranks, rows, LANES), BF),
            pltpu.VMEM((per, rows, LANES), BF),
            dma((line,)), dma((line,)),
            dma((line,)), dma((line,)),
            dma((slots, ranks)), dma((slots, ranks)),
            dma((slots, groups)), dma((slots, groups)),
            dma((line,)), dma((line,)),
            dma((groups, per)), dma((groups, per)),
        ],
        compiler_params=pltpu.CompilerParams(
            collective_id=0, has_side_effects=True, vmem_limit_bytes=VMEM_LIMIT
        ),
        name="front",
    )(x, cot, ids, w_query, w_key, w_value, s_gate, s_up, rest, w_output, cosine, sine)


def project_kernel(
    ranks, groups, heads, slots, count, top, route_at,
    x_ref, mixed_ref, half_ref, small_ref, pack_ref, c_ref,
    resid_ref, n_ref, all_ref, wo_ref, packed_ref, turned_ref, c_all_ref, other_ref, id_ref,
    send, recv, t_send, t_recv, a_send, a_recv, load,
):
    me, g = lax.axis_index("expert"), lax.axis_index("dp")
    chips = ranks // 2
    z = me // 2
    twin = me + 1 - 2 * lax.rem(me, 2)
    per, part = half_ref.shape[1], half_ref.shape[3]
    units = wo_ref.shape[1] // LANES
    peers = [lax.rem(g + d, groups) for d in range(1, groups)]
    lanes = c_all_ref.shape[-1]
    across = Across(lambda r: c_ref.at[r, pl.ds(0, lanes)], c_all_ref, a_send, a_recv)
    meet_near(chips, z, me, peers)
    ids = pltpu.make_async_copy(c_ref.at[:, pl.ds(wo_ref.shape[1], LANES)], id_ref, load)
    ids.start()
    line = LineGather.semaphores(ranks)
    parts = []
    for s in range(slots):
        def head(i, s=s):
            return aligned(jnp.clip(head_of(s, i, ranks), 0, heads - 1), LANES)

        cols = slice(s * LANES, (s + 1) * LANES)
        ok = (lambda i: True) if (s + 1) * ranks <= heads else (lambda i, s=s: head_of(s, i, ranks) < heads)
        gather = LineGather(
            ranks, mixed_ref.at[:, cols], lambda i, head=head: all_ref.at[:, head(i)], send, recv, s * line, ok
        )
        gather.start()
        parts.append(gather)

    across.start()
    across.more()
    for s, gather in enumerate(parts):
        def keep(s=s):
            cols = slice(s * LANES, (s + 1) * LANES)
            all_ref[:, aligned(jnp.clip(head_of(s, me, ranks), 0, heads - 1), LANES)] = mixed_ref[:, cols]

        guarded(gather.valid(me), keep)

    def share_twin(group, k):
        src = half_ref.at[group, k]
        return remote(src, other_ref.at[group, k], t_send.at[group, k], t_recv.at[group, k], expert=twin)

    def each_unit(action):
        for group in range(groups):
            for k in range(per):
                if group * per + k < units:
                    action(share_twin(group, k))

    each_unit(lambda copy: copy.start())
    middle = (chips + 1) // 2
    for step in range(1, chips):
        for gather in parts:
            gather.step(step)
        if step == middle:
            across.relay()
    for gather in parts:
        gather.finish()
    each_unit(lambda copy: copy.wait())
    ids.wait()

    def lay_out(even, odd):
        for u in range(units):
            cols = slice(u * LANES, (u + 1) * LANES)
            for c in range(chips):
                wo_ref[2 * c * part : (2 * c + 1) * part, cols] = even[u // per, u % per, c]
                wo_ref[(2 * c + 1) * part : (2 * c + 2) * part, cols] = odd[u // per, u % per, c]

    pl.when(me == 2 * z)(lambda: lay_out(half_ref, other_ref))
    pl.when(me != 2 * z)(lambda: lay_out(other_ref, half_ref))
    blocks, own, width = x_ref.shape
    names = ranks * count
    gain_at = route_at + names + 1 - (slots - 1) * LANES
    gain = small_ref[gain_at : gain_at + 1, :]
    tile = 2 if own <= 128 and blocks % 2 == 0 else 1

    def rows_of(b):
        rows = aligned(b, tile * own)
        x = x_ref[pl.ds(b * tile, tile)].reshape(tile * own, width).astype(F32)
        resid = x + dot(all_ref[rows, :], wo_ref[...])
        inverse = lax.rsqrt(jnp.mean(resid * resid, -1, keepdims=True) + EPS)
        normed = (resid * inverse * gain).astype(BF)
        n_ref[rows, :] = normed
        for t in range(tile):
            def keep(t=t):
                resid_ref[...] = resid[t * own : (t + 1) * own]

            pl.when(b * tile + t == me)(keep)
        probs = route_probs(dot(normed, pack_ref[...]), route_at, names)
        routes = id_ref[rows, :].astype(jnp.int32)
        lane = lax.broadcasted_iota(jnp.int32, routes.shape, 1)
        out = jnp.zeros((tile * own, LANES), F32)
        for j in range(count):
            mine = me * count + j
            chosen = jnp.max(jnp.where((routes == mine) & (lane < top), 1.0, 0.0), -1, keepdims=True)
            names_at = lax.broadcasted_iota(jnp.int32, probs.shape, 1)
            weight = chosen * jnp.sum(jnp.where(names_at == mine, probs, 0.0), -1, keepdims=True)
            high = weight.astype(BF).astype(F32)
            out = jnp.where(lane == j, high, out)
            out = jnp.where(lane == count + j, weight - high, out)
        packed_ref[rows, :] = out.astype(BF)
        turned_ref[:, rows] = jnp.transpose(out)[:turned_ref.shape[0]].astype(BF)

    half = blocks // tile // 2
    lax.fori_loop(0, half, lambda b, c: (rows_of(b), c)[1], 0)
    across.hand_over()
    lax.fori_loop(half, blocks // tile, lambda b, c: (rows_of(b), c)[1], 0)
    across.finish()


def route_probs(products, first, names):
    logits = products[:, first : first + names]
    raised = jnp.exp(logits - jnp.max(logits, -1, keepdims=True))
    return raised / jnp.sum(raised, -1, keepdims=True)


def project(ranks, groups, heads, slots, count, top, route_at, lanes, x, mixed, half, small, pack, cot):
    blocks, own, width = x.shape
    total = blocks * own
    line = LineGather.semaphores(ranks)
    per = half.shape[1]
    dma = pltpu.SemaphoreType.DMA
    spec = pl.BlockSpec(memory_space=pltpu.VMEM)
    anywhere = pl.BlockSpec(memory_space=pl.ANY)
    shape = jax.ShapeDtypeStruct
    return pl.pallas_call(
        functools.partial(project_kernel, ranks, groups, heads, slots, count, top, route_at),
        out_shape=[
            shape((own, width), F32),
            shape((total, width), BF),
            shape((total, width), BF),
            shape((width, width), BF),
            shape((total, LANES), BF),
            shape((TURNED, total), BF),
            shape((6, total // 2, lanes), BF),
        ],
        in_specs=[spec] * 5 + [anywhere],
        out_specs=[spec] * 6 + [anywhere],
        scratch_shapes=[
            pltpu.VMEM(half.shape, BF), pltpu.VMEM((total, LANES), BF),
            dma((slots * line,)), dma((slots * line,)),
            dma((groups, per)), dma((groups, per)),
            dma((Across.SEMAPHORES,)), dma((Across.SEMAPHORES,)), dma(()),
        ],
        compiler_params=pltpu.CompilerParams(
            collective_id=1, has_side_effects=True, vmem_limit_bytes=VMEM_LIMIT
        ),
        name="project",
    )(x, mixed, half, small, pack, cot)


def attend(
    seqs, slots, gain_at, x_ref, small_ref, wq_ref, wk_ref, wv_ref, cos_ref, sin_ref,
    inv_ref, q_ref, k_ref, v_ref, mixed_ref, lse_ref, hooks,
):
    ranks, own, width = x_ref.shape
    pos = own // seqs
    length = ranks * pos
    block = row_block(length)
    count = block // pos
    scale = HEAD_DIM ** (-0.5)
    gain = small_ref[gain_at : gain_at + 1, :]
    hooks = list(hooks)

    def progress():
        if hooks:
            hooks.pop(0)()

    for s in range(seqs):
        for i in range(length // block):
            rows = pl.ds(s * length + i * block, block)
            x = [x_ref[e, s * pos : (s + 1) * pos, :] for e in range(i * count, (i + 1) * count)]
            x = jnp.concatenate(x, 0).astype(F32)
            inv = lax.rsqrt(jnp.mean(x * x, -1, keepdims=True) + EPS)
            normed = (x * inv * gain).astype(BF)
            inv_ref[rows, :] = inv
            cosine = cos_ref[pl.ds(i * block, block), :]
            sine = sin_ref[pl.ds(i * block, block), :]
            queries, keyed, valued = dot(normed, wq_ref[...]), dot(normed, wk_ref[...]), dot(normed, wv_ref[...])
            for h in range(slots):
                cols = slice(h * HEAD_DIM, (h + 1) * HEAD_DIM)
                q, k = queries[:, cols], keyed[:, cols]
                q_ref[rows, cols] = (q * cosine + pltpu.roll(q, HEAD_DIM // 2, 1) * sine).astype(BF)
                k_ref[rows, cols] = (k * cosine + pltpu.roll(k, HEAD_DIM // 2, 1) * sine).astype(BF)
            v_ref[rows, :] = valued.astype(BF)
    progress()
    for s in range(seqs):
        for i in range(length // block):
            if i:
                progress()
            rows = pl.ds(s * length + i * block, block)
            keys = pl.ds(s * length, (i + 1) * block)
            shape = (block, (i + 1) * block)
            seen = (
                lax.broadcasted_iota(jnp.int32, shape, 1)
                <= lax.broadcasted_iota(jnp.int32, shape, 0) + i * block
            )
            for h in range(slots):
                cols = slice(h * HEAD_DIM, (h + 1) * HEAD_DIM)
                scores = dot_nt(q_ref[rows, cols], k_ref[keys, cols]) * scale
                scores = jnp.where(seen, scores, MASKED)
                top = jnp.max(scores, -1, keepdims=True)
                raised = jnp.exp(scores - top)
                totals = jnp.sum(raised, -1, keepdims=True)
                probs = (raised / totals).astype(BF)
                mixed_ref[rows, cols] = dot(probs, v_ref[keys, cols]).astype(BF)
                lse_ref[rows, h : h + 1] = top + jnp.log(totals)
    while hooks:
        progress()


def attend_back_kernel(
    ranks, heads, seqs, slots, gain_at, da_ref, x_ref, inv_ref, small_ref, wq_ref, wk_ref, wv_ref, wall_ref,
    cos_ref, sin_ref,
    q_ref, k_ref, v_ref, lse_ref,
    dn_ref, dwq_ref, dwk_ref, dwv_ref, gain_ref, dmix_ref, dqkv_ref, dk_ref, dv_ref, wo_ref,
):
    total, width = da_ref.shape
    length = total // seqs
    block = row_block(length)
    count = length // block
    scale = HEAD_DIM ** (-0.5)
    span = slots * HEAD_DIM
    me = lax.axis_index("expert")
    for h in range(slots):
        cols = slice(h * HEAD_DIM, (h + 1) * HEAD_DIM)
        head = head_of(h, me, ranks)
        rows_here = wall_ref[aligned(jnp.minimum(head, heads - 1), HEAD_DIM), :]
        wo_ref[cols, :] = jnp.where(head < heads, rows_here, jnp.zeros_like(rows_here))
    for s in range(seqs):
        for i in range(count):
            rows = pl.ds(s * length + i * block, block)
            dmix_ref[rows, :] = dot_nt(da_ref[rows, :], wo_ref[...]).astype(BF)
        for h in range(slots):
            cols = slice(h * HEAD_DIM, (h + 1) * HEAD_DIM)
            dk_ref[...] = jnp.zeros_like(dk_ref)
            dv_ref[...] = jnp.zeros_like(dv_ref)
            for i in range(count):
                rows = pl.ds(s * length + i * block, block)
                reach = (i + 1) * block
                keys = pl.ds(s * length, reach)
                shape = (block, reach)
                seen = (
                    lax.broadcasted_iota(jnp.int32, shape, 1)
                    <= lax.broadcasted_iota(jnp.int32, shape, 0) + i * block
                )
                q = q_ref[rows, cols]
                k = k_ref[keys, cols]
                dmix = dmix_ref[rows, cols]
                scores = jnp.where(seen, dot_nt(q, k) * scale, MASKED)
                probs = jnp.exp(scores - lse_ref[rows, h : h + 1])
                dp = dot_nt(dmix, v_ref[keys, cols])
                delta = jnp.sum(probs * dp, -1, keepdims=True)
                ds = (probs * (dp - delta)).astype(BF)
                dq = dot(ds, k) * scale
                cosine = cos_ref[pl.ds(i * block, block), :]
                sine = sin_ref[pl.ds(i * block, block), :]
                dqkv_ref[rows, h * HEAD_DIM : (h + 1) * HEAD_DIM] = (
                    dq * cosine - pltpu.roll(dq, HEAD_DIM // 2, 1) * sine
                ).astype(BF)
                dk_ref[pl.ds(0, reach), :] += dot_tn(ds, q)
                dv_ref[pl.ds(0, reach), :] += dot_tn(probs.astype(BF), dmix)
            for i in range(count):
                rows = pl.ds(s * length + i * block, block)
                here = pl.ds(i * block, block)
                dk = dk_ref[here, :] * scale
                dk = dk * cos_ref[here, :] - pltpu.roll(dk, HEAD_DIM // 2, 1) * sin_ref[here, :]
                dqkv_ref[rows, span + h * HEAD_DIM : span + (h + 1) * HEAD_DIM] = dk.astype(BF)
                dqkv_ref[rows, 2 * span + h * HEAD_DIM : 2 * span + (h + 1) * HEAD_DIM] = dv_ref[here, :].astype(BF)
    gain = jnp.zeros((1, width), F32)
    for i in range(total // block):
        rows = pl.ds(i * block, block)
        d_normed = dot_nt(dqkv_ref[rows, :span], wq_ref[...])
        d_normed += dot_nt(dqkv_ref[rows, span : 2 * span], wk_ref[...])
        d_normed += dot_nt(dqkv_ref[rows, 2 * span :], wv_ref[...])
        dn_ref[rows, :] = d_normed.astype(BF)
        gain += jnp.sum(d_normed * x_ref[rows, :].astype(F32) * inv_ref[rows, :], 0, keepdims=True)
    gain_ref[...] = gain
    step = LANES * 2
    for i in range(width // step):
        cols = slice(i * step, (i + 1) * step)
        normed = (x_ref[:, cols].astype(F32) * inv_ref[...] * small_ref[gain_at : gain_at + 1, cols]).astype(BF)
        grads = dot_tn(normed, dqkv_ref[...]).astype(BF)
        dwq_ref[cols, :] = grads[:, :span]
        dwk_ref[cols, :] = grads[:, span : 2 * span]
        dwv_ref[cols, :] = grads[:, 2 * span :]


def attend_back(ranks, heads, seqs, slots, gain_at, d_att, x, inverse, small, w_slices, w_all, cosine, sine, q, k, v, lse):
    total, width = d_att.shape
    span = slots * HEAD_DIM
    shape = jax.ShapeDtypeStruct
    return vmem_call(
        functools.partial(attend_back_kernel, ranks, heads, seqs, slots, gain_at),
        [shape((total, width), BF)] + [shape((width, span), BF)] * 3 + [shape((1, width), F32)],
        d_att, x, inverse, small, *w_slices, w_all, cosine, sine, q, k, v, lse,
        scratch_shapes=[
            pltpu.VMEM((total, span), BF),
            pltpu.VMEM((total, 3 * span), BF),
            pltpu.VMEM((total // seqs, HEAD_DIM), F32),
            pltpu.VMEM((total // seqs, HEAD_DIM), F32),
            pltpu.VMEM((span, width), BF),
        ],
        name="attend_back",
    )


def experts_kernel(
    ranks, count, steps, share, n_ref, c_ref, packed_ref, wg_ref, wu_ref, wd_ref, pack_ref, sd_ref,
    n_group, c_group, w_group,
    out_ref, dx_ref, dpack_ref, dsd_ref, n_all, c_all, w_all, og_ref, ou_ref, od_ref, send, recv,
):
    step = pl.program_id(0)
    me = lax.axis_index("expert")
    names = ranks * count
    part = c_all.shape[-1]
    moves = [
        SameExperts(w_group, w_all, send.at[1], recv.at[1]),
        Across(lambda r: n_group.at[r], n_all, send.at[0], recv.at[0]),
        Across(lambda r: c_group.at[r, pl.ds(n_ref.shape[1] - part, part)], c_all, send.at[2], recv.at[2]),
    ]

    @pl.when(step == 0)
    def _():
        meet(moves[0].peers() + moves[1].peers())
        for move in moves:
            move.start()

    @pl.when(step == min(1, steps - 1))
    def _():
        for move in moves:
            move.more()

    @pl.when(step == steps // 2)
    def _():
        for move in moves:
            move.relay()

    @pl.when(step == steps - 1)
    def _():
        for move in moves:
            move.hand_over()

    n = n_ref[...]
    c_b = c_ref[...]
    c = c_b.astype(F32)
    products = dot(n, pack_ref[...])
    gate, up = products[:, :share], products[:, share : 2 * share]
    hidden = (silu(gate) * up).astype(BF)
    out = dot(hidden, sd_ref[...])
    d_gate_s, d_up_s = swiglu_back(dot_nt(c_b, sd_ref[...]), gate, up)

    @pl.when(step == 0)
    def _():
        for ref in (dpack_ref, dsd_ref, og_ref, ou_ref, od_ref):
            ref[...] = jnp.zeros_like(ref)

    dsd_ref[...] += dot_tn(hidden, c_b)
    probs = route_probs(products, 2 * share, names)
    name = lax.broadcasted_iota(jnp.int32, probs.shape, 1)
    d_log = jnp.zeros_like(probs)
    inner = jnp.zeros((n.shape[0], 1), F32)
    dx = jnp.zeros(c.shape, F32)
    for j in range(count):
        weight = packed_ref[:, j : j + 1].astype(F32) + packed_ref[:, count + j : count + j + 1].astype(F32)
        gate = dot(n, wg_ref[j])
        up = dot(n, wu_ref[j])
        hidden = (silu(gate) * up).astype(BF)
        y = dot(hidden, wd_ref[j]).astype(BF).astype(F32)
        out += weight * y
        d_weight = weight * jnp.sum(c * y, -1, keepdims=True)
        d_log += jnp.where(name == me * count + j, d_weight, 0.0)
        inner += d_weight
        d_y = (weight * c).astype(BF)
        d_gate, d_up = swiglu_back(dot_nt(d_y, wd_ref[j]), gate, up)
        dx += dot_nt(d_gate, wg_ref[j]) + dot_nt(d_up, wu_ref[j])
        if j == count - 1:
            og_ref[...] += dot_tn(n, d_gate)
            ou_ref[...] += dot_tn(n, d_up)
            od_ref[...] += dot_tn(hidden, d_y)
    d_log = (d_log - probs * inner).astype(BF)
    rest = jnp.zeros((n.shape[0], pack_ref.shape[1] - 2 * share - names), BF)
    d_products = jnp.concatenate([d_gate_s, d_up_s, d_log, rest], -1)
    dx += dot_nt(d_products, pack_ref[...])
    dpack_ref[...] += dot_tn(n, d_products)
    out_ref[...] = out.astype(BF)
    dx_ref[...] = dx.astype(BF)

    @pl.when(step == steps - 1)
    def _():
        for move in moves:
            move.finish()


def experts(ranks, lanes, normed, cot, packed, turned, w_gate, w_up, w_down, pack, s_down):
    total, width = normed.shape
    count, _, hidden = w_gate.shape
    tile = 256 if total % 256 == 0 else total
    steps = total // tile
    share = s_down.shape[0]
    anywhere = pl.BlockSpec(memory_space=pl.ANY)
    dma = pltpu.SemaphoreType.DMA

    def rows(cols):
        return pl.BlockSpec((tile, cols), lambda i: (i, 0))

    def whole(a):
        zeros = (0,) * a.ndim
        return pl.BlockSpec(a.shape, lambda i: zeros, pipeline_mode=pl.Buffered(1))

    shape = jax.ShapeDtypeStruct
    fixed = (w_gate, w_up, w_down, pack, s_down)
    flops = total * width * hidden * count * 12
    return pl.pallas_call(
        functools.partial(experts_kernel, ranks, count, steps, share),
        grid=(steps,),
        in_specs=[rows(width), rows(width), rows(LANES)] + [whole(a) for a in fixed] + [anywhere] * 3,
        out_specs=[
            rows(width),
            rows(width),
            pl.BlockSpec(pack.shape, lambda i: (0, 0)),
            pl.BlockSpec((share, width), lambda i: (0, 0)),
            anywhere, anywhere, anywhere,
            *(pl.BlockSpec(a.shape[1:], lambda i: (0, 0), pipeline_mode=pl.Buffered(1)) for a in fixed[:3]),
        ],
        out_shape=[
            shape((total, width), BF),
            shape((total, width), BF),
            shape(pack.shape, F32),
            shape((share, width), F32),
            shape((6, total // 2, width), BF),
            shape((6, total // 2, lanes), BF),
            shape((6, TURNED, total // 2), BF),
            *(shape(a.shape[1:], F32) for a in fixed[:3]),
        ],
        scratch_shapes=[dma((3, Across.SEMAPHORES)), dma((3, Across.SEMAPHORES))],
        compiler_params=pltpu.CompilerParams(
            vmem_limit_bytes=VMEM_LIMIT, collective_id=3, has_side_effects=True
        ),
        cost_estimate=pl.CostEstimate(flops=flops, bytes_accessed=30 * 2**20, transcendentals=0),
        name="experts",
    )(normed, cot, packed, *fixed, normed, cot, turned)


def weight_of(packed, j, count):
    return packed[:, j : j + 1].astype(F32) + packed[:, count + j : count + j + 1].astype(F32)


def routed_tile(n, c, weight, w_gate, w_up, w_down, acc_gate, acc_up, acc_down):
    d_y = jnp.concatenate([(weight * part.astype(F32)).astype(BF) for part in c], -1)
    gate, up = dot(n, w_gate), dot(n, w_up)
    d_gate, d_up = swiglu_back(dot_nt(d_y, w_down), gate, up)
    hidden = (silu(gate) * up).astype(BF)
    acc_gate[...] += dot_tn(n, d_gate)
    acc_up[...] += dot_tn(n, d_up)
    acc_down[...] += dot_tn(hidden, d_y)


def weights_kernel(
    j, count, first, size, own_steps, n_own, c_own, packed_own, n_ref, ca_ref, cb_ref, packed_ref,
    wg_ref, wu_ref, wd_ref, *refs,
):
    dg_ref, du_ref, dd_ref, wg, wu, wd, acc_gate, acc_up, acc_down, load, store = refs[-11:]
    step = pl.program_id(0)
    cols = pl.ds(first, size)

    @pl.when(step == 0)
    def _():
        copies = [
            pltpu.make_async_copy(wg_ref.at[j, :, cols], wg, load.at[0]),
            pltpu.make_async_copy(wu_ref.at[j, :, cols], wu, load.at[1]),
            pltpu.make_async_copy(wd_ref.at[j, cols], wd, load.at[2]),
        ]
        for copy in copies:
            copy.start()
        for acc in (acc_gate, acc_up, acc_down):
            acc[...] = jnp.zeros_like(acc)
        for copy in copies:
            copy.wait()

    ours = step < own_steps
    parts, at = [], 0
    for ref in (ca_ref, cb_ref):
        lanes = ref.shape[-1]
        parts.append(jnp.where(ours, c_own[:, at : at + lanes], ref[...]))
        at += lanes
    theirs = [jnp.transpose(packed_ref[k].astype(F32)) for k in range(packed_ref.shape[0])]
    theirs = weight_of(jnp.concatenate(theirs, 0), j, count)
    routed_tile(
        jnp.where(ours, n_own[...], n_ref[...]),
        parts,
        jnp.where(ours, weight_of(packed_own[...], j, count), theirs),
        wg[...], wu[...], wd[...], acc_gate, acc_up, acc_down,
    )

    @pl.when(step == pl.num_programs(0) - 1)
    def _():
        copies = [
            pltpu.make_async_copy(acc_gate, dg_ref.at[j, :, cols], store.at[0]),
            pltpu.make_async_copy(acc_up, du_ref.at[j, :, cols], store.at[1]),
            pltpu.make_async_copy(acc_down, dd_ref.at[j, cols], store.at[2]),
        ]
        for copy in copies:
            copy.start()
        for copy in copies:
            copy.wait()


def expert_weights(j, first, size, tokens, weights, grads=None):
    own, others = tokens
    width = own[0].shape[1]
    count = weights[0].shape[0]
    turned = others[-1]
    others = [a.reshape(-1, a.shape[-1]) for a in others[:-1]]
    tile = min(1024, own[0].shape[0])
    own_steps = own[0].shape[0] // tile
    steps = own_steps + others[0].shape[0] // tile

    def own_rows(a):
        return pl.BlockSpec((tile, a.shape[-1]), lambda i: (jnp.minimum(i, own_steps - 1), 0))

    def rows(a):
        return pl.BlockSpec((tile, a.shape[-1]), lambda i: (jnp.maximum(i - own_steps, 0), 0))

    half = turned.shape[-1]
    if tile >= half:
        turned_spec = pl.BlockSpec((tile // half, TURNED, half), lambda i: (jnp.maximum(i - own_steps, 0), 0, 0))
    else:
        def place(i):
            k = jnp.maximum(i - own_steps, 0)
            return k // (half // tile), 0, k % (half // tile)

        turned_spec = pl.BlockSpec((1, TURNED, tile), place)

    anywhere = pl.BlockSpec(memory_space=pl.ANY)
    dma = pltpu.SemaphoreType.DMA
    before = [] if grads is None else list(grads)
    return pl.pallas_call(
        functools.partial(weights_kernel, j, count, first, size, own_steps),
        grid=(steps,),
        in_specs=[own_rows(a) for a in own] + [rows(a) for a in others] + [turned_spec]
        + [anywhere] * (3 + len(before)),
        out_specs=[anywhere] * 3,
        out_shape=[jax.ShapeDtypeStruct(w.shape, F32) for w in weights],
        scratch_shapes=[
            pltpu.VMEM((width, size), BF), pltpu.VMEM((width, size), BF), pltpu.VMEM((size, width), BF),
            pltpu.VMEM((width, size), F32), pltpu.VMEM((width, size), F32), pltpu.VMEM((size, width), F32),
            dma((3,)), dma((3,)),
        ],
        input_output_aliases={} if grads is None else {10: 0, 11: 1, 12: 2},
        compiler_params=pltpu.CompilerParams(vmem_limit_bytes=VMEM_LIMIT),
        cost_estimate=pl.CostEstimate(
            flops=steps * tile * width * size * 12, bytes_accessed=40 * 2**20, transcendentals=0
        ),
        name="expert_weights",
    )(*own, *others, turned, *weights, *before)


class Scatter:
    def __init__(self, part, pair, far, stage, mine, theirs, sems):
        self.me = lax.axis_index("expert")
        self.chips = part.shape[0]
        self.z, self.c = self.me // 2, lax.rem(self.me, 2)
        self.part, self.pair, self.far = part, pair, far
        self.stage, self.mine, self.theirs = stage, mine, theirs
        self.send, self.recv, self.local = sems
        self.near = mine is None

    def swap(self):
        twin = self.me + 1 - 2 * self.c
        return remote(self.part.at[:, 1 - self.c], self.pair, self.send.at[0], self.recv.at[0], expert=twin)

    def own(self):
        return pltpu.make_async_copy(self.part.at[:, self.c], self.stage, self.local.at[0])

    def start(self):
        self.swap().start()
        if self.near:
            self.own().start()

    def hop(self, d):
        to, source = lax.rem(self.z + d, self.chips), lax.rem(self.z + self.chips - d, self.chips)
        out = remote(
            self.stage.at[to], self.far.at[self.z], self.send.at[d], self.recv.at[d], expert=2 * to + self.c
        )
        back = remote(
            self.stage.at[to], self.far.at[source], self.send.at[d], self.recv.at[d], expert=2 * to + self.c
        )
        return out, back

    def load(self, src, dst, k):
        copy = pltpu.make_async_copy(src, dst, self.local.at[k])
        copy.start()
        return copy

    def add_pairs(self):
        if self.near:
            self.own().wait()
        self.swap().wait_recv()

        def one(i, carry):
            if self.near:
                self.stage[i] = (self.stage[i].astype(F32) + self.pair[i].astype(F32)).astype(BF)
                return carry
            copies = [self.load(self.part.at[i, self.c], self.mine, 0), self.load(self.pair.at[i], self.theirs, 1)]
            for copy in copies:
                copy.wait()
            self.stage[i] = (self.mine[...].astype(F32) + self.theirs[...].astype(F32)).astype(BF)
            return carry

        lax.fori_loop(0, self.chips, one, 0)
        for d in range(1, self.chips):
            self.hop(d)[0].start()

    def total(self):
        acc = self.stage[self.z].astype(F32)
        for d in range(1, self.chips):
            self.hop(d)[1].wait_recv()
            source = lax.rem(self.z + self.chips - d, self.chips)
            if self.near:
                acc += self.far[source].astype(F32)
            else:
                self.load(self.far.at[source], self.mine, 0).wait()
                acc += self.mine[...].astype(F32)
        return acc

    def finish(self):
        self.swap().wait_send()
        for d in range(1, self.chips):
            self.hop(d)[0].wait_send()


def tail_kernel(
    ranks, groups, heads, slots, j, count,
    dn_ref, dwq_ref, dwk_ref, dwv_ref, dpack_ref,
    n_all, ca_all, cb_all, packed_all, wg_ref, wu_ref, wd_ref, og_ref, ou_ref, od_ref,
    dn_sum, all_ref, dg_ref, du_ref, dd_ref, *refs,
):
    if dn_ref.shape[0] > 4:
        pair, far, mine, theirs = refs[:2] + refs[-2:]
        refs = refs[2:-2]
    else:
        pair, far = refs[-2:]
        mine = theirs = None
        refs = refs[:-2]
    (
        n_buf, c_buf, p_buf, wg, wu, wd, acc_gate, acc_up, acc_down, got_ref, sum_ref, stage,
        a_send, a_recv, a_local, r_send, r_recv, t_send, t_recv, g_send, g_recv,
        e_send, e_recv, load, fetched,
    ) = refs
    me, g = lax.axis_index("expert"), lax.axis_index("dp")
    width = n_all.shape[2]
    rows = width // ranks
    tile = n_buf.shape[1]
    half = n_all.shape[1]
    per = half // tile
    steps = n_all.shape[0] * per
    parts, at = [], 0
    for ref in (ca_all, cb_all):
        parts.append(pl.ds(at, ref.shape[-1]))
        at += ref.shape[-1]
    peers = [lax.rem(g + d, groups) for d in range(1, groups)]
    others = [lax.rem(me + d, ranks) for d in range(1, ranks)]
    banks = (dwq_ref, dwk_ref, dwv_ref, dpack_ref)

    def tile_copies(sources, into):
        targets = (n_buf.at[into], p_buf.at[into], *(c_buf.at[into, :, part] for part in parts))
        return [
            pltpu.make_async_copy(src, dst, fetched.at[into, k]) for k, (src, dst) in enumerate(zip(sources, targets))
        ]

    def fetch(t, into):
        r = aligned(lax.rem(t, per), tile)
        sources = [n_all.at[t // per, r], packed_all.at[t // per, :, r], ca_all.at[t // per, r], cb_all.at[t // per, r]]
        for copy in tile_copies(sources, into):
            copy.start()

    fetch(0, 0)
    copies = [
        pltpu.make_async_copy(src, dst, load.at[k])
        for k, (src, dst) in enumerate((
            (wg_ref.at[j], wg), (wu_ref.at[j], wu), (wd_ref.at[j], wd),
            (og_ref, acc_gate), (ou_ref, acc_up), (od_ref, acc_down),
        ))
    ]
    for copy in copies:
        copy.start()
    meet([{"expert": t} for t in others] + [{"dp": t} for t in peers])
    first = Scatter(dn_ref, pair, far, stage, mine, theirs, (a_send, a_recv, a_local))
    first.start()

    def slot(s):
        return slice(s * LANES, (s + 1) * LANES)

    def has(s, i, group):
        return jnp.logical_or(group == groups - 1, head_of(s, i, ranks) < heads)

    def reduce_copy(d, s, which):
        return remote(
            banks[which].at[:, slot(s)], got_ref.at[d - 1, :, slot(s)], r_send.at[d, s], r_recv.at[d, s], dp=peers[d - 1]
        )

    for d in range(1, groups):
        for s in range(slots):
            for which in range(groups):
                ok = jnp.logical_and(peers[d - 1] == which, has(s, me, which))
                pl.when(ok)(lambda: reduce_copy(d, s, which).start())

    for copy in copies:
        copy.wait()

    def turn_copy(d, s, i, to):
        return remote(
            sum_ref.at[to, :, slot(s)], all_ref.at[g, i, :, slot(s)], t_send.at[d, s], t_recv.at[d, s], expert=to
        )

    def add_groups():
        for s in range(slots):
            def one(s=s):
                for d in range(1, groups):
                    reduce_copy(d, s, 0).wait_recv()
                for which in range(groups):
                    def add(which=which):
                        for r in range(ranks):
                            here = slice(r * rows, (r + 1) * rows)
                            acc = banks[which][here, slot(s)].astype(F32)
                            for d in range(1, groups):
                                acc += got_ref[d - 1, here, slot(s)].astype(F32)
                            sum_ref[r, :, slot(s)] = acc.astype(BF)

                    pl.when(g == which)(add)
                all_ref[g, me, :, slot(s)] = sum_ref[me, :, slot(s)]
                for d in range(1, ranks):
                    turn_copy(d, s, me, others[d - 1]).start()

            pl.when(has(s, me, g))(one)

    def spread(d, s, group, to):
        if (s + 1) * ranks <= heads:
            part = all_ref.at[group, :, :, slot(s)]
            return [(True, remote(part, part, g_send.at[d, s], g_recv.at[d, s], dp=to))]
        whole = all_ref.at[group, :, :, slot(s)]
        found = [(group == groups - 1, remote(whole, whole, g_send.at[d, s], g_recv.at[d, s], dp=to))]
        for k, i in enumerate(i for i in range(ranks) if head_of(s, i, ranks) < heads):
            part = all_ref.at[group, i, :, slot(s)]
            found.append((group != groups - 1, remote(part, part, e_send.at[d, k], e_recv.at[d, k], dp=to)))
        return found

    def spread_out():
        for d in range(1, ranks):
            i = lax.rem(me + ranks - d, ranks)
            for s in range(slots):
                pl.when(has(s, i, g))(lambda: turn_copy(d, s, i, others[0]).wait_recv())
        for d in range(1, groups):
            for s in range(slots):
                for ok, copy in spread(d, s, g, peers[d - 1]):
                    guarded(ok, copy.start)

    def keep_first():
        dn_sum[...] = first.total()

    first.add_pairs()
    hooks = [None, None, add_groups, None, spread_out, keep_first]

    def step(t, carry):
        now = lax.rem(t, 2)
        pl.when(t + 1 < steps)(lambda: fetch(t + 1, 1 - now))
        r = pl.ds(0, tile)
        for copy in tile_copies([n_all.at[0, r], packed_all.at[0, :, r], ca_all.at[0, r], cb_all.at[0, r]], now):
            copy.wait()
        routed_tile(
            n_buf[now], [c_buf[now]], weight_of(jnp.transpose(p_buf[now].astype(F32)), j, count),
            wg[...], wu[...], wd[...], acc_gate, acc_up, acc_down,
        )
        for k, hook in enumerate(hooks):
            if hook is not None:
                pl.when(t == k * steps // len(hooks))(hook)
        return carry

    lax.fori_loop(0, steps, step, 0)
    stores = []
    for k, (acc, out) in enumerate(((acc_gate, dg_ref), (acc_up, du_ref), (acc_down, dd_ref))):
        half_size = (wg, wu, wd)[k]
        half_size[...] = acc[...].astype(BF)
        stores.append(pltpu.make_async_copy(half_size, out, load.at[k]))
        stores[-1].start()
    first.finish()
    for d in range(1, groups):
        source = lax.rem(g + groups - d, groups)
        for s in range(slots):
            pl.when(has(s, me, peers[d - 1]))(lambda: reduce_copy(d, s, 0).wait_send())
            for ok, copy in spread(d, s, source, peers[d - 1]):
                guarded(ok, copy.wait_recv)
            for ok, copy in spread(d, s, g, peers[d - 1]):
                guarded(ok, copy.wait_send)
    for d in range(1, ranks):
        for s in range(slots):
            pl.when(has(s, me, g))(lambda: turn_copy(d, s, me, others[d - 1]).wait_send())
    for copy in stores:
        copy.wait()


def tail(ranks, groups, heads, slots, j, d_normed, d_weights, others, weights, own_grads):
    half, width = others[0].shape[1:]
    count, _, hidden = weights[0].shape
    chips = ranks // 2
    total = d_normed.shape[0]
    own = total // ranks
    rows = width // ranks
    span = slots * LANES
    tile = min(512, half)
    dma = pltpu.SemaphoreType.DMA
    shape = jax.ShapeDtypeStruct
    vmem, anywhere = pl.BlockSpec(memory_space=pltpu.VMEM), pl.BlockSpec(memory_space=pl.ANY)
    block = shape((chips, own, width), BF)
    near = chips <= 4
    return pl.pallas_call(
        functools.partial(tail_kernel, ranks, groups, heads, slots, j, count),
        out_shape=[
            shape((own, width), F32), shape((groups, ranks, rows, span), BF),
            shape((width, hidden), BF), shape((width, hidden), BF), shape((hidden, width), BF),
        ]
        + [block] * (0 if near else 2),
        in_specs=[anywhere] + [vmem] * 4 + [anywhere] * 10,
        out_specs=[vmem] * 2 + [anywhere] * (3 if near else 5),
        scratch_shapes=[
            pltpu.VMEM((2, tile, width), BF), pltpu.VMEM((2, tile, width), BF), pltpu.VMEM((2, TURNED, tile), BF),
            pltpu.VMEM((width, hidden), BF), pltpu.VMEM((width, hidden), BF), pltpu.VMEM((hidden, width), BF),
            pltpu.VMEM((width, hidden), F32), pltpu.VMEM((width, hidden), F32), pltpu.VMEM((hidden, width), F32),
            pltpu.VMEM((groups - 1, width, span), BF), pltpu.VMEM((ranks, rows, span), BF),
            pltpu.VMEM((chips, own, width), BF),
            dma((chips,)), dma((chips,)), dma((2,)),
            dma((groups, slots)), dma((groups, slots)),
            dma((ranks, slots)), dma((ranks, slots)),
            dma((groups, slots)), dma((groups, slots)),
            dma((groups, ranks)), dma((groups, ranks)),
            dma((6,)), dma((2, 4)),
        ]
        + ([pltpu.VMEM((chips, own, width), BF)] * 2 if near else [pltpu.VMEM((own, width), BF)] * 2),
        compiler_params=pltpu.CompilerParams(
            vmem_limit_bytes=VMEM_LIMIT, collective_id=4, has_side_effects=True
        ),
        cost_estimate=pl.CostEstimate(flops=total * groups * width * hidden * 12, bytes_accessed=2**26, transcendentals=0),
        name="tail",
    )(
        d_normed.reshape(chips, 2, own, width), *d_weights,
        *others, *weights, *own_grads,
    )[:5]


def outputs_kernel(
    heads, slots, j, gain_at, dn_ref, out_ref, resid_ref, dres_ref, x_ref, gain_ref, all_ref, wo_ref, sd_ref,
    eg_ref, eu_ref, ed_ref, bg_ref, bu_ref, bd_ref,
    layer_ref, dx_ref, q_ref, k_ref, v_ref, o_ref, sg_ref, su_ref, dsd_ref, small_ref, dg_ref, du_ref, dd_ref,
    hg, hu, hd, wide_g, wide_u, wide_d, load, store,
):
    loads = [
        pltpu.make_async_copy(src, dst, load.at[k])
        for k, (src, dst) in enumerate(((eg_ref, hg), (eu_ref, hu), (ed_ref, hd)))
    ]
    for copy in loads:
        copy.start()
    copies = []
    for k, (src, wide, dst) in enumerate(((hg, wide_g, dg_ref), (hu, wide_u, du_ref), (hd, wide_d, dd_ref))):
        loads[k].wait()
        wide[...] = src[...].astype(F32)
        copies.append(pltpu.make_async_copy(wide, dst.at[j], store.at[k]))
        copies[-1].start()
    layer_ref[...] = (resid_ref[...] + out_ref[...].astype(F32)).astype(BF)
    x = x_ref[...].astype(F32)
    inverse = lax.rsqrt(jnp.mean(x * x, -1, keepdims=True) + EPS)
    dx_ref[...] = (dres_ref[...] + norm_back(dn_ref[...], x, inverse, gain_ref[gain_at : gain_at + 1, :])).astype(BF)
    ranks = all_ref.shape[1]
    share = sg_ref.shape[1] // ranks
    for which, ref in enumerate((q_ref, k_ref, v_ref)):
        for h in range(heads):
            s, i = next((s, i) for s in range(slots) for i in range(ranks) if head_of(s, i, ranks) == h)
            ref[:, h * LANES : (h + 1) * LANES] = all_ref[which, i, :, s * LANES : (s + 1) * LANES].astype(F32)
    last = all_ref.shape[0] - 1
    small = jnp.zeros(small_ref.shape, F32)
    for i in range(ranks):
        here = all_ref[last, i].astype(F32)
        sg_ref[:, i * share : (i + 1) * share] = here[:, :share]
        su_ref[:, i * share : (i + 1) * share] = here[:, share : 2 * share]
        small += here
    small_ref[...] = small
    o_ref[...] = wo_ref[...].astype(F32)
    dsd_ref[...] = sd_ref[...].astype(F32)
    for copy in copies:
        copy.wait()


def outputs(heads, slots, j, gain_at, share_width, arrays, last_grads, grads):
    dn, out, resid, d_resid, x, gain, everything, d_wo, d_sd = arrays
    rows, span = everything.shape[2:]
    own, width = x.shape
    shape = jax.ShapeDtypeStruct
    vmem, anywhere = pl.BlockSpec(memory_space=pltpu.VMEM), pl.BlockSpec(memory_space=pl.ANY)
    return pl.pallas_call(
        functools.partial(outputs_kernel, heads, slots, j, gain_at),
        out_shape=[shape((own, width), BF)] * 2
        + [shape((rows, width), F32)] * 4
        + [shape((rows, share_width), F32)] * 2
        + [shape(d_sd.shape, F32), shape((rows, span), F32)]
        + [shape(a.shape, F32) for a in grads],
        in_specs=[vmem] * 9 + [anywhere] * 6,
        out_specs=[vmem] * 10 + [anywhere] * 3,
        scratch_shapes=[pltpu.VMEM(a.shape, BF) for a in last_grads]
        + [pltpu.VMEM(a.shape, F32) for a in last_grads]
        + [pltpu.SemaphoreType.DMA((3,)), pltpu.SemaphoreType.DMA((3,))],
        input_output_aliases={12: 10, 13: 11, 14: 12},
        compiler_params=pltpu.CompilerParams(vmem_limit_bytes=VMEM_LIMIT),
        name="outputs",
    )(*arrays, *last_grads, *grads)


def norm_back(grad, values, inverse, gain):
    scaled = grad * gain
    inner = jnp.mean(scaled * values, -1, keepdims=True)
    return inverse * scaled - values * inverse**3 * inner


def body(
    tokens, cotangent, attn_gain, ffn_gain, w_query, w_key, w_value, w_output, router,
    shared_gate, shared_up, shared_down, expert_gate, expert_up, expert_down, expert_ids,
):
    ranks = lax.axis_size("expert")
    me = lax.axis_index("expert")
    seqs, own_pos, width = tokens.shape
    length = own_pos * ranks
    total = seqs * length
    own = seqs * own_pos
    rows = w_query.shape[0]
    heads = width // HEAD_DIM
    slots = -(-heads // ranks)
    span = slots * HEAD_DIM
    share = shared_gate.shape[1] // ranks
    names = router.shape[1]
    count = expert_gate.shape[0]

    groups = lax.axis_size("dp")

    def in_order(a):
        return a.reshape(ranks, seqs, own_pos, -1).transpose(1, 0, 2, 3).reshape(total, -1)

    def by_rank(a):
        return a.reshape(seqs, ranks, own_pos, -1).transpose(1, 0, 2, 3).reshape(total, -1)

    rest = jnp.concatenate([router, attn_gain[:, None], ffn_gain[:, None]], -1)
    edges = [0, share, 2 * share, 2 * share + names, 2 * share + names + 1]
    gain_at = edges[3] - (slots - 1) * LANES
    top = expert_ids.shape[-1]
    cosine, sine = rotary_tables(length)
    (
        group_x, group_c, w_q, w_k, w_v, w_pack, small, half_out, inverse_one, q, k, v, mixed, lse,
    ) = front(
        ranks, groups, heads, seqs, slots, gain_at, tokens.reshape(own, width), cotangent.reshape(own, width),
        expert_ids.reshape(own, top), w_query, w_key, w_value, shared_gate, shared_up, rest, w_output,
        cosine, sine,
    )
    group_c = group_c.reshape(total, -1)
    gain_two = small[gain_at + 1 : gain_at + 2]
    units = width // LANES
    c_last = max(3 * units // 10, 1) * LANES
    c_first = width - c_last
    resid, normed_two, all_mixed, all_out, packed, turned, all_ca = project(
        ranks, groups, heads, slots, count, top, edges[2], c_first, group_x, by_rank(mixed), half_out, small, w_pack, group_c
    )
    layer_part, d_normed_part, d_pack, d_s_down, all_n, all_cb, all_w, *own_grads = experts(
        ranks, c_last, normed_two, group_c, packed, turned, expert_gate, expert_up, expert_down, w_pack, shared_down
    )
    every = ((normed_two, group_c, packed), (all_n, all_ca, all_cb, all_w))
    banks = (expert_gate, expert_up, expert_down)
    hidden = expert_gate.shape[-1]
    cut = hidden * 4 // 7 if hidden % (7 * LANES) == 0 else hidden // 2

    def after(late, *earlier):
        return lax.optimization_barrier((late, earlier))[0]

    def scatter(partial):
        return lax.psum_scatter(partial, "expert", scatter_dimension=0, tiled=True)

    grads = expert_weights(0, 0, cut, every, banks)
    d_normed_two, grads = lax.optimization_barrier((scatter(d_normed_part), grads))
    d_normed_two = d_normed_two.astype(F32)
    inverse_two = lax.rsqrt(jnp.mean(resid * resid, -1, keepdims=True) + EPS)
    ffn_gain_part = jnp.sum(d_normed_two * resid * inverse_two, 0)
    d_out = cotangent.reshape(own, width).astype(F32)
    d_resid = d_out + norm_back(d_normed_two, resid, inverse_two, gain_two)
    own_att = d_resid.astype(BF)
    d_att = lax.all_gather(own_att, "expert", axis=0, tiled=True)
    grads = expert_weights(0, cut, hidden - cut, after(every, own_att), banks, grads)
    d_att, grads = lax.optimization_barrier((d_att, grads))

    d_normed_part, d_wq, d_wk, d_wv, attn_gain_part = attend_back(
        ranks, heads, seqs, slots, gain_at, in_order(d_att), in_order(group_x), inverse_one, small,
        (w_q, w_k, w_v), all_out, cosine, sine, q, k, v, lse
    )
    column = jnp.arange(span)[None, :]
    d_pack = jnp.where(column == edges[3], attn_gain_part.reshape(width, 1), d_pack)
    d_pack = jnp.where(column == edges[4], ffn_gain_part[:, None], d_pack).astype(BF)
    own_mixed = lax.dynamic_slice_in_dim(all_mixed, me * rows, rows, 1)
    d_wo_rows = dot_tn(own_mixed, d_att).astype(BF)
    d_wo_rows, d_sd_rows = lax.psum((d_wo_rows, d_s_down.astype(BF)), "dp")
    dn_sum, all_grads, *last_grads = tail(
        ranks, groups, heads, slots, 1, by_rank(d_normed_part), (d_wq, d_wk, d_wv, d_pack), every[1], banks, own_grads
    )
    layer_output, input_grad, g_q, g_k, g_v, g_o, g_sg, g_su, g_sd, small, g_gate, g_up, g_down = outputs(
        heads, slots, 1, gain_at, ranks * share,
        (dn_sum, scatter(after(layer_part, d_att)), resid, d_resid, tokens.reshape(own, width), small, all_grads, d_wo_rows, d_sd_rows),
        last_grads, grads,
    )
    g_r = small[:, edges[2] : edges[3]]
    g_one = small[:, edges[3]]
    g_two = small[:, edges[4]]
    return (
        layer_output.reshape(tokens.shape), input_grad.reshape(tokens.shape),
        g_one, g_two, g_q, g_k, g_v, g_o, g_r, g_sg, g_su, g_sd, g_gate, g_up, g_down,
    )


def solution(mesh):
    row = P("expert", None)
    experts_spec = P("expert", None, None)
    tokens_spec = P("dp", "expert", None)
    return jax.shard_map(
        body,
        mesh=mesh,
        in_specs=(tokens_spec, tokens_spec, P("expert"), P("expert"))
        + (row,) * 8
        + (experts_spec,) * 3
        + (P(("dp", "expert"), None, None),),
        out_specs=(tokens_spec, tokens_spec, P("expert"), P("expert")) + (row,) * 8 + (experts_spec,) * 3,
        check_vma=False,
    )
```

```python
import functools

import jax
import jax.numpy as jnp
import numpy as np
from jax import lax
from jax.experimental import pallas as pl
from jax.experimental.pallas import tpu as pltpu
from jax.sharding import PartitionSpec as P

HEAD_DIM = 128
LANES = 128
TURNED = 16
EPS = 1e-06
MASKED = -1e30
VMEM_LIMIT = 60 * 2**20
BF = jnp.bfloat16
F32 = jnp.float32


def dot(a, b):
    return jnp.dot(a, b, preferred_element_type=F32)


def dot_nt(a, b):
    return lax.dot_general(a, b, (((1,), (1,)), ((), ())), preferred_element_type=F32)


def dot_tn(a, b):
    return lax.dot_general(a, b, (((0,), (0,)), ((), ())), preferred_element_type=F32)


def silu(v):
    return v / (1.0 + jnp.exp(-v))


def swiglu_back(d_hidden, gates, ups):
    sigma = 1.0 / (1.0 + jnp.exp(-gates))
    d_gate = d_hidden * ups * sigma * (1.0 + gates * (1.0 - sigma))
    d_up = d_hidden * (gates * sigma)
    return d_gate.astype(BF), d_up.astype(BF)


def rotary_tables(length):
    half = HEAD_DIM // 2
    inverse_freq = np.float32(10000.0) ** (-np.arange(half, dtype=np.float32) * np.float32(2.0 / HEAD_DIM))
    angles = np.arange(length, dtype=np.float32)[:, None] * inverse_freq[None, :]
    cosine, sine = np.cos(angles), np.sin(angles)
    tables = np.concatenate([cosine, cosine], -1), np.concatenate([-sine, sine], -1)
    return tuple(jnp.asarray(t.astype(np.float32)) for t in tables)


def vmem_call(kernel, outs, *args, **kwargs):
    spec = pl.BlockSpec(memory_space=pltpu.VMEM)
    return pl.pallas_call(
        kernel,
        out_shape=outs,
        in_specs=[spec] * len(args),
        out_specs=[spec] * len(outs),
        compiler_params=pltpu.CompilerParams(vmem_limit_bytes=VMEM_LIMIT),
        **kwargs,
    )(*args)


def row_block(length):
    return 256 if length % 256 == 0 else length


def remote(src, dst, send, recv, **device):
    return pltpu.make_async_remote_copy(
        src_ref=src, dst_ref=dst, send_sem=send, recv_sem=recv, device_id=device, device_id_type=pl.DeviceIdType.MESH
    )


def meet(peers):
    barrier = pltpu.get_barrier_semaphore()
    for peer in peers:
        pl.semaphore_signal(barrier, inc=1, device_id=peer, device_id_type=pl.DeviceIdType.MESH)
    pl.semaphore_wait(barrier, len(peers))


def meet_near(chips, z, me, peers=()):
    barrier = pltpu.get_barrier_semaphore()
    near = [(True, {"expert": me + 1 - 2 * lax.rem(me, 2)}), (z > 0, {"expert": me - 2}), (z < chips - 1, {"expert": me + 2})]
    near += [(True, {"dp": t}) for t in peers]

    def signal(t):
        pl.semaphore_signal(barrier, inc=1, device_id=t, device_id_type=pl.DeviceIdType.MESH)

    for ok, t in near:
        guarded(ok, functools.partial(signal, t))
    ends = jnp.where(z > 0, 1, 0) + jnp.where(z < chips - 1, 1, 0)
    pl.semaphore_wait(barrier, 1 + len(peers) + ends)


def both(*conditions):
    held = [c for c in conditions if c is not True]
    if not held:
        return True
    out = held[0]
    for c in held[1:]:
        out = jnp.logical_and(out, c)
    return out


def guarded(condition, action):
    if condition is True:
        action()
    else:
        pl.when(condition)(action)


class LineGather:
    def __init__(self, ranks, own, block, send, recv, base=0, valid=lambda i: True, twins=True):
        self.me = lax.axis_index("expert")
        self.chips = ranks // 2
        self.z = self.me // 2
        self.twin = self.me + 1 - 2 * lax.rem(self.me, 2)
        self.own, self.block, self.send, self.recv, self.base, self.valid = own, block, send, recv, base, valid
        self.twins = twins

    @staticmethod
    def semaphores(ranks):
        return 4 * (ranks // 2 - 1) + 1

    def copy(self, src, i, k, to):
        return remote(src, self.block(i), self.send.at[self.base + k], self.recv.at[self.base + k], expert=to)

    def sources(self, s):
        hops = self.chips - 1
        return (
            (self.me - 2 * s, self.z - s >= 0, self.z < hops, self.me + 2, 0, 2 * hops, -2 * s),
            (self.me + 2 * s, self.z + s <= hops, self.z > 0, self.me - 2, hops, 3 * hops, 2 * s),
        )

    def start(self):
        hops = self.chips - 1
        mine = self.valid(self.me)
        if hops:
            guarded(both(self.z < hops, mine), lambda: self.copy(self.own, self.me, 0, self.me + 2).start())
            guarded(both(self.z > 0, mine), lambda: self.copy(self.own, self.me, hops, self.me - 2).start())
        if self.twins:
            guarded(mine, lambda: self.copy(self.own, self.me, 2 * hops, self.twin).start())

    def step(self, s):
        for i, there, more, to, k, pair, _ in self.sources(s):
            known = both(there, self.valid(i))
            src = self.block(i)
            guarded(known, lambda: self.copy(src, i, k + s - 1, self.twin).wait_recv())
            if s < self.chips - 1:
                guarded(both(known, more), lambda: self.copy(src, i, k + s, to).start())
            if self.twins:
                guarded(known, lambda: self.copy(src, i, pair + s, self.twin).start())

    def finish(self):
        hops = self.chips - 1
        mine = self.valid(self.me)
        theirs = self.valid(self.twin)
        if self.twins:
            guarded(mine, lambda: self.copy(self.own, self.me, 2 * hops, self.twin).wait_send())
            guarded(theirs, lambda: self.copy(self.own, self.twin, 2 * hops, self.twin).wait_recv())
        if hops:
            guarded(both(self.z < hops, mine), lambda: self.copy(self.own, self.me, 0, self.twin).wait_send())
            guarded(both(self.z > 0, mine), lambda: self.copy(self.own, self.me, hops, self.twin).wait_send())
        for s in range(1, self.chips):
            for i, there, more, to, k, pair, shift in self.sources(s):
                known = both(there, self.valid(i))
                src = self.block(i)
                if s < hops:
                    guarded(both(known, more), lambda: self.copy(src, i, k + s, self.twin).wait_send())
                if not self.twins:
                    continue
                guarded(known, lambda: self.copy(src, i, pair + s, self.twin).wait_send())
                j = self.twin + shift
                got = both(there, self.valid(j))
                guarded(got, lambda: self.copy(self.block(j), j, pair + s, self.twin).wait_recv())


class Across:
    SEMAPHORES = 12

    def __init__(self, source, dst, send, recv):
        self.me, self.g = lax.axis_index("expert"), lax.axis_index("dp")
        self.twin = self.me + 1 - 2 * lax.rem(self.me, 2)
        self.by_x = self.g + 1 - 2 * lax.rem(self.g, 2)
        self.by_y = lax.rem(self.g + 2, 4)
        self.source, self.dst, self.send, self.recv = source, dst, send, recv
        self.half = dst.shape[1]
        self.part = self.half // 2

    def peers(self):
        return [{"dp": self.by_x}, {"dp": self.by_y}, {"expert": self.twin}]

    def piece(self, slot, j):
        return self.dst.at[slot, pl.ds(j * self.part, self.part)]

    def mine(self, j):
        first = lax.rem(self.me, 2) * self.half + j * self.part
        return self.source(pl.ds(pl.multiple_of(first, self.part), self.part))

    def copy(self, k, src, dst, **to):
        return remote(src, dst, self.send.at[k], self.recv.at[k], **to)

    def direct(self, k):
        slot, j, to = ((0, 0, self.by_x), (1, 1, self.by_y), (0, 1, self.by_x), (1, 0, self.by_y))[k]
        return self.copy(k, self.mine(j), self.piece(slot, j), dp=to)

    def relayed(self, j):
        if j == 0:
            return self.copy(4, self.piece(0, 0), self.piece(2, 0), dp=self.by_y)
        return self.copy(5, self.piece(1, 1), self.piece(2, 1), dp=self.by_x)

    def shared(self, slot, j):
        return self.copy(6 + 2 * slot + j, self.piece(slot, j), self.piece(slot + 3, j), expert=self.twin)

    def start(self):
        for k in range(2):
            self.direct(k).start()

    def more(self):
        for k in range(2, 4):
            self.direct(k).start()

    def relay(self):
        self.direct(0).wait_recv()
        self.relayed(0).start()
        self.direct(1).wait_recv()
        self.relayed(1).start()
        self.shared(0, 0).start()
        self.shared(1, 1).start()

    def hand_over(self):
        self.direct(2).wait_recv()
        self.shared(0, 1).start()
        self.direct(3).wait_recv()
        self.shared(1, 0).start()

    def finish(self):
        for j in range(2):
            self.relayed(j).wait_recv()
            self.shared(2, j).start()
        for k in range(4):
            self.direct(k).wait_send()
        for j in range(2):
            self.relayed(j).wait_send()
            for slot in range(3):
                self.shared(slot, j).wait()


class SameExperts:
    SEMAPHORES = 6

    def __init__(self, source, dst, send, recv):
        self.me, self.g = lax.axis_index("expert"), lax.axis_index("dp")
        self.near = [self.g + 1 - 2 * lax.rem(self.g, 2), lax.rem(self.g + 2, 4)]
        self.near.append(self.near[1] + 1 - 2 * lax.rem(self.near[1], 2))
        self.source, self.dst, self.send, self.recv = source, dst, send, recv
        self.half = dst.shape[2]

    def peers(self):
        return [{"dp": self.near[2]}]

    def copy(self, k, h):
        slot = k + 3 * lax.rem(lax.rem(self.me, 2) + h, 2)
        i = 2 * k + h
        src = self.source.at[:, pl.ds(h * self.half, self.half)]
        return remote(src, self.dst.at[slot], self.send.at[i], self.recv.at[i], dp=self.near[k])

    def start(self):
        for k in range(3):
            for h in range(2):
                self.copy(k, h).start()

    def relay(self):
        pass

    hand_over = more = relay

    def finish(self):
        for k in range(3):
            for h in range(2):
                self.copy(k, h).wait()


def head_of(s, i, ranks):
    return i if s == 0 else s * ranks + i // 2 + (i % 2) * (ranks // 2)


def aligned(i, size):
    return pl.ds(pl.multiple_of(i * size, size), size)


def front_kernel(
    ranks, groups, heads, seqs, slots, gain_at,
    x_ref, c_ref, id_ref, wq_ref, wk_ref, wv_ref, sg_ref, su_ref, rest_ref, wo_ref, cos_ref, sin_ref,
    gx_ref, gc_ref, wqs_ref, wks_ref, wvs_ref, wps_ref, small_ref, half_ref,
    inv_ref, q_ref, k_ref, v_ref, mixed_ref, lse_ref, stage_ref, land_ref, ostage_ref,
    x_send, x_recv, c_send, c_recv, w_send, w_recv, d_send, d_recv, o_send, o_recv, p_send, p_recv,
):
    me, g = lax.axis_index("expert"), lax.axis_index("dp")
    rows, width = wq_ref.shape
    units = width // LANES
    per = ostage_ref.shape[0]
    peers = [lax.rem(g + d, groups) for d in range(1, groups)]
    others = [lax.rem(me + d, ranks) for d in range(1, ranks)]
    meet([{"expert": t} for t in others] + [{"dp": t} for t in peers])

    def stage_heads(w):
        for u in range(heads):
            stage_ref[u] = w[:, u * LANES : (u + 1) * LANES]

    for which, w in enumerate((wq_ref, wk_ref, wv_ref)):
        pl.when(g == which)(functools.partial(stage_heads, w))

    def stage_pack():
        share = sg_ref.shape[1] // ranks
        spare = slots * LANES - 2 * share - rest_ref.shape[1]
        for t in range(ranks):
            cols = slice(t * share, (t + 1) * share)
            pieces = [sg_ref[:, cols], su_ref[:, cols], rest_ref[...]]
            if spare:
                pieces.append(jnp.zeros((rows, spare), BF))
            packed = jnp.concatenate(pieces, -1)
            for s in range(slots):
                stage_ref[head_of(s, t, ranks)] = packed[:, s * LANES : (s + 1) * LANES]

    pl.when(g == groups - 1)(stage_pack)

    def known(s, t, group=None):
        return jnp.logical_or((g if group is None else group) == groups - 1, head_of(s, t, ranks) < heads)

    def weight_copy(s, d, unit, i, to):
        return remote(
            stage_ref.at[unit], land_ref.at[g, s, i], w_send.at[s, d], w_recv.at[s, d], expert=to
        )

    for d in range(1, ranks):
        t = others[d - 1]
        for s in range(slots):
            guarded(known(s, t), lambda: weight_copy(s, d, head_of(s, t, ranks), me, t).start())

    def stage_out(which):
        for k in range(per):
            u = which * per + k
            if u < units:
                ostage_ref[k] = wo_ref[:, u * LANES : (u + 1) * LANES]

    for which in range(groups):
        pl.when(g == which)(functools.partial(stage_out, which))
    out_rows = LineGather(
        ranks, ostage_ref, lambda i: half_ref.at[g, :, i // 2], o_send, o_recv, twins=False
    )
    out_rows.start()
    tokens = LineGather(ranks, x_ref, lambda i: gx_ref.at[i], x_send, x_recv)
    tokens.start()
    half_ref[g, :, me // 2] = ostage_ref[...]
    for s in range(slots):
        def keep(s=s):
            land_ref[g, s, me] = stage_ref[head_of(s, me, ranks)]

        pl.when(known(s, me))(keep)
        for which in range(groups - 1):
            def clear(s=s, which=which):
                land_ref[which, s] = jnp.zeros(land_ref.shape[2:], BF)

            pl.when(head_of(s, me, ranks) >= heads)(clear)
    gx_ref[me] = x_ref[...]
    gc_ref[me, :, :width] = c_ref[...]
    routes = id_ref[...].astype(F32).astype(BF)
    blank = jnp.zeros((routes.shape[0], LANES - routes.shape[1]), BF)
    gc_ref[me, :, width:] = jnp.concatenate([routes, blank], -1)

    def share(s, part, d, to):
        return remote(part, part, d_send.at[s, d], d_recv.at[s, d], dp=to)

    def pass_on(i):
        for s in range(slots):
            part = land_ref.at[g, s, i]
            for d in range(1, groups):
                pl.when(known(s, me))(lambda: share(s, part, d, peers[d - 1]).start())

    def out_share(d, k, group):
        part = half_ref.at[group, k]
        return remote(part, part, p_send.at[d, k], p_recv.at[d, k], dp=peers[d - 1])

    def held(group, k):
        return True if (groups - 1) * per + k < units else group * per + k < units

    pass_on(me)
    for d in range(1, ranks):
        i = lax.rem(me + ranks - d, ranks)
        for s in range(slots):
            pl.when(known(s, me))(lambda: weight_copy(s, d, 0, i, others[0]).wait_recv())
        pass_on(i)
    steps = ranks // 2 - 1
    for step in range(1, steps + 1):
        out_rows.step(step)
        if step == 1:
            tokens.step(1)
    out_rows.finish()
    for d in range(1, groups):
        for k in range(per):
            guarded(held(g, k), out_share(d, k, g).start)
    cots = LineGather(ranks, gc_ref.at[me], lambda i: gc_ref.at[i], c_send, c_recv)
    for step in range(2, steps + 1):
        tokens.step(step)
        if step == steps - 1:
            cots.start()
    if steps < 3:
        cots.start()
    tokens.finish()
    for d in range(1, groups):
        there = lax.rem(g + groups - d, groups)
        for s in range(slots):
            pl.when(known(s, me, there))(lambda: share(s, land_ref.at[there, s], d, peers[d - 1]).wait_recv())
    for which, ref in enumerate((wqs_ref, wks_ref, wvs_ref, wps_ref)):
        for s in range(slots):
            for r in range(ranks):
                ref[r * rows : (r + 1) * rows, s * LANES : (s + 1) * LANES] = land_ref[which, s, r]
    small_ref[...] = jnp.transpose(wps_ref[:, (slots - 1) * LANES :].astype(F32))
    attend(
        seqs, slots, gain_at, gx_ref, small_ref, wqs_ref, wks_ref, wvs_ref, cos_ref, sin_ref,
        inv_ref, q_ref, k_ref, v_ref, mixed_ref, lse_ref,
        [functools.partial(cots.step, step) for step in range(1, steps + 1)],
    )
    cots.finish()
    for d in range(1, ranks):
        t = others[d - 1]
        for s in range(slots):
            pl.when(known(s, t))(lambda: weight_copy(s, d, 0, me, t).wait_send())
    for d in range(1, groups):
        there = lax.rem(g + groups - d, groups)
        for s in range(slots):
            pl.when(known(s, me))(lambda: share(s, land_ref.at[g, s], d, peers[d - 1]).wait_send())
        for k in range(per):
            guarded(held(g, k), out_share(d, k, g).wait_send)
            guarded(held(there, k), out_share(d, k, there).wait_recv)


def front(
    ranks, groups, heads, seqs, slots, gain_at, x, cot, ids, w_query, w_key, w_value, s_gate, s_up, rest, w_output,
    cosine, sine,
):
    own, width = x.shape
    total, span = ranks * own, slots * LANES
    rows = w_query.shape[0]
    per = -(-(width // LANES) // groups)
    line = LineGather.semaphores(ranks)
    dma = pltpu.SemaphoreType.DMA
    spec = pl.BlockSpec(memory_space=pltpu.VMEM)
    shape = jax.ShapeDtypeStruct
    return pl.pallas_call(
        functools.partial(front_kernel, ranks, groups, heads, seqs, slots, gain_at),
        out_shape=[shape((ranks, own, width), BF), shape((ranks, own, width + LANES), BF)]
        + [shape((width, slots * LANES), BF)] * 4
        + [shape((LANES, width), F32), shape((groups, per, ranks // 2, rows, LANES), BF)]
        + [shape((total, 1), F32)]
        + [shape((total, span), BF)] * 4
        + [shape((total, slots), F32)],
        in_specs=[spec] * 12,
        out_specs=[spec] * 14,
        scratch_shapes=[
            pltpu.VMEM((slots * ranks, rows, LANES), BF),
            pltpu.VMEM((groups, slots, ranks, rows, LANES), BF),
            pltpu.VMEM((per, rows, LANES), BF),
            dma((line,)), dma((line,)),
            dma((line,)), dma((line,)),
            dma((slots, ranks)), dma((slots, ranks)),
            dma((slots, groups)), dma((slots, groups)),
            dma((line,)), dma((line,)),
            dma((groups, per)), dma((groups, per)),
        ],
        compiler_params=pltpu.CompilerParams(
            collective_id=0, has_side_effects=True, vmem_limit_bytes=VMEM_LIMIT
        ),
        name="front",
    )(x, cot, ids, w_query, w_key, w_value, s_gate, s_up, rest, w_output, cosine, sine)


def project_kernel(
    ranks, groups, heads, slots, count, top, route_at,
    x_ref, mixed_ref, half_ref, small_ref, pack_ref, c_ref,
    resid_ref, n_ref, all_ref, wo_ref, packed_ref, turned_ref, c_all_ref, other_ref, id_ref,
    send, recv, t_send, t_recv, a_send, a_recv, load,
):
    me, g = lax.axis_index("expert"), lax.axis_index("dp")
    chips = ranks // 2
    z = me // 2
    twin = me + 1 - 2 * lax.rem(me, 2)
    per, part = half_ref.shape[1], half_ref.shape[3]
    units = wo_ref.shape[1] // LANES
    peers = [lax.rem(g + d, groups) for d in range(1, groups)]
    lanes = c_all_ref.shape[-1]
    across = Across(lambda r: c_ref.at[r, pl.ds(0, lanes)], c_all_ref, a_send, a_recv)
    meet_near(chips, z, me, peers)
    ids = pltpu.make_async_copy(c_ref.at[:, pl.ds(wo_ref.shape[1], LANES)], id_ref, load)
    ids.start()
    line = LineGather.semaphores(ranks)
    parts = []
    for s in range(slots):
        def head(i, s=s):
            return aligned(jnp.clip(head_of(s, i, ranks), 0, heads - 1), LANES)

        cols = slice(s * LANES, (s + 1) * LANES)
        ok = (lambda i: True) if (s + 1) * ranks <= heads else (lambda i, s=s: head_of(s, i, ranks) < heads)
        gather = LineGather(
            ranks, mixed_ref.at[:, cols], lambda i, head=head: all_ref.at[:, head(i)], send, recv, s * line, ok
        )
        gather.start()
        parts.append(gather)

    across.start()
    across.more()
    for s, gather in enumerate(parts):
        def keep(s=s):
            cols = slice(s * LANES, (s + 1) * LANES)
            all_ref[:, aligned(jnp.clip(head_of(s, me, ranks), 0, heads - 1), LANES)] = mixed_ref[:, cols]

        guarded(gather.valid(me), keep)

    def share_twin(group, k):
        src = half_ref.at[group, k]
        return remote(src, other_ref.at[group, k], t_send.at[group, k], t_recv.at[group, k], expert=twin)

    def each_unit(action):
        for group in range(groups):
            for k in range(per):
                if group * per + k < units:
                    action(share_twin(group, k))

    each_unit(lambda copy: copy.start())
    middle = (chips + 1) // 2
    for step in range(1, chips):
        for gather in parts:
            gather.step(step)
        if step == middle:
            across.relay()
    for gather in parts:
        gather.finish()
    each_unit(lambda copy: copy.wait())
    ids.wait()

    def lay_out(even, odd):
        for u in range(units):
            cols = slice(u * LANES, (u + 1) * LANES)
            for c in range(chips):
                wo_ref[2 * c * part : (2 * c + 1) * part, cols] = even[u // per, u % per, c]
                wo_ref[(2 * c + 1) * part : (2 * c + 2) * part, cols] = odd[u // per, u % per, c]

    pl.when(me == 2 * z)(lambda: lay_out(half_ref, other_ref))
    pl.when(me != 2 * z)(lambda: lay_out(other_ref, half_ref))
    blocks, own, width = x_ref.shape
    names = ranks * count
    gain_at = route_at + names + 1 - (slots - 1) * LANES
    gain = small_ref[gain_at : gain_at + 1, :]
    tile = 2 if own <= 128 and blocks % 2 == 0 else 1

    def rows_of(b):
        rows = aligned(b, tile * own)
        x = x_ref[pl.ds(b * tile, tile)].reshape(tile * own, width).astype(F32)
        resid = x + dot(all_ref[rows, :], wo_ref[...])
        inverse = lax.rsqrt(jnp.mean(resid * resid, -1, keepdims=True) + EPS)
        normed = (resid * inverse * gain).astype(BF)
        n_ref[rows, :] = normed
        for t in range(tile):
            def keep(t=t):
                resid_ref[...] = resid[t * own : (t + 1) * own]

            pl.when(b * tile + t == me)(keep)
        probs = route_probs(dot(normed, pack_ref[...]), route_at, names)
        routes = id_ref[rows, :].astype(jnp.int32)
        lane = lax.broadcasted_iota(jnp.int32, routes.shape, 1)
        out = jnp.zeros((tile * own, LANES), F32)
        for j in range(count):
            mine = me * count + j
            chosen = jnp.max(jnp.where((routes == mine) & (lane < top), 1.0, 0.0), -1, keepdims=True)
            names_at = lax.broadcasted_iota(jnp.int32, probs.shape, 1)
            weight = chosen * jnp.sum(jnp.where(names_at == mine, probs, 0.0), -1, keepdims=True)
            high = weight.astype(BF).astype(F32)
            out = jnp.where(lane == j, high, out)
            out = jnp.where(lane == count + j, weight - high, out)
        packed_ref[rows, :] = out.astype(BF)
        turned_ref[:, rows] = jnp.transpose(out)[:turned_ref.shape[0]].astype(BF)

    half = blocks // tile // 2
    lax.fori_loop(0, half, lambda b, c: (rows_of(b), c)[1], 0)
    across.hand_over()
    lax.fori_loop(half, blocks // tile, lambda b, c: (rows_of(b), c)[1], 0)
    across.finish()


def route_probs(products, first, names):
    logits = products[:, first : first + names]
    raised = jnp.exp(logits - jnp.max(logits, -1, keepdims=True))
    return raised / jnp.sum(raised, -1, keepdims=True)


def project(ranks, groups, heads, slots, count, top, route_at, lanes, x, mixed, half, small, pack, cot):
    blocks, own, width = x.shape
    total = blocks * own
    line = LineGather.semaphores(ranks)
    per = half.shape[1]
    dma = pltpu.SemaphoreType.DMA
    spec = pl.BlockSpec(memory_space=pltpu.VMEM)
    anywhere = pl.BlockSpec(memory_space=pl.ANY)
    shape = jax.ShapeDtypeStruct
    return pl.pallas_call(
        functools.partial(project_kernel, ranks, groups, heads, slots, count, top, route_at),
        out_shape=[
            shape((own, width), F32),
            shape((total, width), BF),
            shape((total, width), BF),
            shape((width, width), BF),
            shape((total, LANES), BF),
            shape((TURNED, total), BF),
            shape((6, total // 2, lanes), BF),
        ],
        in_specs=[spec] * 5 + [anywhere],
        out_specs=[spec] * 6 + [anywhere],
        scratch_shapes=[
            pltpu.VMEM(half.shape, BF), pltpu.VMEM((total, LANES), BF),
            dma((slots * line,)), dma((slots * line,)),
            dma((groups, per)), dma((groups, per)),
            dma((Across.SEMAPHORES,)), dma((Across.SEMAPHORES,)), dma(()),
        ],
        compiler_params=pltpu.CompilerParams(
            collective_id=1, has_side_effects=True, vmem_limit_bytes=VMEM_LIMIT
        ),
        name="project",
    )(x, mixed, half, small, pack, cot)


def attend(
    seqs, slots, gain_at, x_ref, small_ref, wq_ref, wk_ref, wv_ref, cos_ref, sin_ref,
    inv_ref, q_ref, k_ref, v_ref, mixed_ref, lse_ref, hooks,
):
    ranks, own, width = x_ref.shape
    pos = own // seqs
    length = ranks * pos
    block = row_block(length)
    count = block // pos
    scale = HEAD_DIM ** (-0.5)
    gain = small_ref[gain_at : gain_at + 1, :]
    hooks = list(hooks)

    def progress():
        if hooks:
            hooks.pop(0)()

    for s in range(seqs):
        for i in range(length // block):
            rows = pl.ds(s * length + i * block, block)
            x = [x_ref[e, s * pos : (s + 1) * pos, :] for e in range(i * count, (i + 1) * count)]
            x = jnp.concatenate(x, 0).astype(F32)
            inv = lax.rsqrt(jnp.mean(x * x, -1, keepdims=True) + EPS)
            normed = (x * inv * gain).astype(BF)
            inv_ref[rows, :] = inv
            cosine = cos_ref[pl.ds(i * block, block), :]
            sine = sin_ref[pl.ds(i * block, block), :]
            queries, keyed, valued = dot(normed, wq_ref[...]), dot(normed, wk_ref[...]), dot(normed, wv_ref[...])
            for h in range(slots):
                cols = slice(h * HEAD_DIM, (h + 1) * HEAD_DIM)
                q, k = queries[:, cols], keyed[:, cols]
                q_ref[rows, cols] = (q * cosine + pltpu.roll(q, HEAD_DIM // 2, 1) * sine).astype(BF)
                k_ref[rows, cols] = (k * cosine + pltpu.roll(k, HEAD_DIM // 2, 1) * sine).astype(BF)
            v_ref[rows, :] = valued.astype(BF)
    progress()
    for s in range(seqs):
        for i in range(length // block):
            if i:
                progress()
            rows = pl.ds(s * length + i * block, block)
            keys = pl.ds(s * length, (i + 1) * block)
            shape = (block, (i + 1) * block)
            seen = (
                lax.broadcasted_iota(jnp.int32, shape, 1)
                <= lax.broadcasted_iota(jnp.int32, shape, 0) + i * block
            )
            for h in range(slots):
                cols = slice(h * HEAD_DIM, (h + 1) * HEAD_DIM)
                scores = dot_nt(q_ref[rows, cols], k_ref[keys, cols]) * scale
                scores = jnp.where(seen, scores, MASKED)
                top = jnp.max(scores, -1, keepdims=True)
                raised = jnp.exp(scores - top)
                totals = jnp.sum(raised, -1, keepdims=True)
                probs = (raised / totals).astype(BF)
                mixed_ref[rows, cols] = dot(probs, v_ref[keys, cols]).astype(BF)
                lse_ref[rows, h : h + 1] = top + jnp.log(totals)
    while hooks:
        progress()


def attend_back_kernel(
    ranks, heads, seqs, slots, gain_at, da_ref, x_ref, inv_ref, small_ref, wq_ref, wk_ref, wv_ref, wall_ref,
    cos_ref, sin_ref,
    q_ref, k_ref, v_ref, lse_ref,
    dn_ref, dwq_ref, dwk_ref, dwv_ref, gain_ref, dmix_ref, dqkv_ref, dk_ref, dv_ref, wo_ref,
):
    total, width = da_ref.shape
    length = total // seqs
    block = row_block(length)
    count = length // block
    scale = HEAD_DIM ** (-0.5)
    span = slots * HEAD_DIM
    me = lax.axis_index("expert")
    for h in range(slots):
        cols = slice(h * HEAD_DIM, (h + 1) * HEAD_DIM)
        head = head_of(h, me, ranks)
        rows_here = wall_ref[aligned(jnp.minimum(head, heads - 1), HEAD_DIM), :]
        wo_ref[cols, :] = jnp.where(head < heads, rows_here, jnp.zeros_like(rows_here))
    for s in range(seqs):
        for i in range(count):
            rows = pl.ds(s * length + i * block, block)
            dmix_ref[rows, :] = dot_nt(da_ref[rows, :], wo_ref[...]).astype(BF)
        for h in range(slots):
            cols = slice(h * HEAD_DIM, (h + 1) * HEAD_DIM)
            dk_ref[...] = jnp.zeros_like(dk_ref)
            dv_ref[...] = jnp.zeros_like(dv_ref)
            for i in range(count):
                rows = pl.ds(s * length + i * block, block)
                reach = (i + 1) * block
                keys = pl.ds(s * length, reach)
                shape = (block, reach)
                seen = (
                    lax.broadcasted_iota(jnp.int32, shape, 1)
                    <= lax.broadcasted_iota(jnp.int32, shape, 0) + i * block
                )
                q = q_ref[rows, cols]
                k = k_ref[keys, cols]
                dmix = dmix_ref[rows, cols]
                scores = jnp.where(seen, dot_nt(q, k) * scale, MASKED)
                probs = jnp.exp(scores - lse_ref[rows, h : h + 1])
                dp = dot_nt(dmix, v_ref[keys, cols])
                delta = jnp.sum(probs * dp, -1, keepdims=True)
                ds = (probs * (dp - delta)).astype(BF)
                dq = dot(ds, k) * scale
                cosine = cos_ref[pl.ds(i * block, block), :]
                sine = sin_ref[pl.ds(i * block, block), :]
                dqkv_ref[rows, h * HEAD_DIM : (h + 1) * HEAD_DIM] = (
                    dq * cosine - pltpu.roll(dq, HEAD_DIM // 2, 1) * sine
                ).astype(BF)
                dk_ref[pl.ds(0, reach), :] += dot_tn(ds, q)
                dv_ref[pl.ds(0, reach), :] += dot_tn(probs.astype(BF), dmix)
            for i in range(count):
                rows = pl.ds(s * length + i * block, block)
                here = pl.ds(i * block, block)
                dk = dk_ref[here, :] * scale
                dk = dk * cos_ref[here, :] - pltpu.roll(dk, HEAD_DIM // 2, 1) * sin_ref[here, :]
                dqkv_ref[rows, span + h * HEAD_DIM : span + (h + 1) * HEAD_DIM] = dk.astype(BF)
                dqkv_ref[rows, 2 * span + h * HEAD_DIM : 2 * span + (h + 1) * HEAD_DIM] = dv_ref[here, :].astype(BF)
    gain = jnp.zeros((1, width), F32)
    for i in range(total // block):
        rows = pl.ds(i * block, block)
        d_normed = dot_nt(dqkv_ref[rows, :span], wq_ref[...])
        d_normed += dot_nt(dqkv_ref[rows, span : 2 * span], wk_ref[...])
        d_normed += dot_nt(dqkv_ref[rows, 2 * span :], wv_ref[...])
        dn_ref[rows, :] = d_normed.astype(BF)
        gain += jnp.sum(d_normed * x_ref[rows, :].astype(F32) * inv_ref[rows, :], 0, keepdims=True)
    gain_ref[...] = gain
    step = LANES * 2
    for i in range(width // step):
        cols = slice(i * step, (i + 1) * step)
        normed = (x_ref[:, cols].astype(F32) * inv_ref[...] * small_ref[gain_at : gain_at + 1, cols]).astype(BF)
        grads = dot_tn(normed, dqkv_ref[...]).astype(BF)
        dwq_ref[cols, :] = grads[:, :span]
        dwk_ref[cols, :] = grads[:, span : 2 * span]
        dwv_ref[cols, :] = grads[:, 2 * span :]


def attend_back(ranks, heads, seqs, slots, gain_at, d_att, x, inverse, small, w_slices, w_all, cosine, sine, q, k, v, lse):
    total, width = d_att.shape
    span = slots * HEAD_DIM
    shape = jax.ShapeDtypeStruct
    return vmem_call(
        functools.partial(attend_back_kernel, ranks, heads, seqs, slots, gain_at),
        [shape((total, width), BF)] + [shape((width, span), BF)] * 3 + [shape((1, width), F32)],
        d_att, x, inverse, small, *w_slices, w_all, cosine, sine, q, k, v, lse,
        scratch_shapes=[
            pltpu.VMEM((total, span), BF),
            pltpu.VMEM((total, 3 * span), BF),
            pltpu.VMEM((total // seqs, HEAD_DIM), F32),
            pltpu.VMEM((total // seqs, HEAD_DIM), F32),
            pltpu.VMEM((span, width), BF),
        ],
        name="attend_back",
    )


def experts_kernel(
    ranks, count, steps, share, n_ref, c_ref, packed_ref, wg_ref, wu_ref, wd_ref, pack_ref, sd_ref,
    n_group, c_group, w_group,
    out_ref, dx_ref, dpack_ref, dsd_ref, n_all, c_all, w_all, og_ref, ou_ref, od_ref, send, recv,
):
    step = pl.program_id(0)
    me = lax.axis_index("expert")
    names = ranks * count
    part = c_all.shape[-1]
    moves = [
        SameExperts(w_group, w_all, send.at[1], recv.at[1]),
        Across(lambda r: n_group.at[r], n_all, send.at[0], recv.at[0]),
        Across(lambda r: c_group.at[r, pl.ds(n_ref.shape[1] - part, part)], c_all, send.at[2], recv.at[2]),
    ]

    @pl.when(step == 0)
    def _():
        meet(moves[0].peers() + moves[1].peers())
        for move in moves:
            move.start()

    @pl.when(step == min(1, steps - 1))
    def _():
        for move in moves:
            move.more()

    @pl.when(step == steps // 2)
    def _():
        for move in moves:
            move.relay()

    @pl.when(step == steps - 1)
    def _():
        for move in moves:
            move.hand_over()

    n = n_ref[...]
    c_b = c_ref[...]
    c = c_b.astype(F32)
    products = dot(n, pack_ref[...])
    gate, up = products[:, :share], products[:, share : 2 * share]
    hidden = (silu(gate) * up).astype(BF)
    out = dot(hidden, sd_ref[...])
    d_gate_s, d_up_s = swiglu_back(dot_nt(c_b, sd_ref[...]), gate, up)

    @pl.when(step == 0)
    def _():
        for ref in (dpack_ref, dsd_ref, og_ref, ou_ref, od_ref):
            ref[...] = jnp.zeros_like(ref)

    dsd_ref[...] += dot_tn(hidden, c_b)
    probs = route_probs(products, 2 * share, names)
    name = lax.broadcasted_iota(jnp.int32, probs.shape, 1)
    d_log = jnp.zeros_like(probs)
    inner = jnp.zeros((n.shape[0], 1), F32)
    dx = jnp.zeros(c.shape, F32)
    for j in range(count):
        weight = packed_ref[:, j : j + 1].astype(F32) + packed_ref[:, count + j : count + j + 1].astype(F32)
        gate = dot(n, wg_ref[j])
        up = dot(n, wu_ref[j])
        hidden = (silu(gate) * up).astype(BF)
        y = dot(hidden, wd_ref[j]).astype(BF).astype(F32)
        out += weight * y
        d_weight = weight * jnp.sum(c * y, -1, keepdims=True)
        d_log += jnp.where(name == me * count + j, d_weight, 0.0)
        inner += d_weight
        d_y = (weight * c).astype(BF)
        d_gate, d_up = swiglu_back(dot_nt(d_y, wd_ref[j]), gate, up)
        dx += dot_nt(d_gate, wg_ref[j]) + dot_nt(d_up, wu_ref[j])
        if j == count - 1:
            og_ref[...] += dot_tn(n, d_gate)
            ou_ref[...] += dot_tn(n, d_up)
            od_ref[...] += dot_tn(hidden, d_y)
    d_log = (d_log - probs * inner).astype(BF)
    rest = jnp.zeros((n.shape[0], pack_ref.shape[1] - 2 * share - names), BF)
    d_products = jnp.concatenate([d_gate_s, d_up_s, d_log, rest], -1)
    dx += dot_nt(d_products, pack_ref[...])
    dpack_ref[...] += dot_tn(n, d_products)
    out_ref[...] = out.astype(BF)
    dx_ref[...] = dx.astype(BF)

    @pl.when(step == steps - 1)
    def _():
        for move in moves:
            move.finish()


def experts(ranks, lanes, normed, cot, packed, turned, w_gate, w_up, w_down, pack, s_down):
    total, width = normed.shape
    count, _, hidden = w_gate.shape
    tile = 256 if total % 256 == 0 else total
    steps = total // tile
    share = s_down.shape[0]
    anywhere = pl.BlockSpec(memory_space=pl.ANY)
    dma = pltpu.SemaphoreType.DMA

    def rows(cols):
        return pl.BlockSpec((tile, cols), lambda i: (i, 0))

    def whole(a):
        zeros = (0,) * a.ndim
        return pl.BlockSpec(a.shape, lambda i: zeros, pipeline_mode=pl.Buffered(1))

    shape = jax.ShapeDtypeStruct
    fixed = (w_gate, w_up, w_down, pack, s_down)
    flops = total * width * hidden * count * 12
    return pl.pallas_call(
        functools.partial(experts_kernel, ranks, count, steps, share),
        grid=(steps,),
        in_specs=[rows(width), rows(width), rows(LANES)] + [whole(a) for a in fixed] + [anywhere] * 3,
        out_specs=[
            rows(width),
            rows(width),
            pl.BlockSpec(pack.shape, lambda i: (0, 0)),
            pl.BlockSpec((share, width), lambda i: (0, 0)),
            anywhere, anywhere, anywhere,
            *(pl.BlockSpec(a.shape[1:], lambda i: (0, 0), pipeline_mode=pl.Buffered(1)) for a in fixed[:3]),
        ],
        out_shape=[
            shape((total, width), BF),
            shape((total, width), BF),
            shape(pack.shape, F32),
            shape((share, width), F32),
            shape((6, total // 2, width), BF),
            shape((6, total // 2, lanes), BF),
            shape((6, TURNED, total // 2), BF),
            *(shape(a.shape[1:], F32) for a in fixed[:3]),
        ],
        scratch_shapes=[dma((3, Across.SEMAPHORES)), dma((3, Across.SEMAPHORES))],
        compiler_params=pltpu.CompilerParams(
            vmem_limit_bytes=VMEM_LIMIT, collective_id=3, has_side_effects=True
        ),
        cost_estimate=pl.CostEstimate(flops=flops, bytes_accessed=30 * 2**20, transcendentals=0),
        name="experts",
    )(normed, cot, packed, *fixed, normed, cot, turned)


def weight_of(packed, j, count):
    return packed[:, j : j + 1].astype(F32) + packed[:, count + j : count + j + 1].astype(F32)


def routed_tile(n, c, weight, w_gate, w_up, w_down, acc_gate, acc_up, acc_down):
    d_y = jnp.concatenate([(weight * part.astype(F32)).astype(BF) for part in c], -1)
    gate, up = dot(n, w_gate), dot(n, w_up)
    d_gate, d_up = swiglu_back(dot_nt(d_y, w_down), gate, up)
    hidden = (silu(gate) * up).astype(BF)
    acc_gate[...] += dot_tn(n, d_gate)
    acc_up[...] += dot_tn(n, d_up)
    acc_down[...] += dot_tn(hidden, d_y)


def weights_kernel(
    j, count, first, size, own_steps, n_own, c_own, packed_own, n_ref, ca_ref, cb_ref, packed_ref,
    wg_ref, wu_ref, wd_ref, *refs,
):
    dg_ref, du_ref, dd_ref, wg, wu, wd, acc_gate, acc_up, acc_down, load, store = refs[-11:]
    step = pl.program_id(0)
    cols = pl.ds(first, size)

    @pl.when(step == 0)
    def _():
        copies = [
            pltpu.make_async_copy(wg_ref.at[j, :, cols], wg, load.at[0]),
            pltpu.make_async_copy(wu_ref.at[j, :, cols], wu, load.at[1]),
            pltpu.make_async_copy(wd_ref.at[j, cols], wd, load.at[2]),
        ]
        for copy in copies:
            copy.start()
        for acc in (acc_gate, acc_up, acc_down):
            acc[...] = jnp.zeros_like(acc)
        for copy in copies:
            copy.wait()

    ours = step < own_steps
    parts, at = [], 0
    for ref in (ca_ref, cb_ref):
        lanes = ref.shape[-1]
        parts.append(jnp.where(ours, c_own[:, at : at + lanes], ref[...]))
        at += lanes
    theirs = [jnp.transpose(packed_ref[k].astype(F32)) for k in range(packed_ref.shape[0])]
    theirs = weight_of(jnp.concatenate(theirs, 0), j, count)
    routed_tile(
        jnp.where(ours, n_own[...], n_ref[...]),
        parts,
        jnp.where(ours, weight_of(packed_own[...], j, count), theirs),
        wg[...], wu[...], wd[...], acc_gate, acc_up, acc_down,
    )

    @pl.when(step == pl.num_programs(0) - 1)
    def _():
        copies = [
            pltpu.make_async_copy(acc_gate, dg_ref.at[j, :, cols], store.at[0]),
            pltpu.make_async_copy(acc_up, du_ref.at[j, :, cols], store.at[1]),
            pltpu.make_async_copy(acc_down, dd_ref.at[j, cols], store.at[2]),
        ]
        for copy in copies:
            copy.start()
        for copy in copies:
            copy.wait()


def expert_weights(j, first, size, tokens, weights, grads=None):
    own, others = tokens
    width = own[0].shape[1]
    count = weights[0].shape[0]
    turned = others[-1]
    others = [a.reshape(-1, a.shape[-1]) for a in others[:-1]]
    tile = min(1024, own[0].shape[0])
    own_steps = own[0].shape[0] // tile
    steps = own_steps + others[0].shape[0] // tile

    def own_rows(a):
        return pl.BlockSpec((tile, a.shape[-1]), lambda i: (jnp.minimum(i, own_steps - 1), 0))

    def rows(a):
        return pl.BlockSpec((tile, a.shape[-1]), lambda i: (jnp.maximum(i - own_steps, 0), 0))

    half = turned.shape[-1]
    if tile >= half:
        turned_spec = pl.BlockSpec((tile // half, TURNED, half), lambda i: (jnp.maximum(i - own_steps, 0), 0, 0))
    else:
        def place(i):
            k = jnp.maximum(i - own_steps, 0)
            return k // (half // tile), 0, k % (half // tile)

        turned_spec = pl.BlockSpec((1, TURNED, tile), place)

    anywhere = pl.BlockSpec(memory_space=pl.ANY)
    dma = pltpu.SemaphoreType.DMA
    before = [] if grads is None else list(grads)
    return pl.pallas_call(
        functools.partial(weights_kernel, j, count, first, size, own_steps),
        grid=(steps,),
        in_specs=[own_rows(a) for a in own] + [rows(a) for a in others] + [turned_spec]
        + [anywhere] * (3 + len(before)),
        out_specs=[anywhere] * 3,
        out_shape=[jax.ShapeDtypeStruct(w.shape, F32) for w in weights],
        scratch_shapes=[
            pltpu.VMEM((width, size), BF), pltpu.VMEM((width, size), BF), pltpu.VMEM((size, width), BF),
            pltpu.VMEM((width, size), F32), pltpu.VMEM((width, size), F32), pltpu.VMEM((size, width), F32),
            dma((3,)), dma((3,)),
        ],
        input_output_aliases={} if grads is None else {10: 0, 11: 1, 12: 2},
        compiler_params=pltpu.CompilerParams(vmem_limit_bytes=VMEM_LIMIT),
        cost_estimate=pl.CostEstimate(
            flops=steps * tile * width * size * 12, bytes_accessed=40 * 2**20, transcendentals=0
        ),
        name="expert_weights",
    )(*own, *others, turned, *weights, *before)


class Scatter:
    def __init__(self, part, pair, far, stage, mine, theirs, sems):
        self.me = lax.axis_index("expert")
        self.chips = part.shape[0]
        self.z, self.c = self.me // 2, lax.rem(self.me, 2)
        self.part, self.pair, self.far = part, pair, far
        self.stage, self.mine, self.theirs = stage, mine, theirs
        self.send, self.recv, self.local = sems
        self.near = mine is None

    def swap(self):
        twin = self.me + 1 - 2 * self.c
        return remote(self.part.at[:, 1 - self.c], self.pair, self.send.at[0], self.recv.at[0], expert=twin)

    def own(self):
        return pltpu.make_async_copy(self.part.at[:, self.c], self.stage, self.local.at[0])

    def start(self):
        self.swap().start()
        if self.near:
            self.own().start()

    def hop(self, d):
        to, source = lax.rem(self.z + d, self.chips), lax.rem(self.z + self.chips - d, self.chips)
        out = remote(
            self.stage.at[to], self.far.at[self.z], self.send.at[d], self.recv.at[d], expert=2 * to + self.c
        )
        back = remote(
            self.stage.at[to], self.far.at[source], self.send.at[d], self.recv.at[d], expert=2 * to + self.c
        )
        return out, back

    def load(self, src, dst, k):
        copy = pltpu.make_async_copy(src, dst, self.local.at[k])
        copy.start()
        return copy

    def add_pairs(self):
        if self.near:
            self.own().wait()
        self.swap().wait_recv()

        def one(i, carry):
            if self.near:
                self.stage[i] = (self.stage[i].astype(F32) + self.pair[i].astype(F32)).astype(BF)
                return carry
            copies = [self.load(self.part.at[i, self.c], self.mine, 0), self.load(self.pair.at[i], self.theirs, 1)]
            for copy in copies:
                copy.wait()
            self.stage[i] = (self.mine[...].astype(F32) + self.theirs[...].astype(F32)).astype(BF)
            return carry

        lax.fori_loop(0, self.chips, one, 0)
        for d in range(1, self.chips):
            self.hop(d)[0].start()

    def total(self):
        acc = self.stage[self.z].astype(F32)
        for d in range(1, self.chips):
            self.hop(d)[1].wait_recv()
            source = lax.rem(self.z + self.chips - d, self.chips)
            if self.near:
                acc += self.far[source].astype(F32)
            else:
                self.load(self.far.at[source], self.mine, 0).wait()
                acc += self.mine[...].astype(F32)
        return acc

    def finish(self):
        self.swap().wait_send()
        for d in range(1, self.chips):
            self.hop(d)[0].wait_send()


def tail_kernel(
    ranks, groups, heads, slots, j, count,
    dn_ref, dwq_ref, dwk_ref, dwv_ref, dpack_ref,
    n_all, ca_all, cb_all, packed_all, wg_ref, wu_ref, wd_ref, og_ref, ou_ref, od_ref,
    dn_sum, all_ref, dg_ref, du_ref, dd_ref, *refs,
):
    if dn_ref.shape[0] > 4:
        pair, far, mine, theirs = refs[:2] + refs[-2:]
        refs = refs[2:-2]
    else:
        pair, far = refs[-2:]
        mine = theirs = None
        refs = refs[:-2]
    (
        n_buf, c_buf, p_buf, wg, wu, wd, acc_gate, acc_up, acc_down, got_ref, sum_ref, stage,
        a_send, a_recv, a_local, r_send, r_recv, t_send, t_recv, g_send, g_recv, load, fetched,
    ) = refs
    me, g = lax.axis_index("expert"), lax.axis_index("dp")
    width = n_all.shape[2]
    rows = width // ranks
    tile = n_buf.shape[1]
    half = n_all.shape[1]
    per = half // tile
    steps = n_all.shape[0] * per
    parts, at = [], 0
    for ref in (ca_all, cb_all):
        parts.append(pl.ds(at, ref.shape[-1]))
        at += ref.shape[-1]
    peers = [lax.rem(g + d, groups) for d in range(1, groups)]
    others = [lax.rem(me + d, ranks) for d in range(1, ranks)]
    banks = (dwq_ref, dwk_ref, dwv_ref, dpack_ref)

    def tile_copies(sources, into):
        targets = (n_buf.at[into], p_buf.at[into], *(c_buf.at[into, :, part] for part in parts))
        return [
            pltpu.make_async_copy(src, dst, fetched.at[into, k]) for k, (src, dst) in enumerate(zip(sources, targets))
        ]

    def fetch(t, into):
        r = aligned(lax.rem(t, per), tile)
        sources = [n_all.at[t // per, r], packed_all.at[t // per, :, r], ca_all.at[t // per, r], cb_all.at[t // per, r]]
        for copy in tile_copies(sources, into):
            copy.start()

    fetch(0, 0)
    copies = [
        pltpu.make_async_copy(src, dst, load.at[k])
        for k, (src, dst) in enumerate((
            (wg_ref.at[j], wg), (wu_ref.at[j], wu), (wd_ref.at[j], wd),
            (og_ref, acc_gate), (ou_ref, acc_up), (od_ref, acc_down),
        ))
    ]
    for copy in copies:
        copy.start()
    meet([{"expert": t} for t in others] + [{"dp": t} for t in peers])
    first = Scatter(dn_ref, pair, far, stage, mine, theirs, (a_send, a_recv, a_local))
    first.start()

    def slot(s):
        return slice(s * LANES, (s + 1) * LANES)

    def has(s, i, group):
        return jnp.logical_or(group == groups - 1, head_of(s, i, ranks) < heads)

    def reduce_copy(d, s, which):
        return remote(
            banks[which].at[:, slot(s)], got_ref.at[d - 1, :, slot(s)], r_send.at[d, s], r_recv.at[d, s], dp=peers[d - 1]
        )

    for d in range(1, groups):
        for s in range(slots):
            for which in range(groups):
                ok = jnp.logical_and(peers[d - 1] == which, has(s, me, which))
                pl.when(ok)(lambda: reduce_copy(d, s, which).start())

    for copy in copies:
        copy.wait()

    def turn_copy(d, s, i, to):
        return remote(
            sum_ref.at[to, :, slot(s)], all_ref.at[g, i, :, slot(s)], t_send.at[d, s], t_recv.at[d, s], expert=to
        )

    def add_groups():
        for s in range(slots):
            def one(s=s):
                for d in range(1, groups):
                    reduce_copy(d, s, 0).wait_recv()
                for which in range(groups):
                    def add(which=which):
                        for r in range(ranks):
                            here = slice(r * rows, (r + 1) * rows)
                            acc = banks[which][here, slot(s)].astype(F32)
                            for d in range(1, groups):
                                acc += got_ref[d - 1, here, slot(s)].astype(F32)
                            sum_ref[r, :, slot(s)] = acc.astype(BF)

                    pl.when(g == which)(add)
                all_ref[g, me, :, slot(s)] = sum_ref[me, :, slot(s)]
                for d in range(1, ranks):
                    turn_copy(d, s, me, others[d - 1]).start()

            pl.when(has(s, me, g))(one)

    by_x = g + 1 - 2 * lax.rem(g, 2)
    by_y = lax.rem(g + 2, 4)
    by_both = by_y + 1 - 2 * lax.rem(by_y, 2)

    def pieces(group, h):
        mid = ranks // 2
        found = []
        for s in range(slots):
            part = all_ref.at[group, pl.ds(h * mid, mid), :, slot(s)]
            if (s + 1) * ranks <= heads:
                found.append((True, part))
                continue
            found.append((group == groups - 1, part))
            present = [i for i in range(ranks) if head_of(s, i, ranks) < heads]
            for i in present[h::2]:
                found.append((group != groups - 1, all_ref.at[group, i, :, slot(s)]))
        return found

    def spread(k, group, h, to):
        copies = []
        for n, (ok, part) in enumerate(pieces(group, h)):
            at = (k * 2 + h) * ranks + n
            copies.append((ok, remote(part, part, g_send.at[at], g_recv.at[at], dp=to)))
        return copies

    def act(copies, what):
        for ok, copy in copies:
            guarded(ok, getattr(copy, what))

    def spread_out():
        for d in range(1, ranks):
            i = lax.rem(me + ranks - d, ranks)
            for s in range(slots):
                pl.when(has(s, i, g))(lambda: turn_copy(d, s, i, others[0]).wait_recv())
        for k, h, to in ((0, 0, by_x), (1, 1, by_y), (0, 1, by_x), (1, 0, by_y)):
            act(spread(k, g, h, to), "start")

    def pass_on():
        act(spread(0, by_x, 0, by_x), "wait_recv")
        act(spread(2, by_x, 0, by_y), "start")
        act(spread(1, by_y, 1, by_y), "wait_recv")
        act(spread(3, by_y, 1, by_x), "start")

    def keep_first():
        dn_sum[...] = first.total()

    first.add_pairs()
    hooks = [None, add_groups, None, spread_out, pass_on, keep_first]

    def step(t, carry):
        now = lax.rem(t, 2)
        pl.when(t + 1 < steps)(lambda: fetch(t + 1, 1 - now))
        r = pl.ds(0, tile)
        for copy in tile_copies([n_all.at[0, r], packed_all.at[0, :, r], ca_all.at[0, r], cb_all.at[0, r]], now):
            copy.wait()
        routed_tile(
            n_buf[now], [c_buf[now]], weight_of(jnp.transpose(p_buf[now].astype(F32)), j, count),
            wg[...], wu[...], wd[...], acc_gate, acc_up, acc_down,
        )
        for k, hook in enumerate(hooks):
            if hook is not None:
                pl.when(t == k * steps // len(hooks))(hook)
        return carry

    lax.fori_loop(0, steps, step, 0)
    stores = []
    for k, (acc, out) in enumerate(((acc_gate, dg_ref), (acc_up, du_ref), (acc_down, dd_ref))):
        half_size = (wg, wu, wd)[k]
        half_size[...] = acc[...].astype(BF)
        stores.append(pltpu.make_async_copy(half_size, out, load.at[k]))
        stores[-1].start()
    first.finish()
    for d in range(1, groups):
        for s in range(slots):
            pl.when(has(s, me, peers[d - 1]))(lambda: reduce_copy(d, s, 0).wait_send())
    act(spread(0, by_x, 1, by_x), "wait_recv")
    act(spread(1, by_y, 0, by_y), "wait_recv")
    act(spread(2, by_both, 0, by_y), "wait_recv")
    act(spread(3, by_both, 1, by_x), "wait_recv")
    for k, h, to in ((0, 0, by_x), (1, 1, by_y), (0, 1, by_x), (1, 0, by_y)):
        act(spread(k, g, h, to), "wait_send")
    act(spread(2, by_x, 0, by_y), "wait_send")
    act(spread(3, by_y, 1, by_x), "wait_send")
    for d in range(1, ranks):
        for s in range(slots):
            pl.when(has(s, me, g))(lambda: turn_copy(d, s, me, others[d - 1]).wait_send())
    for copy in stores:
        copy.wait()


def tail(ranks, groups, heads, slots, j, d_normed, d_weights, others, weights, own_grads):
    half, width = others[0].shape[1:]
    count, _, hidden = weights[0].shape
    chips = ranks // 2
    total = d_normed.shape[0]
    own = total // ranks
    rows = width // ranks
    span = slots * LANES
    tile = min(512, half)
    dma = pltpu.SemaphoreType.DMA
    shape = jax.ShapeDtypeStruct
    vmem, anywhere = pl.BlockSpec(memory_space=pltpu.VMEM), pl.BlockSpec(memory_space=pl.ANY)
    block = shape((chips, own, width), BF)
    near = chips <= 4
    return pl.pallas_call(
        functools.partial(tail_kernel, ranks, groups, heads, slots, j, count),
        out_shape=[
            shape((own, width), F32), shape((groups, ranks, rows, span), BF),
            shape((width, hidden), BF), shape((width, hidden), BF), shape((hidden, width), BF),
        ]
        + [block] * (0 if near else 2),
        in_specs=[anywhere] + [vmem] * 4 + [anywhere] * 10,
        out_specs=[vmem] * 2 + [anywhere] * (3 if near else 5),
        scratch_shapes=[
            pltpu.VMEM((2, tile, width), BF), pltpu.VMEM((2, tile, width), BF), pltpu.VMEM((2, TURNED, tile), BF),
            pltpu.VMEM((width, hidden), BF), pltpu.VMEM((width, hidden), BF), pltpu.VMEM((hidden, width), BF),
            pltpu.VMEM((width, hidden), F32), pltpu.VMEM((width, hidden), F32), pltpu.VMEM((hidden, width), F32),
            pltpu.VMEM((groups - 1, width, span), BF), pltpu.VMEM((ranks, rows, span), BF),
            pltpu.VMEM((chips, own, width), BF),
            dma((chips,)), dma((chips,)), dma((2,)),
            dma((groups, slots)), dma((groups, slots)),
            dma((ranks, slots)), dma((ranks, slots)),
            dma((8 * ranks,)), dma((8 * ranks,)),
            dma((6,)), dma((2, 4)),
        ]
        + ([pltpu.VMEM((chips, own, width), BF)] * 2 if near else [pltpu.VMEM((own, width), BF)] * 2),
        compiler_params=pltpu.CompilerParams(
            vmem_limit_bytes=VMEM_LIMIT, collective_id=4, has_side_effects=True
        ),
        cost_estimate=pl.CostEstimate(flops=total * groups * width * hidden * 12, bytes_accessed=2**26, transcendentals=0),
        name="tail",
    )(
        d_normed.reshape(chips, 2, own, width), *d_weights,
        *others, *weights, *own_grads,
    )[:5]


def outputs_kernel(
    heads, slots, j, gain_at, dn_ref, out_ref, resid_ref, dres_ref, x_ref, gain_ref, all_ref, wo_ref, sd_ref,
    eg_ref, eu_ref, ed_ref, bg_ref, bu_ref, bd_ref,
    layer_ref, dx_ref, q_ref, k_ref, v_ref, o_ref, sg_ref, su_ref, dsd_ref, small_ref, dg_ref, du_ref, dd_ref,
    hg, hu, hd, wide_g, wide_u, wide_d, load, store,
):
    loads = [
        pltpu.make_async_copy(src, dst, load.at[k])
        for k, (src, dst) in enumerate(((eg_ref, hg), (eu_ref, hu), (ed_ref, hd)))
    ]
    for copy in loads:
        copy.start()
    copies = []
    for k, (src, wide, dst) in enumerate(((hg, wide_g, dg_ref), (hu, wide_u, du_ref), (hd, wide_d, dd_ref))):
        loads[k].wait()
        wide[...] = src[...].astype(F32)
        copies.append(pltpu.make_async_copy(wide, dst.at[j], store.at[k]))
        copies[-1].start()
    layer_ref[...] = (resid_ref[...] + out_ref[...].astype(F32)).astype(BF)
    x = x_ref[...].astype(F32)
    inverse = lax.rsqrt(jnp.mean(x * x, -1, keepdims=True) + EPS)
    dx_ref[...] = (dres_ref[...] + norm_back(dn_ref[...], x, inverse, gain_ref[gain_at : gain_at + 1, :])).astype(BF)
    ranks = all_ref.shape[1]
    share = sg_ref.shape[1] // ranks
    for which, ref in enumerate((q_ref, k_ref, v_ref)):
        for h in range(heads):
            s, i = next((s, i) for s in range(slots) for i in range(ranks) if head_of(s, i, ranks) == h)
            ref[:, h * LANES : (h + 1) * LANES] = all_ref[which, i, :, s * LANES : (s + 1) * LANES].astype(F32)
    last = all_ref.shape[0] - 1
    small = jnp.zeros(small_ref.shape, F32)
    for i in range(ranks):
        here = all_ref[last, i].astype(F32)
        sg_ref[:, i * share : (i + 1) * share] = here[:, :share]
        su_ref[:, i * share : (i + 1) * share] = here[:, share : 2 * share]
        small += here
    small_ref[...] = small
    o_ref[...] = wo_ref[...].astype(F32)
    dsd_ref[...] = sd_ref[...].astype(F32)
    for copy in copies:
        copy.wait()


def outputs(heads, slots, j, gain_at, share_width, arrays, last_grads, grads):
    dn, out, resid, d_resid, x, gain, everything, d_wo, d_sd = arrays
    rows, span = everything.shape[2:]
    own, width = x.shape
    shape = jax.ShapeDtypeStruct
    vmem, anywhere = pl.BlockSpec(memory_space=pltpu.VMEM), pl.BlockSpec(memory_space=pl.ANY)
    return pl.pallas_call(
        functools.partial(outputs_kernel, heads, slots, j, gain_at),
        out_shape=[shape((own, width), BF)] * 2
        + [shape((rows, width), F32)] * 4
        + [shape((rows, share_width), F32)] * 2
        + [shape(d_sd.shape, F32), shape((rows, span), F32)]
        + [shape(a.shape, F32) for a in grads],
        in_specs=[vmem] * 9 + [anywhere] * 6,
        out_specs=[vmem] * 10 + [anywhere] * 3,
        scratch_shapes=[pltpu.VMEM(a.shape, BF) for a in last_grads]
        + [pltpu.VMEM(a.shape, F32) for a in last_grads]
        + [pltpu.SemaphoreType.DMA((3,)), pltpu.SemaphoreType.DMA((3,))],
        input_output_aliases={12: 10, 13: 11, 14: 12},
        compiler_params=pltpu.CompilerParams(vmem_limit_bytes=VMEM_LIMIT),
        name="outputs",
    )(*arrays, *last_grads, *grads)


def norm_back(grad, values, inverse, gain):
    scaled = grad * gain
    inner = jnp.mean(scaled * values, -1, keepdims=True)
    return inverse * scaled - values * inverse**3 * inner


def body(
    tokens, cotangent, attn_gain, ffn_gain, w_query, w_key, w_value, w_output, router,
    shared_gate, shared_up, shared_down, expert_gate, expert_up, expert_down, expert_ids,
):
    ranks = lax.axis_size("expert")
    me = lax.axis_index("expert")
    seqs, own_pos, width = tokens.shape
    length = own_pos * ranks
    total = seqs * length
    own = seqs * own_pos
    rows = w_query.shape[0]
    heads = width // HEAD_DIM
    slots = -(-heads // ranks)
    span = slots * HEAD_DIM
    share = shared_gate.shape[1] // ranks
    names = router.shape[1]
    count = expert_gate.shape[0]

    groups = lax.axis_size("dp")

    def in_order(a):
        return a.reshape(ranks, seqs, own_pos, -1).transpose(1, 0, 2, 3).reshape(total, -1)

    def by_rank(a):
        return a.reshape(seqs, ranks, own_pos, -1).transpose(1, 0, 2, 3).reshape(total, -1)

    rest = jnp.concatenate([router, attn_gain[:, None], ffn_gain[:, None]], -1)
    edges = [0, share, 2 * share, 2 * share + names, 2 * share + names + 1]
    gain_at = edges[3] - (slots - 1) * LANES
    top = expert_ids.shape[-1]
    cosine, sine = rotary_tables(length)
    (
        group_x, group_c, w_q, w_k, w_v, w_pack, small, half_out, inverse_one, q, k, v, mixed, lse,
    ) = front(
        ranks, groups, heads, seqs, slots, gain_at, tokens.reshape(own, width), cotangent.reshape(own, width),
        expert_ids.reshape(own, top), w_query, w_key, w_value, shared_gate, shared_up, rest, w_output,
        cosine, sine,
    )
    group_c = group_c.reshape(total, -1)
    gain_two = small[gain_at + 1 : gain_at + 2]
    units = width // LANES
    c_last = max(units // 5, 1) * LANES
    c_first = width - c_last
    resid, normed_two, all_mixed, all_out, packed, turned, all_ca = project(
        ranks, groups, heads, slots, count, top, edges[2], c_first, group_x, by_rank(mixed), half_out, small, w_pack, group_c
    )
    layer_part, d_normed_part, d_pack, d_s_down, all_n, all_cb, all_w, *own_grads = experts(
        ranks, c_last, normed_two, group_c, packed, turned, expert_gate, expert_up, expert_down, w_pack, shared_down
    )
    every = ((normed_two, group_c, packed), (all_n, all_ca, all_cb, all_w))
    banks = (expert_gate, expert_up, expert_down)
    hidden = expert_gate.shape[-1]
    cut = hidden * 4 // 7 if hidden % (7 * LANES) == 0 else hidden // 2

    def after(late, *earlier):
        return lax.optimization_barrier((late, earlier))[0]

    def scatter(partial):
        return lax.psum_scatter(partial, "expert", scatter_dimension=0, tiled=True)

    grads = expert_weights(0, 0, cut, every, banks)
    d_normed_two, grads = lax.optimization_barrier((scatter(d_normed_part), grads))
    d_normed_two = d_normed_two.astype(F32)
    inverse_two = lax.rsqrt(jnp.mean(resid * resid, -1, keepdims=True) + EPS)
    ffn_gain_part = jnp.sum(d_normed_two * resid * inverse_two, 0)
    d_out = cotangent.reshape(own, width).astype(F32)
    d_resid = d_out + norm_back(d_normed_two, resid, inverse_two, gain_two)
    own_att = d_resid.astype(BF)
    d_att = lax.all_gather(own_att, "expert", axis=0, tiled=True)
    grads = expert_weights(0, cut, hidden - cut, after(every, own_att), banks, grads)
    d_att, grads = lax.optimization_barrier((d_att, grads))

    d_normed_part, d_wq, d_wk, d_wv, attn_gain_part = attend_back(
        ranks, heads, seqs, slots, gain_at, in_order(d_att), in_order(group_x), inverse_one, small,
        (w_q, w_k, w_v), all_out, cosine, sine, q, k, v, lse
    )
    column = jnp.arange(span)[None, :]
    d_pack = jnp.where(column == edges[3], attn_gain_part.reshape(width, 1), d_pack)
    d_pack = jnp.where(column == edges[4], ffn_gain_part[:, None], d_pack).astype(BF)
    own_mixed = lax.dynamic_slice_in_dim(all_mixed, me * rows, rows, 1)
    d_wo_rows = dot_tn(own_mixed, d_att).astype(BF)
    d_wo_rows, d_sd_rows = lax.psum((d_wo_rows, d_s_down.astype(BF)), "dp")
    dn_sum, all_grads, *last_grads = tail(
        ranks, groups, heads, slots, 1, by_rank(d_normed_part), (d_wq, d_wk, d_wv, d_pack), every[1], banks, own_grads
    )
    layer_output, input_grad, g_q, g_k, g_v, g_o, g_sg, g_su, g_sd, small, g_gate, g_up, g_down = outputs(
        heads, slots, 1, gain_at, ranks * share,
        (dn_sum, scatter(after(layer_part, d_att)), resid, d_resid, tokens.reshape(own, width), small, all_grads, d_wo_rows, d_sd_rows),
        last_grads, grads,
    )
    g_r = small[:, edges[2] : edges[3]]
    g_one = small[:, edges[3]]
    g_two = small[:, edges[4]]
    return (
        layer_output.reshape(tokens.shape), input_grad.reshape(tokens.shape),
        g_one, g_two, g_q, g_k, g_v, g_o, g_r, g_sg, g_su, g_sd, g_gate, g_up, g_down,
    )


def solution(mesh):
    row = P("expert", None)
    experts_spec = P("expert", None, None)
    tokens_spec = P("dp", "expert", None)
    return jax.shard_map(
        body,
        mesh=mesh,
        in_specs=(tokens_spec, tokens_spec, P("expert"), P("expert"))
        + (row,) * 8
        + (experts_spec,) * 3
        + (P(("dp", "expert"), None, None),),
        out_specs=(tokens_spec, tokens_spec, P("expert"), P("expert")) + (row,) * 8 + (experts_spec,) * 3,
        check_vma=False,
    )
```

```python
import functools

import jax
import jax.numpy as jnp
import numpy as np
from jax import lax
from jax.experimental import pallas as pl
from jax.experimental.pallas import tpu as pltpu
from jax.sharding import PartitionSpec as P

HEAD_DIM = 128
LANES = 128
TURNED = 16
EPS = 1e-06
MASKED = -1e30
VMEM_LIMIT = 60 * 2**20
BF = jnp.bfloat16
F32 = jnp.float32


def dot(a, b):
    return jnp.dot(a, b, preferred_element_type=F32)


def dot_nt(a, b):
    return lax.dot_general(a, b, (((1,), (1,)), ((), ())), preferred_element_type=F32)


def dot_tn(a, b):
    return lax.dot_general(a, b, (((0,), (0,)), ((), ())), preferred_element_type=F32)


def silu(v):
    return v / (1.0 + jnp.exp(-v))


def swiglu_back(d_hidden, gates, ups):
    sigma = 1.0 / (1.0 + jnp.exp(-gates))
    d_gate = d_hidden * ups * sigma * (1.0 + gates * (1.0 - sigma))
    d_up = d_hidden * (gates * sigma)
    return d_gate.astype(BF), d_up.astype(BF)


def rotary_tables(length):
    half = HEAD_DIM // 2
    inverse_freq = np.float32(10000.0) ** (-np.arange(half, dtype=np.float32) * np.float32(2.0 / HEAD_DIM))
    angles = np.arange(length, dtype=np.float32)[:, None] * inverse_freq[None, :]
    cosine, sine = np.cos(angles), np.sin(angles)
    tables = np.concatenate([cosine, cosine], -1), np.concatenate([-sine, sine], -1)
    return tuple(jnp.asarray(t.astype(np.float32)) for t in tables)


def vmem_call(kernel, outs, *args, **kwargs):
    spec = pl.BlockSpec(memory_space=pltpu.VMEM)
    return pl.pallas_call(
        kernel,
        out_shape=outs,
        in_specs=[spec] * len(args),
        out_specs=[spec] * len(outs),
        compiler_params=pltpu.CompilerParams(vmem_limit_bytes=VMEM_LIMIT),
        **kwargs,
    )(*args)


def row_block(length):
    return 256 if length % 256 == 0 else length


def remote(src, dst, send, recv, **device):
    return pltpu.make_async_remote_copy(
        src_ref=src, dst_ref=dst, send_sem=send, recv_sem=recv, device_id=device, device_id_type=pl.DeviceIdType.MESH
    )


def meet(peers):
    barrier = pltpu.get_barrier_semaphore()
    for peer in peers:
        pl.semaphore_signal(barrier, inc=1, device_id=peer, device_id_type=pl.DeviceIdType.MESH)
    pl.semaphore_wait(barrier, len(peers))


def meet_near(chips, z, me, peers=()):
    barrier = pltpu.get_barrier_semaphore()
    near = [(True, {"expert": me + 1 - 2 * lax.rem(me, 2)}), (z > 0, {"expert": me - 2}), (z < chips - 1, {"expert": me + 2})]
    near += [(True, {"dp": t}) for t in peers]

    def signal(t):
        pl.semaphore_signal(barrier, inc=1, device_id=t, device_id_type=pl.DeviceIdType.MESH)

    for ok, t in near:
        guarded(ok, functools.partial(signal, t))
    ends = jnp.where(z > 0, 1, 0) + jnp.where(z < chips - 1, 1, 0)
    pl.semaphore_wait(barrier, 1 + len(peers) + ends)


def both(*conditions):
    held = [c for c in conditions if c is not True]
    if not held:
        return True
    out = held[0]
    for c in held[1:]:
        out = jnp.logical_and(out, c)
    return out


def guarded(condition, action):
    if condition is True:
        action()
    else:
        pl.when(condition)(action)


class LineGather:
    def __init__(self, ranks, own, block, send, recv, base=0, valid=lambda i: True, twins=True):
        self.me = lax.axis_index("expert")
        self.chips = ranks // 2
        self.z = self.me // 2
        self.twin = self.me + 1 - 2 * lax.rem(self.me, 2)
        self.own, self.block, self.send, self.recv, self.base, self.valid = own, block, send, recv, base, valid
        self.twins = twins

    @staticmethod
    def semaphores(ranks):
        return 4 * (ranks // 2 - 1) + 1

    def copy(self, src, i, k, to):
        return remote(src, self.block(i), self.send.at[self.base + k], self.recv.at[self.base + k], expert=to)

    def sources(self, s):
        hops = self.chips - 1
        return (
            (self.me - 2 * s, self.z - s >= 0, self.z < hops, self.me + 2, 0, 2 * hops, -2 * s),
            (self.me + 2 * s, self.z + s <= hops, self.z > 0, self.me - 2, hops, 3 * hops, 2 * s),
        )

    def start(self):
        hops = self.chips - 1
        mine = self.valid(self.me)
        if hops:
            guarded(both(self.z < hops, mine), lambda: self.copy(self.own, self.me, 0, self.me + 2).start())
            guarded(both(self.z > 0, mine), lambda: self.copy(self.own, self.me, hops, self.me - 2).start())
        if self.twins:
            guarded(mine, lambda: self.copy(self.own, self.me, 2 * hops, self.twin).start())

    def step(self, s):
        for i, there, more, to, k, pair, _ in self.sources(s):
            known = both(there, self.valid(i))
            src = self.block(i)
            guarded(known, lambda: self.copy(src, i, k + s - 1, self.twin).wait_recv())
            if s < self.chips - 1:
                guarded(both(known, more), lambda: self.copy(src, i, k + s, to).start())
            if self.twins:
                guarded(known, lambda: self.copy(src, i, pair + s, self.twin).start())

    def finish(self):
        hops = self.chips - 1
        mine = self.valid(self.me)
        theirs = self.valid(self.twin)
        if self.twins:
            guarded(mine, lambda: self.copy(self.own, self.me, 2 * hops, self.twin).wait_send())
            guarded(theirs, lambda: self.copy(self.own, self.twin, 2 * hops, self.twin).wait_recv())
        if hops:
            guarded(both(self.z < hops, mine), lambda: self.copy(self.own, self.me, 0, self.twin).wait_send())
            guarded(both(self.z > 0, mine), lambda: self.copy(self.own, self.me, hops, self.twin).wait_send())
        for s in range(1, self.chips):
            for i, there, more, to, k, pair, shift in self.sources(s):
                known = both(there, self.valid(i))
                src = self.block(i)
                if s < hops:
                    guarded(both(known, more), lambda: self.copy(src, i, k + s, self.twin).wait_send())
                if not self.twins:
                    continue
                guarded(known, lambda: self.copy(src, i, pair + s, self.twin).wait_send())
                j = self.twin + shift
                got = both(there, self.valid(j))
                guarded(got, lambda: self.copy(self.block(j), j, pair + s, self.twin).wait_recv())


class Across:
    SEMAPHORES = 12

    def __init__(self, source, dst, send, recv):
        self.me, self.g = lax.axis_index("expert"), lax.axis_index("dp")
        self.twin = self.me + 1 - 2 * lax.rem(self.me, 2)
        self.by_x = self.g + 1 - 2 * lax.rem(self.g, 2)
        self.by_y = lax.rem(self.g + 2, 4)
        self.source, self.dst, self.send, self.recv = source, dst, send, recv
        self.half = dst.shape[1]
        self.part = self.half // 2

    def peers(self):
        return [{"dp": self.by_x}, {"dp": self.by_y}, {"expert": self.twin}]

    def piece(self, slot, j):
        return self.dst.at[slot, pl.ds(j * self.part, self.part)]

    def mine(self, j):
        first = lax.rem(self.me, 2) * self.half + j * self.part
        return self.source(pl.ds(pl.multiple_of(first, self.part), self.part))

    def copy(self, k, src, dst, **to):
        return remote(src, dst, self.send.at[k], self.recv.at[k], **to)

    def direct(self, k):
        slot, j, to = ((0, 0, self.by_x), (1, 1, self.by_y), (0, 1, self.by_x), (1, 0, self.by_y))[k]
        return self.copy(k, self.mine(j), self.piece(slot, j), dp=to)

    def relayed(self, j):
        if j == 0:
            return self.copy(4, self.piece(0, 0), self.piece(2, 0), dp=self.by_y)
        return self.copy(5, self.piece(1, 1), self.piece(2, 1), dp=self.by_x)

    def shared(self, slot, j):
        return self.copy(6 + 2 * slot + j, self.piece(slot, j), self.piece(slot + 3, j), expert=self.twin)

    def start(self):
        for k in range(2):
            self.direct(k).start()

    def more(self):
        for k in range(2, 4):
            self.direct(k).start()

    def relay(self):
        self.direct(0).wait_recv()
        self.relayed(0).start()
        self.direct(1).wait_recv()
        self.relayed(1).start()
        self.shared(0, 0).start()
        self.shared(1, 1).start()

    def hand_over(self):
        self.direct(2).wait_recv()
        self.shared(0, 1).start()
        self.direct(3).wait_recv()
        self.shared(1, 0).start()

    def finish(self):
        for j in range(2):
            self.relayed(j).wait_recv()
            self.shared(2, j).start()
        for k in range(4):
            self.direct(k).wait_send()
        for j in range(2):
            self.relayed(j).wait_send()
            for slot in range(3):
                self.shared(slot, j).wait()


class SameExperts:
    SEMAPHORES = 6

    def __init__(self, source, dst, send, recv):
        self.me, self.g = lax.axis_index("expert"), lax.axis_index("dp")
        self.near = [self.g + 1 - 2 * lax.rem(self.g, 2), lax.rem(self.g + 2, 4)]
        self.near.append(self.near[1] + 1 - 2 * lax.rem(self.near[1], 2))
        self.source, self.dst, self.send, self.recv = source, dst, send, recv
        self.half = dst.shape[2]

    def peers(self):
        return [{"dp": self.near[2]}]

    def copy(self, k, h):
        slot = k + 3 * lax.rem(lax.rem(self.me, 2) + h, 2)
        i = 2 * k + h
        src = self.source.at[:, pl.ds(h * self.half, self.half)]
        return remote(src, self.dst.at[slot], self.send.at[i], self.recv.at[i], dp=self.near[k])

    def start(self):
        for k in range(3):
            for h in range(2):
                self.copy(k, h).start()

    def relay(self):
        pass

    hand_over = more = relay

    def finish(self):
        for k in range(3):
            for h in range(2):
                self.copy(k, h).wait()


def head_of(s, i, ranks):
    return i if s == 0 else s * ranks + i // 2 + (i % 2) * (ranks // 2)


def aligned(i, size):
    return pl.ds(pl.multiple_of(i * size, size), size)


def front_kernel(
    ranks, groups, heads, seqs, slots, gain_at,
    x_ref, c_ref, id_ref, wq_ref, wk_ref, wv_ref, sg_ref, su_ref, rest_ref, wo_ref, cos_ref, sin_ref,
    gx_ref, gc_ref, wqs_ref, wks_ref, wvs_ref, wps_ref, small_ref, half_ref,
    inv_ref, q_ref, k_ref, v_ref, mixed_ref, lse_ref, stage_ref, land_ref, ostage_ref,
    x_send, x_recv, c_send, c_recv, w_send, w_recv, d_send, d_recv, o_send, o_recv, p_send, p_recv,
):
    me, g = lax.axis_index("expert"), lax.axis_index("dp")
    rows, width = wq_ref.shape
    units = width // LANES
    per = ostage_ref.shape[0]
    peers = [lax.rem(g + d, groups) for d in range(1, groups)]
    others = [lax.rem(me + d, ranks) for d in range(1, ranks)]
    meet([{"expert": t} for t in others] + [{"dp": t} for t in peers])

    def stage_heads(w):
        for u in range(heads):
            stage_ref[u] = w[:, u * LANES : (u + 1) * LANES]

    for which, w in enumerate((wq_ref, wk_ref, wv_ref)):
        pl.when(g == which)(functools.partial(stage_heads, w))

    def stage_pack():
        share = sg_ref.shape[1] // ranks
        spare = slots * LANES - 2 * share - rest_ref.shape[1]
        for t in range(ranks):
            cols = slice(t * share, (t + 1) * share)
            pieces = [sg_ref[:, cols], su_ref[:, cols], rest_ref[...]]
            if spare:
                pieces.append(jnp.zeros((rows, spare), BF))
            packed = jnp.concatenate(pieces, -1)
            for s in range(slots):
                stage_ref[head_of(s, t, ranks)] = packed[:, s * LANES : (s + 1) * LANES]

    pl.when(g == groups - 1)(stage_pack)

    def known(s, t, group=None):
        return jnp.logical_or((g if group is None else group) == groups - 1, head_of(s, t, ranks) < heads)

    def weight_copy(s, d, unit, i, to):
        return remote(
            stage_ref.at[unit], land_ref.at[g, s, i], w_send.at[s, d], w_recv.at[s, d], expert=to
        )

    for d in range(1, ranks):
        t = others[d - 1]
        for s in range(slots):
            guarded(known(s, t), lambda: weight_copy(s, d, head_of(s, t, ranks), me, t).start())

    def stage_out(which):
        for k in range(per):
            u = which * per + k
            if u < units:
                ostage_ref[k] = wo_ref[:, u * LANES : (u + 1) * LANES]

    for which in range(groups):
        pl.when(g == which)(functools.partial(stage_out, which))
    out_rows = LineGather(
        ranks, ostage_ref, lambda i: half_ref.at[g, :, i // 2], o_send, o_recv, twins=False
    )
    out_rows.start()
    tokens = LineGather(ranks, x_ref, lambda i: gx_ref.at[i], x_send, x_recv)
    tokens.start()
    half_ref[g, :, me // 2] = ostage_ref[...]
    for s in range(slots):
        def keep(s=s):
            land_ref[g, s, me] = stage_ref[head_of(s, me, ranks)]

        pl.when(known(s, me))(keep)
        for which in range(groups - 1):
            def clear(s=s, which=which):
                land_ref[which, s] = jnp.zeros(land_ref.shape[2:], BF)

            pl.when(head_of(s, me, ranks) >= heads)(clear)
    gx_ref[me] = x_ref[...]
    gc_ref[me, :, :width] = c_ref[...]
    routes = id_ref[...].astype(F32).astype(BF)
    blank = jnp.zeros((routes.shape[0], LANES - routes.shape[1]), BF)
    gc_ref[me, :, width:] = jnp.concatenate([routes, blank], -1)

    def share(s, part, d, to):
        return remote(part, part, d_send.at[s, d], d_recv.at[s, d], dp=to)

    def pass_on(i):
        for s in range(slots):
            part = land_ref.at[g, s, i]
            for d in range(1, groups):
                pl.when(known(s, me))(lambda: share(s, part, d, peers[d - 1]).start())

    def out_share(d, k, group):
        part = half_ref.at[group, k]
        return remote(part, part, p_send.at[d, k], p_recv.at[d, k], dp=peers[d - 1])

    def held(group, k):
        return True if (groups - 1) * per + k < units else group * per + k < units

    pass_on(me)
    for d in range(1, ranks):
        i = lax.rem(me + ranks - d, ranks)
        for s in range(slots):
            pl.when(known(s, me))(lambda: weight_copy(s, d, 0, i, others[0]).wait_recv())
        pass_on(i)
    steps = ranks // 2 - 1
    for step in range(1, steps + 1):
        out_rows.step(step)
        if step == 1:
            tokens.step(1)
    out_rows.finish()
    for d in range(1, groups):
        for k in range(per):
            guarded(held(g, k), out_share(d, k, g).start)
    cots = LineGather(ranks, gc_ref.at[me], lambda i: gc_ref.at[i], c_send, c_recv)
    for step in range(2, steps + 1):
        tokens.step(step)
        if step == steps - 1:
            cots.start()
    if steps < 3:
        cots.start()
    tokens.finish()
    for d in range(1, groups):
        there = lax.rem(g + groups - d, groups)
        for s in range(slots):
            pl.when(known(s, me, there))(lambda: share(s, land_ref.at[there, s], d, peers[d - 1]).wait_recv())
    for which, ref in enumerate((wqs_ref, wks_ref, wvs_ref, wps_ref)):
        for s in range(slots):
            for r in range(ranks):
                ref[r * rows : (r + 1) * rows, s * LANES : (s + 1) * LANES] = land_ref[which, s, r]
    small_ref[...] = jnp.transpose(wps_ref[:, (slots - 1) * LANES :].astype(F32))
    attend(
        seqs, slots, gain_at, gx_ref, small_ref, wqs_ref, wks_ref, wvs_ref, cos_ref, sin_ref,
        inv_ref, q_ref, k_ref, v_ref, mixed_ref, lse_ref,
        [functools.partial(cots.step, step) for step in range(1, steps + 1)],
    )
    cots.finish()
    for d in range(1, ranks):
        t = others[d - 1]
        for s in range(slots):
            pl.when(known(s, t))(lambda: weight_copy(s, d, 0, me, t).wait_send())
    for d in range(1, groups):
        there = lax.rem(g + groups - d, groups)
        for s in range(slots):
            pl.when(known(s, me))(lambda: share(s, land_ref.at[g, s], d, peers[d - 1]).wait_send())
        for k in range(per):
            guarded(held(g, k), out_share(d, k, g).wait_send)
            guarded(held(there, k), out_share(d, k, there).wait_recv)


def front(
    ranks, groups, heads, seqs, slots, gain_at, x, cot, ids, w_query, w_key, w_value, s_gate, s_up, rest, w_output,
    cosine, sine,
):
    own, width = x.shape
    total, span = ranks * own, slots * LANES
    rows = w_query.shape[0]
    per = -(-(width // LANES) // groups)
    line = LineGather.semaphores(ranks)
    dma = pltpu.SemaphoreType.DMA
    spec = pl.BlockSpec(memory_space=pltpu.VMEM)
    shape = jax.ShapeDtypeStruct
    return pl.pallas_call(
        functools.partial(front_kernel, ranks, groups, heads, seqs, slots, gain_at),
        out_shape=[shape((ranks, own, width), BF), shape((ranks, own, width + LANES), BF)]
        + [shape((width, slots * LANES), BF)] * 4
        + [shape((LANES, width), F32), shape((groups, per, ranks // 2, rows, LANES), BF)]
        + [shape((total, 1), F32)]
        + [shape((total, span), BF)] * 4
        + [shape((total, slots), F32)],
        in_specs=[spec] * 12,
        out_specs=[spec] * 14,
        scratch_shapes=[
            pltpu.VMEM((slots * ranks, rows, LANES), BF),
            pltpu.VMEM((groups, slots, ranks, rows, LANES), BF),
            pltpu.VMEM((per, rows, LANES), BF),
            dma((line,)), dma((line,)),
            dma((line,)), dma((line,)),
            dma((slots, ranks)), dma((slots, ranks)),
            dma((slots, groups)), dma((slots, groups)),
            dma((line,)), dma((line,)),
            dma((groups, per)), dma((groups, per)),
        ],
        compiler_params=pltpu.CompilerParams(
            collective_id=0, has_side_effects=True, vmem_limit_bytes=VMEM_LIMIT
        ),
        name="front",
    )(x, cot, ids, w_query, w_key, w_value, s_gate, s_up, rest, w_output, cosine, sine)


def project_kernel(
    ranks, groups, heads, slots, count, top, route_at,
    x_ref, mixed_ref, half_ref, small_ref, pack_ref, c_ref,
    resid_ref, n_ref, all_ref, wo_ref, packed_ref, turned_ref, c_all_ref, other_ref, id_ref,
    send, recv, t_send, t_recv, a_send, a_recv, load,
):
    me, g = lax.axis_index("expert"), lax.axis_index("dp")
    chips = ranks // 2
    z = me // 2
    twin = me + 1 - 2 * lax.rem(me, 2)
    per, part = half_ref.shape[1], half_ref.shape[3]
    units = wo_ref.shape[1] // LANES
    peers = [lax.rem(g + d, groups) for d in range(1, groups)]
    lanes = c_all_ref.shape[-1]
    across = Across(lambda r: c_ref.at[r, pl.ds(0, lanes)], c_all_ref, a_send, a_recv)
    meet_near(chips, z, me, peers)
    ids = pltpu.make_async_copy(c_ref.at[:, pl.ds(wo_ref.shape[1], LANES)], id_ref, load)
    ids.start()
    line = LineGather.semaphores(ranks)
    parts = []
    for s in range(slots):
        def head(i, s=s):
            return aligned(jnp.clip(head_of(s, i, ranks), 0, heads - 1), LANES)

        cols = slice(s * LANES, (s + 1) * LANES)
        ok = (lambda i: True) if (s + 1) * ranks <= heads else (lambda i, s=s: head_of(s, i, ranks) < heads)
        gather = LineGather(
            ranks, mixed_ref.at[:, cols], lambda i, head=head: all_ref.at[:, head(i)], send, recv, s * line, ok
        )
        gather.start()
        parts.append(gather)

    across.start()
    across.more()
    for s, gather in enumerate(parts):
        def keep(s=s):
            cols = slice(s * LANES, (s + 1) * LANES)
            all_ref[:, aligned(jnp.clip(head_of(s, me, ranks), 0, heads - 1), LANES)] = mixed_ref[:, cols]

        guarded(gather.valid(me), keep)

    def share_twin(group, k):
        src = half_ref.at[group, k]
        return remote(src, other_ref.at[group, k], t_send.at[group, k], t_recv.at[group, k], expert=twin)

    def each_unit(action):
        for group in range(groups):
            for k in range(per):
                if group * per + k < units:
                    action(share_twin(group, k))

    each_unit(lambda copy: copy.start())
    def lay_out(even, odd):
        for u in range(units):
            cols = slice(u * LANES, (u + 1) * LANES)
            for c in range(chips):
                wo_ref[2 * c * part : (2 * c + 1) * part, cols] = even[u // per, u % per, c]
                wo_ref[(2 * c + 1) * part : (2 * c + 2) * part, cols] = odd[u // per, u % per, c]

    middle = (chips + 1) // 2
    for step in range(1, chips):
        for gather in parts:
            gather.step(step)
        if step == middle:
            across.relay()
            each_unit(lambda copy: copy.wait())
            pl.when(me == 2 * z)(lambda: lay_out(half_ref, other_ref))
            pl.when(me != 2 * z)(lambda: lay_out(other_ref, half_ref))
    for gather in parts:
        gather.finish()
    ids.wait()
    blocks, own, width = x_ref.shape
    names = ranks * count
    gain_at = route_at + names + 1 - (slots - 1) * LANES
    gain = small_ref[gain_at : gain_at + 1, :]
    tile = 2 if own <= 128 and blocks % 2 == 0 else 1

    def rows_of(b):
        rows = aligned(b, tile * own)
        x = x_ref[pl.ds(b * tile, tile)].reshape(tile * own, width).astype(F32)
        resid = x + dot(all_ref[rows, :], wo_ref[...])
        inverse = lax.rsqrt(jnp.mean(resid * resid, -1, keepdims=True) + EPS)
        normed = (resid * inverse * gain).astype(BF)
        n_ref[rows, :] = normed
        for t in range(tile):
            def keep(t=t):
                resid_ref[...] = resid[t * own : (t + 1) * own]

            pl.when(b * tile + t == me)(keep)
        probs = route_probs(dot(normed, pack_ref[...]), route_at, names)
        routes = id_ref[rows, :].astype(jnp.int32)
        lane = lax.broadcasted_iota(jnp.int32, routes.shape, 1)
        out = jnp.zeros((tile * own, LANES), F32)
        for j in range(count):
            mine = me * count + j
            chosen = jnp.max(jnp.where((routes == mine) & (lane < top), 1.0, 0.0), -1, keepdims=True)
            names_at = lax.broadcasted_iota(jnp.int32, probs.shape, 1)
            weight = chosen * jnp.sum(jnp.where(names_at == mine, probs, 0.0), -1, keepdims=True)
            high = weight.astype(BF).astype(F32)
            out = jnp.where(lane == j, high, out)
            out = jnp.where(lane == count + j, weight - high, out)
        packed_ref[rows, :] = out.astype(BF)
        turned_ref[:, rows] = jnp.transpose(out)[:turned_ref.shape[0]].astype(BF)

    half = blocks // tile // 2
    lax.fori_loop(0, half, lambda b, c: (rows_of(b), c)[1], 0)
    across.hand_over()
    lax.fori_loop(half, blocks // tile, lambda b, c: (rows_of(b), c)[1], 0)
    across.finish()


def route_probs(products, first, names):
    logits = products[:, first : first + names]
    raised = jnp.exp(logits - jnp.max(logits, -1, keepdims=True))
    return raised / jnp.sum(raised, -1, keepdims=True)


def project(ranks, groups, heads, slots, count, top, route_at, lanes, x, mixed, half, small, pack, cot):
    blocks, own, width = x.shape
    total = blocks * own
    line = LineGather.semaphores(ranks)
    per = half.shape[1]
    dma = pltpu.SemaphoreType.DMA
    spec = pl.BlockSpec(memory_space=pltpu.VMEM)
    anywhere = pl.BlockSpec(memory_space=pl.ANY)
    shape = jax.ShapeDtypeStruct
    return pl.pallas_call(
        functools.partial(project_kernel, ranks, groups, heads, slots, count, top, route_at),
        out_shape=[
            shape((own, width), F32),
            shape((total, width), BF),
            shape((total, width), BF),
            shape((width, width), BF),
            shape((total, LANES), BF),
            shape((TURNED, total), BF),
            shape((6, total // 2, lanes), BF),
        ],
        in_specs=[spec] * 5 + [anywhere],
        out_specs=[spec] * 6 + [anywhere],
        scratch_shapes=[
            pltpu.VMEM(half.shape, BF), pltpu.VMEM((total, LANES), BF),
            dma((slots * line,)), dma((slots * line,)),
            dma((groups, per)), dma((groups, per)),
            dma((Across.SEMAPHORES,)), dma((Across.SEMAPHORES,)), dma(()),
        ],
        compiler_params=pltpu.CompilerParams(
            collective_id=1, has_side_effects=True, vmem_limit_bytes=VMEM_LIMIT
        ),
        name="project",
    )(x, mixed, half, small, pack, cot)


def attend(
    seqs, slots, gain_at, x_ref, small_ref, wq_ref, wk_ref, wv_ref, cos_ref, sin_ref,
    inv_ref, q_ref, k_ref, v_ref, mixed_ref, lse_ref, hooks,
):
    ranks, own, width = x_ref.shape
    pos = own // seqs
    length = ranks * pos
    block = row_block(length)
    count = block // pos
    scale = HEAD_DIM ** (-0.5)
    gain = small_ref[gain_at : gain_at + 1, :]
    hooks = list(hooks)

    def progress():
        if hooks:
            hooks.pop(0)()

    for s in range(seqs):
        for i in range(length // block):
            rows = pl.ds(s * length + i * block, block)
            x = [x_ref[e, s * pos : (s + 1) * pos, :] for e in range(i * count, (i + 1) * count)]
            x = jnp.concatenate(x, 0).astype(F32)
            inv = lax.rsqrt(jnp.mean(x * x, -1, keepdims=True) + EPS)
            normed = (x * inv * gain).astype(BF)
            inv_ref[rows, :] = inv
            cosine = cos_ref[pl.ds(i * block, block), :]
            sine = sin_ref[pl.ds(i * block, block), :]
            queries, keyed, valued = dot(normed, wq_ref[...]), dot(normed, wk_ref[...]), dot(normed, wv_ref[...])
            for h in range(slots):
                cols = slice(h * HEAD_DIM, (h + 1) * HEAD_DIM)
                q, k = queries[:, cols], keyed[:, cols]
                q_ref[rows, cols] = (q * cosine + pltpu.roll(q, HEAD_DIM // 2, 1) * sine).astype(BF)
                k_ref[rows, cols] = (k * cosine + pltpu.roll(k, HEAD_DIM // 2, 1) * sine).astype(BF)
            v_ref[rows, :] = valued.astype(BF)
    progress()
    for s in range(seqs):
        for i in range(length // block):
            if i:
                progress()
            rows = pl.ds(s * length + i * block, block)
            keys = pl.ds(s * length, (i + 1) * block)
            shape = (block, (i + 1) * block)
            seen = (
                lax.broadcasted_iota(jnp.int32, shape, 1)
                <= lax.broadcasted_iota(jnp.int32, shape, 0) + i * block
            )
            for h in range(slots):
                cols = slice(h * HEAD_DIM, (h + 1) * HEAD_DIM)
                scores = dot_nt(q_ref[rows, cols], k_ref[keys, cols]) * scale
                scores = jnp.where(seen, scores, MASKED)
                top = jnp.max(scores, -1, keepdims=True)
                raised = jnp.exp(scores - top)
                totals = jnp.sum(raised, -1, keepdims=True)
                probs = (raised / totals).astype(BF)
                mixed_ref[rows, cols] = dot(probs, v_ref[keys, cols]).astype(BF)
                lse_ref[rows, h : h + 1] = top + jnp.log(totals)
    while hooks:
        progress()


def attend_back_kernel(
    ranks, heads, seqs, slots, gain_at, da_ref, x_ref, inv_ref, small_ref, wq_ref, wk_ref, wv_ref, wall_ref,
    cos_ref, sin_ref,
    q_ref, k_ref, v_ref, lse_ref,
    dn_ref, dwq_ref, dwk_ref, dwv_ref, gain_ref, dmix_ref, dqkv_ref, dk_ref, dv_ref, wo_ref,
):
    total, width = da_ref.shape
    length = total // seqs
    block = row_block(length)
    count = length // block
    scale = HEAD_DIM ** (-0.5)
    span = slots * HEAD_DIM
    me = lax.axis_index("expert")
    for h in range(slots):
        cols = slice(h * HEAD_DIM, (h + 1) * HEAD_DIM)
        head = head_of(h, me, ranks)
        rows_here = wall_ref[aligned(jnp.minimum(head, heads - 1), HEAD_DIM), :]
        wo_ref[cols, :] = jnp.where(head < heads, rows_here, jnp.zeros_like(rows_here))
    for s in range(seqs):
        for i in range(count):
            rows = pl.ds(s * length + i * block, block)
            dmix_ref[rows, :] = dot_nt(da_ref[rows, :], wo_ref[...]).astype(BF)
        for h in range(slots):
            cols = slice(h * HEAD_DIM, (h + 1) * HEAD_DIM)
            dk_ref[...] = jnp.zeros_like(dk_ref)
            dv_ref[...] = jnp.zeros_like(dv_ref)
            for i in range(count):
                rows = pl.ds(s * length + i * block, block)
                reach = (i + 1) * block
                keys = pl.ds(s * length, reach)
                shape = (block, reach)
                seen = (
                    lax.broadcasted_iota(jnp.int32, shape, 1)
                    <= lax.broadcasted_iota(jnp.int32, shape, 0) + i * block
                )
                q = q_ref[rows, cols]
                k = k_ref[keys, cols]
                dmix = dmix_ref[rows, cols]
                scores = jnp.where(seen, dot_nt(q, k) * scale, MASKED)
                probs = jnp.exp(scores - lse_ref[rows, h : h + 1])
                dp = dot_nt(dmix, v_ref[keys, cols])
                delta = jnp.sum(probs * dp, -1, keepdims=True)
                ds = (probs * (dp - delta)).astype(BF)
                dq = dot(ds, k) * scale
                cosine = cos_ref[pl.ds(i * block, block), :]
                sine = sin_ref[pl.ds(i * block, block), :]
                dqkv_ref[rows, h * HEAD_DIM : (h + 1) * HEAD_DIM] = (
                    dq * cosine - pltpu.roll(dq, HEAD_DIM // 2, 1) * sine
                ).astype(BF)
                dk_ref[pl.ds(0, reach), :] += dot_tn(ds, q)
                dv_ref[pl.ds(0, reach), :] += dot_tn(probs.astype(BF), dmix)
            for i in range(count):
                rows = pl.ds(s * length + i * block, block)
                here = pl.ds(i * block, block)
                dk = dk_ref[here, :] * scale
                dk = dk * cos_ref[here, :] - pltpu.roll(dk, HEAD_DIM // 2, 1) * sin_ref[here, :]
                dqkv_ref[rows, span + h * HEAD_DIM : span + (h + 1) * HEAD_DIM] = dk.astype(BF)
                dqkv_ref[rows, 2 * span + h * HEAD_DIM : 2 * span + (h + 1) * HEAD_DIM] = dv_ref[here, :].astype(BF)
    gain = jnp.zeros((1, width), F32)
    for i in range(total // block):
        rows = pl.ds(i * block, block)
        d_normed = dot_nt(dqkv_ref[rows, :span], wq_ref[...])
        d_normed += dot_nt(dqkv_ref[rows, span : 2 * span], wk_ref[...])
        d_normed += dot_nt(dqkv_ref[rows, 2 * span :], wv_ref[...])
        dn_ref[rows, :] = d_normed.astype(BF)
        gain += jnp.sum(d_normed * x_ref[rows, :].astype(F32) * inv_ref[rows, :], 0, keepdims=True)
    gain_ref[...] = gain
    step = LANES * 2
    for i in range(width // step):
        cols = slice(i * step, (i + 1) * step)
        normed = (x_ref[:, cols].astype(F32) * inv_ref[...] * small_ref[gain_at : gain_at + 1, cols]).astype(BF)
        grads = dot_tn(normed, dqkv_ref[...]).astype(BF)
        dwq_ref[cols, :] = grads[:, :span]
        dwk_ref[cols, :] = grads[:, span : 2 * span]
        dwv_ref[cols, :] = grads[:, 2 * span :]


def attend_back(ranks, heads, seqs, slots, gain_at, d_att, x, inverse, small, w_slices, w_all, cosine, sine, q, k, v, lse):
    total, width = d_att.shape
    span = slots * HEAD_DIM
    shape = jax.ShapeDtypeStruct
    return vmem_call(
        functools.partial(attend_back_kernel, ranks, heads, seqs, slots, gain_at),
        [shape((total, width), BF)] + [shape((width, span), BF)] * 3 + [shape((1, width), F32)],
        d_att, x, inverse, small, *w_slices, w_all, cosine, sine, q, k, v, lse,
        scratch_shapes=[
            pltpu.VMEM((total, span), BF),
            pltpu.VMEM((total, 3 * span), BF),
            pltpu.VMEM((total // seqs, HEAD_DIM), F32),
            pltpu.VMEM((total // seqs, HEAD_DIM), F32),
            pltpu.VMEM((span, width), BF),
        ],
        name="attend_back",
    )


def experts_kernel(
    ranks, count, steps, share, n_ref, c_ref, packed_ref, wg_ref, wu_ref, wd_ref, pack_ref, sd_ref,
    n_group, c_group, w_group,
    out_ref, dx_ref, dpack_ref, dsd_ref, n_all, c_all, w_all, og_out, ou_out, od_out,
    og_ref, ou_ref, od_ref, send, recv, store,
):
    step = pl.program_id(0)
    me = lax.axis_index("expert")
    names = ranks * count
    part = c_all.shape[-1]
    moves = [
        SameExperts(w_group, w_all, send.at[1], recv.at[1]),
        Across(lambda r: n_group.at[r], n_all, send.at[0], recv.at[0]),
        Across(lambda r: c_group.at[r, pl.ds(n_ref.shape[1] - part, part)], c_all, send.at[2], recv.at[2]),
    ]

    @pl.when(step == 0)
    def _():
        meet(moves[0].peers() + moves[1].peers())
        for move in moves:
            move.start()

    @pl.when(step == min(1, steps - 1))
    def _():
        for move in moves:
            move.more()

    @pl.when(step == steps // 2)
    def _():
        for move in moves:
            move.relay()

    @pl.when(step == steps - 1)
    def _():
        for move in moves:
            move.hand_over()

    n = n_ref[...]
    c_b = c_ref[...]
    c = c_b.astype(F32)
    products = dot(n, pack_ref[...])
    gate, up = products[:, :share], products[:, share : 2 * share]
    hidden = (silu(gate) * up).astype(BF)
    out = dot(hidden, sd_ref[...])
    d_gate_s, d_up_s = swiglu_back(dot_nt(c_b, sd_ref[...]), gate, up)

    @pl.when(step == 0)
    def _():
        for ref in (dpack_ref, dsd_ref, og_ref, ou_ref, od_ref):
            ref[...] = jnp.zeros_like(ref)

    dsd_ref[...] += dot_tn(hidden, c_b)
    probs = route_probs(products, 2 * share, names)
    name = lax.broadcasted_iota(jnp.int32, probs.shape, 1)
    d_log = jnp.zeros_like(probs)
    inner = jnp.zeros((n.shape[0], 1), F32)
    dx = jnp.zeros(c.shape, F32)
    for j in range(count):
        weight = packed_ref[:, j : j + 1].astype(F32) + packed_ref[:, count + j : count + j + 1].astype(F32)
        gate = dot(n, wg_ref[j])
        up = dot(n, wu_ref[j])
        hidden = (silu(gate) * up).astype(BF)
        y = dot(hidden, wd_ref[j]).astype(BF).astype(F32)
        out += weight * y
        d_weight = weight * jnp.sum(c * y, -1, keepdims=True)
        d_log += jnp.where(name == me * count + j, d_weight, 0.0)
        inner += d_weight
        d_y = (weight * c).astype(BF)
        d_gate, d_up = swiglu_back(dot_nt(d_y, wd_ref[j]), gate, up)
        dx += dot_nt(d_gate, wg_ref[j]) + dot_nt(d_up, wu_ref[j])
        if j == count - 1:
            og_ref[...] += dot_tn(n, d_gate)
            ou_ref[...] += dot_tn(n, d_up)
            od_ref[...] += dot_tn(hidden, d_y)
    d_log = (d_log - probs * inner).astype(BF)
    rest = jnp.zeros((n.shape[0], pack_ref.shape[1] - 2 * share - names), BF)
    d_products = jnp.concatenate([d_gate_s, d_up_s, d_log, rest], -1)
    dx += dot_nt(d_products, pack_ref[...])
    dpack_ref[...] += dot_tn(n, d_products)
    out_ref[...] = out.astype(BF)
    dx_ref[...] = dx.astype(BF)

    @pl.when(step == steps - 1)
    def _():
        copies = [
            pltpu.make_async_copy(src, dst, store.at[k])
            for k, (src, dst) in enumerate(((og_ref, og_out), (ou_ref, ou_out), (od_ref, od_out)))
        ]
        for copy in copies:
            copy.start()
        for move in moves:
            move.finish()
        for copy in copies:
            copy.wait()


def experts(ranks, lanes, normed, cot, packed, turned, w_gate, w_up, w_down, pack, s_down):
    total, width = normed.shape
    count, _, hidden = w_gate.shape
    tile = 256 if total % 256 == 0 else total
    steps = total // tile
    share = s_down.shape[0]
    anywhere = pl.BlockSpec(memory_space=pl.ANY)
    dma = pltpu.SemaphoreType.DMA

    def rows(cols):
        return pl.BlockSpec((tile, cols), lambda i: (i, 0))

    def whole(a):
        zeros = (0,) * a.ndim
        return pl.BlockSpec(a.shape, lambda i: zeros, pipeline_mode=pl.Buffered(1))

    shape = jax.ShapeDtypeStruct
    fixed = (w_gate, w_up, w_down, pack, s_down)
    flops = total * width * hidden * count * 12
    return pl.pallas_call(
        functools.partial(experts_kernel, ranks, count, steps, share),
        grid=(steps,),
        in_specs=[rows(width), rows(width), rows(LANES)] + [whole(a) for a in fixed] + [anywhere] * 3,
        out_specs=[
            rows(width),
            rows(width),
            pl.BlockSpec(pack.shape, lambda i: (0, 0)),
            pl.BlockSpec((share, width), lambda i: (0, 0)),
            *([anywhere] * 6),
        ],
        out_shape=[
            shape((total, width), BF),
            shape((total, width), BF),
            shape(pack.shape, F32),
            shape((share, width), F32),
            shape((6, total // 2, width), BF),
            shape((6, total // 2, lanes), BF),
            shape((6, TURNED, total // 2), BF),
            *(shape(a.shape[1:], F32) for a in fixed[:3]),
        ],
        scratch_shapes=[
            *(pltpu.VMEM(a.shape[1:], F32) for a in fixed[:3]),
            dma((3, Across.SEMAPHORES)), dma((3, Across.SEMAPHORES)), dma((3,)),
        ],
        compiler_params=pltpu.CompilerParams(
            vmem_limit_bytes=VMEM_LIMIT, collective_id=3, has_side_effects=True
        ),
        cost_estimate=pl.CostEstimate(flops=flops, bytes_accessed=30 * 2**20, transcendentals=0),
        name="experts",
    )(normed, cot, packed, *fixed, normed, cot, turned)


def weight_of(packed, j, count):
    return packed[:, j : j + 1].astype(F32) + packed[:, count + j : count + j + 1].astype(F32)


def routed_tile(n, c, weight, w_gate, w_up, w_down, acc_gate, acc_up, acc_down):
    d_y = jnp.concatenate([(weight * part.astype(F32)).astype(BF) for part in c], -1)
    gate, up = dot(n, w_gate), dot(n, w_up)
    d_gate, d_up = swiglu_back(dot_nt(d_y, w_down), gate, up)
    hidden = (silu(gate) * up).astype(BF)
    acc_gate[...] += dot_tn(n, d_gate)
    acc_up[...] += dot_tn(n, d_up)
    acc_down[...] += dot_tn(hidden, d_y)


def weights_kernel(
    j, count, first, size, own_steps, n_own, c_own, packed_own, n_ref, ca_ref, cb_ref, packed_ref,
    wg_ref, wu_ref, wd_ref, *refs,
):
    dg_ref, du_ref, dd_ref, wg, wu, wd, acc_gate, acc_up, acc_down, load, store = refs[-11:]
    step = pl.program_id(0)
    cols = pl.ds(first, size)

    @pl.when(step == 0)
    def _():
        copies = [
            pltpu.make_async_copy(wg_ref.at[j, :, cols], wg, load.at[0]),
            pltpu.make_async_copy(wu_ref.at[j, :, cols], wu, load.at[1]),
            pltpu.make_async_copy(wd_ref.at[j, cols], wd, load.at[2]),
        ]
        for copy in copies:
            copy.start()
        for acc in (acc_gate, acc_up, acc_down):
            acc[...] = jnp.zeros_like(acc)
        for copy in copies:
            copy.wait()

    ours = step < own_steps
    parts, at = [], 0
    for ref in (ca_ref, cb_ref):
        lanes = ref.shape[-1]
        parts.append(jnp.where(ours, c_own[:, at : at + lanes], ref[...]))
        at += lanes
    theirs = [jnp.transpose(packed_ref[k].astype(F32)) for k in range(packed_ref.shape[0])]
    theirs = weight_of(jnp.concatenate(theirs, 0), j, count)
    routed_tile(
        jnp.where(ours, n_own[...], n_ref[...]),
        parts,
        jnp.where(ours, weight_of(packed_own[...], j, count), theirs),
        wg[...], wu[...], wd[...], acc_gate, acc_up, acc_down,
    )

    @pl.when(step == pl.num_programs(0) - 1)
    def _():
        copies = [
            pltpu.make_async_copy(acc_gate, dg_ref.at[j, :, cols], store.at[0]),
            pltpu.make_async_copy(acc_up, du_ref.at[j, :, cols], store.at[1]),
            pltpu.make_async_copy(acc_down, dd_ref.at[j, cols], store.at[2]),
        ]
        for copy in copies:
            copy.start()
        for copy in copies:
            copy.wait()


def expert_weights(j, first, size, tokens, weights, grads=None):
    own, others = tokens
    width = own[0].shape[1]
    count = weights[0].shape[0]
    turned = others[-1]
    others = [a.reshape(-1, a.shape[-1]) for a in others[:-1]]
    tile = min(1024, own[0].shape[0])
    own_steps = own[0].shape[0] // tile
    steps = own_steps + others[0].shape[0] // tile

    def own_rows(a):
        return pl.BlockSpec((tile, a.shape[-1]), lambda i: (jnp.minimum(i, own_steps - 1), 0))

    def rows(a):
        return pl.BlockSpec((tile, a.shape[-1]), lambda i: (jnp.maximum(i - own_steps, 0), 0))

    half = turned.shape[-1]
    if tile >= half:
        turned_spec = pl.BlockSpec((tile // half, TURNED, half), lambda i: (jnp.maximum(i - own_steps, 0), 0, 0))
    else:
        def place(i):
            k = jnp.maximum(i - own_steps, 0)
            return k // (half // tile), 0, k % (half // tile)

        turned_spec = pl.BlockSpec((1, TURNED, tile), place)

    anywhere = pl.BlockSpec(memory_space=pl.ANY)
    dma = pltpu.SemaphoreType.DMA
    before = [] if grads is None else list(grads)
    return pl.pallas_call(
        functools.partial(weights_kernel, j, count, first, size, own_steps),
        grid=(steps,),
        in_specs=[own_rows(a) for a in own] + [rows(a) for a in others] + [turned_spec]
        + [anywhere] * (3 + len(before)),
        out_specs=[anywhere] * 3,
        out_shape=[jax.ShapeDtypeStruct(w.shape, F32) for w in weights],
        scratch_shapes=[
            pltpu.VMEM((width, size), BF), pltpu.VMEM((width, size), BF), pltpu.VMEM((size, width), BF),
            pltpu.VMEM((width, size), F32), pltpu.VMEM((width, size), F32), pltpu.VMEM((size, width), F32),
            dma((3,)), dma((3,)),
        ],
        input_output_aliases={} if grads is None else {10: 0, 11: 1, 12: 2},
        compiler_params=pltpu.CompilerParams(vmem_limit_bytes=VMEM_LIMIT),
        cost_estimate=pl.CostEstimate(
            flops=steps * tile * width * size * 12, bytes_accessed=40 * 2**20, transcendentals=0
        ),
        name="expert_weights",
    )(*own, *others, turned, *weights, *before)


class Scatter:
    def __init__(self, part, pair, far, stage, mine, theirs, sems):
        self.me = lax.axis_index("expert")
        self.chips = part.shape[0]
        self.z, self.c = self.me // 2, lax.rem(self.me, 2)
        self.part, self.pair, self.far = part, pair, far
        self.stage, self.mine, self.theirs = stage, mine, theirs
        self.send, self.recv, self.local = sems
        self.near = mine is None

    def swap(self):
        twin = self.me + 1 - 2 * self.c
        return remote(self.part.at[:, 1 - self.c], self.pair, self.send.at[0], self.recv.at[0], expert=twin)

    def own(self):
        return pltpu.make_async_copy(self.part.at[:, self.c], self.stage, self.local.at[0])

    def start(self):
        self.swap().start()
        if self.near:
            self.own().start()

    def hop(self, d):
        to, source = lax.rem(self.z + d, self.chips), lax.rem(self.z + self.chips - d, self.chips)
        out = remote(
            self.stage.at[to], self.far.at[self.z], self.send.at[d], self.recv.at[d], expert=2 * to + self.c
        )
        back = remote(
            self.stage.at[to], self.far.at[source], self.send.at[d], self.recv.at[d], expert=2 * to + self.c
        )
        return out, back

    def load(self, src, dst, k):
        copy = pltpu.make_async_copy(src, dst, self.local.at[k])
        copy.start()
        return copy

    def add_pairs(self):
        if self.near:
            self.own().wait()
        self.swap().wait_recv()

        def one(i, carry):
            if self.near:
                self.stage[i] = (self.stage[i].astype(F32) + self.pair[i].astype(F32)).astype(BF)
                return carry
            copies = [self.load(self.part.at[i, self.c], self.mine, 0), self.load(self.pair.at[i], self.theirs, 1)]
            for copy in copies:
                copy.wait()
            self.stage[i] = (self.mine[...].astype(F32) + self.theirs[...].astype(F32)).astype(BF)
            return carry

        lax.fori_loop(0, self.chips, one, 0)
        for d in range(1, self.chips):
            self.hop(d)[0].start()

    def total(self):
        acc = self.stage[self.z].astype(F32)
        for d in range(1, self.chips):
            self.hop(d)[1].wait_recv()
            source = lax.rem(self.z + self.chips - d, self.chips)
            if self.near:
                acc += self.far[source].astype(F32)
            else:
                self.load(self.far.at[source], self.mine, 0).wait()
                acc += self.mine[...].astype(F32)
        return acc

    def finish(self):
        self.swap().wait_send()
        for d in range(1, self.chips):
            self.hop(d)[0].wait_send()


def tail_kernel(
    ranks, groups, heads, slots, j, count,
    dn_ref, dwq_ref, dwk_ref, dwv_ref, dpack_ref,
    n_all, ca_all, cb_all, packed_all, wg_ref, wu_ref, wd_ref, og_ref, ou_ref, od_ref,
    dn_sum, all_ref, dg_ref, du_ref, dd_ref, *refs,
):
    if dn_ref.shape[0] > 4:
        pair, far, mine, theirs = refs[:2] + refs[-2:]
        refs = refs[2:-2]
    else:
        pair, far = refs[-2:]
        mine = theirs = None
        refs = refs[:-2]
    (
        n_buf, c_buf, p_buf, wg, wu, wd, acc_gate, acc_up, acc_down, got_ref, sum_ref, stage,
        a_send, a_recv, a_local, r_send, r_recv, t_send, t_recv, g_send, g_recv, load, fetched,
    ) = refs
    me, g = lax.axis_index("expert"), lax.axis_index("dp")
    width = n_all.shape[2]
    rows = width // ranks
    tile = n_buf.shape[1]
    half = n_all.shape[1]
    per = half // tile
    steps = n_all.shape[0] * per
    parts, at = [], 0
    for ref in (ca_all, cb_all):
        parts.append(pl.ds(at, ref.shape[-1]))
        at += ref.shape[-1]
    peers = [lax.rem(g + d, groups) for d in range(1, groups)]
    others = [lax.rem(me + d, ranks) for d in range(1, ranks)]
    banks = (dwq_ref, dwk_ref, dwv_ref, dpack_ref)

    def tile_copies(sources, into):
        targets = (n_buf.at[into], p_buf.at[into], *(c_buf.at[into, :, part] for part in parts))
        return [
            pltpu.make_async_copy(src, dst, fetched.at[into, k]) for k, (src, dst) in enumerate(zip(sources, targets))
        ]

    def fetch(t, into):
        r = aligned(lax.rem(t, per), tile)
        sources = [n_all.at[t // per, r], packed_all.at[t // per, :, r], ca_all.at[t // per, r], cb_all.at[t // per, r]]
        for copy in tile_copies(sources, into):
            copy.start()

    fetch(0, 0)
    copies = [
        pltpu.make_async_copy(src, dst, load.at[k])
        for k, (src, dst) in enumerate((
            (wg_ref.at[j], wg), (wu_ref.at[j], wu), (wd_ref.at[j], wd),
            (og_ref, acc_gate), (ou_ref, acc_up), (od_ref, acc_down),
        ))
    ]
    for copy in copies:
        copy.start()
    meet([{"expert": t} for t in others] + [{"dp": t} for t in peers])
    first = Scatter(dn_ref, pair, far, stage, mine, theirs, (a_send, a_recv, a_local))
    first.start()

    def slot(s):
        return slice(s * LANES, (s + 1) * LANES)

    def has(s, i, group):
        return jnp.logical_or(group == groups - 1, head_of(s, i, ranks) < heads)

    def reduce_copy(d, s, which):
        return remote(
            banks[which].at[:, slot(s)], got_ref.at[d - 1, :, slot(s)], r_send.at[d, s], r_recv.at[d, s], dp=peers[d - 1]
        )

    for d in range(1, groups):
        for s in range(slots):
            for which in range(groups):
                ok = jnp.logical_and(peers[d - 1] == which, has(s, me, which))
                pl.when(ok)(lambda: reduce_copy(d, s, which).start())

    for copy in copies:
        copy.wait()

    def turn_copy(d, s, i, to):
        return remote(
            sum_ref.at[to, :, slot(s)], all_ref.at[g, i, :, slot(s)], t_send.at[d, s], t_recv.at[d, s], expert=to
        )

    def add_groups():
        for s in range(slots):
            def one(s=s):
                for d in range(1, groups):
                    reduce_copy(d, s, 0).wait_recv()
                for which in range(groups):
                    def add(which=which):
                        for r in range(ranks):
                            here = slice(r * rows, (r + 1) * rows)
                            acc = banks[which][here, slot(s)].astype(F32)
                            for d in range(1, groups):
                                acc += got_ref[d - 1, here, slot(s)].astype(F32)
                            sum_ref[r, :, slot(s)] = acc.astype(BF)

                    pl.when(g == which)(add)
                all_ref[g, me, :, slot(s)] = sum_ref[me, :, slot(s)]
                for d in range(1, ranks):
                    turn_copy(d, s, me, others[d - 1]).start()

            pl.when(has(s, me, g))(one)

    by_x = g + 1 - 2 * lax.rem(g, 2)
    by_y = lax.rem(g + 2, 4)
    by_both = by_y + 1 - 2 * lax.rem(by_y, 2)

    def pieces(group, h):
        mid = ranks // 2
        found = []
        for s in range(slots):
            part = all_ref.at[group, pl.ds(h * mid, mid), :, slot(s)]
            if (s + 1) * ranks <= heads:
                found.append((True, part))
                continue
            found.append((group == groups - 1, part))
            present = [i for i in range(ranks) if head_of(s, i, ranks) < heads]
            for i in present[h::2]:
                found.append((group != groups - 1, all_ref.at[group, i, :, slot(s)]))
        return found

    def spread(k, group, h, to):
        copies = []
        for n, (ok, part) in enumerate(pieces(group, h)):
            at = (k * 2 + h) * ranks + n
            copies.append((ok, remote(part, part, g_send.at[at], g_recv.at[at], dp=to)))
        return copies

    def act(copies, what):
        for ok, copy in copies:
            guarded(ok, getattr(copy, what))

    def spread_out():
        for d in range(1, ranks):
            i = lax.rem(me + ranks - d, ranks)
            for s in range(slots):
                pl.when(has(s, i, g))(lambda: turn_copy(d, s, i, others[0]).wait_recv())
        for k, h, to in ((0, 0, by_x), (1, 1, by_y), (0, 1, by_x), (1, 0, by_y)):
            act(spread(k, g, h, to), "start")

    def pass_on():
        act(spread(0, by_x, 0, by_x), "wait_recv")
        act(spread(2, by_x, 0, by_y), "start")
        act(spread(1, by_y, 1, by_y), "wait_recv")
        act(spread(3, by_y, 1, by_x), "start")

    def keep_first():
        dn_sum[...] = first.total()

    first.add_pairs()
    hooks = [None, add_groups, None, spread_out, pass_on, keep_first]

    def step(t, carry):
        now = lax.rem(t, 2)
        pl.when(t + 1 < steps)(lambda: fetch(t + 1, 1 - now))
        r = pl.ds(0, tile)
        for copy in tile_copies([n_all.at[0, r], packed_all.at[0, :, r], ca_all.at[0, r], cb_all.at[0, r]], now):
            copy.wait()
        routed_tile(
            n_buf[now], [c_buf[now]], weight_of(jnp.transpose(p_buf[now].astype(F32)), j, count),
            wg[...], wu[...], wd[...], acc_gate, acc_up, acc_down,
        )
        for k, hook in enumerate(hooks):
            if hook is not None:
                pl.when(t == k * steps // len(hooks))(hook)
        return carry

    lax.fori_loop(0, steps, step, 0)
    stores = []
    for k, (acc, out) in enumerate(((acc_gate, dg_ref), (acc_up, du_ref), (acc_down, dd_ref))):
        half_size = (wg, wu, wd)[k]
        half_size[...] = acc[...].astype(BF)
        stores.append(pltpu.make_async_copy(half_size, out, load.at[k]))
        stores[-1].start()
    first.finish()
    for d in range(1, groups):
        for s in range(slots):
            pl.when(has(s, me, peers[d - 1]))(lambda: reduce_copy(d, s, 0).wait_send())
    act(spread(0, by_x, 1, by_x), "wait_recv")
    act(spread(1, by_y, 0, by_y), "wait_recv")
    act(spread(2, by_both, 0, by_y), "wait_recv")
    act(spread(3, by_both, 1, by_x), "wait_recv")
    for k, h, to in ((0, 0, by_x), (1, 1, by_y), (0, 1, by_x), (1, 0, by_y)):
        act(spread(k, g, h, to), "wait_send")
    act(spread(2, by_x, 0, by_y), "wait_send")
    act(spread(3, by_y, 1, by_x), "wait_send")
    for d in range(1, ranks):
        for s in range(slots):
            pl.when(has(s, me, g))(lambda: turn_copy(d, s, me, others[d - 1]).wait_send())
    for copy in stores:
        copy.wait()


def tail(ranks, groups, heads, slots, j, d_normed, d_weights, others, weights, own_grads):
    half, width = others[0].shape[1:]
    count, _, hidden = weights[0].shape
    chips = ranks // 2
    total = d_normed.shape[0]
    own = total // ranks
    rows = width // ranks
    span = slots * LANES
    tile = min(512, half)
    dma = pltpu.SemaphoreType.DMA
    shape = jax.ShapeDtypeStruct
    vmem, anywhere = pl.BlockSpec(memory_space=pltpu.VMEM), pl.BlockSpec(memory_space=pl.ANY)
    block = shape((chips, own, width), BF)
    near = chips <= 4
    return pl.pallas_call(
        functools.partial(tail_kernel, ranks, groups, heads, slots, j, count),
        out_shape=[
            shape((own, width), F32), shape((groups, ranks, rows, span), BF),
            shape((width, hidden), BF), shape((width, hidden), BF), shape((hidden, width), BF),
        ]
        + [block] * (0 if near else 2),
        in_specs=[anywhere] + [vmem] * 4 + [anywhere] * 10,
        out_specs=[vmem] * 2 + [anywhere] * (3 if near else 5),
        scratch_shapes=[
            pltpu.VMEM((2, tile, width), BF), pltpu.VMEM((2, tile, width), BF), pltpu.VMEM((2, TURNED, tile), BF),
            pltpu.VMEM((width, hidden), BF), pltpu.VMEM((width, hidden), BF), pltpu.VMEM((hidden, width), BF),
            pltpu.VMEM((width, hidden), F32), pltpu.VMEM((width, hidden), F32), pltpu.VMEM((hidden, width), F32),
            pltpu.VMEM((groups - 1, width, span), BF), pltpu.VMEM((ranks, rows, span), BF),
            pltpu.VMEM((chips, own, width), BF),
            dma((chips,)), dma((chips,)), dma((2,)),
            dma((groups, slots)), dma((groups, slots)),
            dma((ranks, slots)), dma((ranks, slots)),
            dma((8 * ranks,)), dma((8 * ranks,)),
            dma((6,)), dma((2, 4)),
        ]
        + ([pltpu.VMEM((chips, own, width), BF)] * 2 if near else [pltpu.VMEM((own, width), BF)] * 2),
        compiler_params=pltpu.CompilerParams(
            vmem_limit_bytes=VMEM_LIMIT, collective_id=4, has_side_effects=True
        ),
        cost_estimate=pl.CostEstimate(flops=total * groups * width * hidden * 12, bytes_accessed=2**26, transcendentals=0),
        name="tail",
    )(
        d_normed.reshape(chips, 2, own, width), *d_weights,
        *others, *weights, *own_grads,
    )[:5]


def outputs_kernel(
    heads, slots, j, gain_at, dn_ref, out_ref, resid_ref, dres_ref, x_ref, gain_ref, all_ref, wo_ref, sd_ref,
    eg_ref, eu_ref, ed_ref, bg_ref, bu_ref, bd_ref,
    layer_ref, dx_ref, q_ref, k_ref, v_ref, o_ref, sg_ref, su_ref, dsd_ref, small_ref, dg_ref, du_ref, dd_ref,
    hg, hu, hd, wide_g, wide_u, wide_d, load, store,
):
    loads = [
        pltpu.make_async_copy(src, dst, load.at[k])
        for k, (src, dst) in enumerate(((eg_ref, hg), (eu_ref, hu), (ed_ref, hd)))
    ]
    for copy in loads:
        copy.start()
    copies = []
    for k, (src, wide, dst) in enumerate(((hg, wide_g, dg_ref), (hu, wide_u, du_ref), (hd, wide_d, dd_ref))):
        loads[k].wait()
        wide[...] = src[...].astype(F32)
        copies.append(pltpu.make_async_copy(wide, dst.at[j], store.at[k]))
        copies[-1].start()
    layer_ref[...] = (resid_ref[...] + out_ref[...].astype(F32)).astype(BF)
    x = x_ref[...].astype(F32)
    inverse = lax.rsqrt(jnp.mean(x * x, -1, keepdims=True) + EPS)
    dx_ref[...] = (dres_ref[...] + norm_back(dn_ref[...], x, inverse, gain_ref[gain_at : gain_at + 1, :])).astype(BF)
    ranks = all_ref.shape[1]
    share = sg_ref.shape[1] // ranks
    for which, ref in enumerate((q_ref, k_ref, v_ref)):
        for h in range(heads):
            s, i = next((s, i) for s in range(slots) for i in range(ranks) if head_of(s, i, ranks) == h)
            ref[:, h * LANES : (h + 1) * LANES] = all_ref[which, i, :, s * LANES : (s + 1) * LANES].astype(F32)
    last = all_ref.shape[0] - 1
    small = jnp.zeros(small_ref.shape, F32)
    for i in range(ranks):
        here = all_ref[last, i].astype(F32)
        sg_ref[:, i * share : (i + 1) * share] = here[:, :share]
        su_ref[:, i * share : (i + 1) * share] = here[:, share : 2 * share]
        small += here
    small_ref[...] = small
    o_ref[...] = wo_ref[...].astype(F32)
    dsd_ref[...] = sd_ref[...].astype(F32)
    for copy in copies:
        copy.wait()


def outputs(heads, slots, j, gain_at, share_width, arrays, last_grads, grads):
    dn, out, resid, d_resid, x, gain, everything, d_wo, d_sd = arrays
    rows, span = everything.shape[2:]
    own, width = x.shape
    shape = jax.ShapeDtypeStruct
    vmem, anywhere = pl.BlockSpec(memory_space=pltpu.VMEM), pl.BlockSpec(memory_space=pl.ANY)
    return pl.pallas_call(
        functools.partial(outputs_kernel, heads, slots, j, gain_at),
        out_shape=[shape((own, width), BF)] * 2
        + [shape((rows, width), F32)] * 4
        + [shape((rows, share_width), F32)] * 2
        + [shape(d_sd.shape, F32), shape((rows, span), F32)]
        + [shape(a.shape, F32) for a in grads],
        in_specs=[vmem] * 9 + [anywhere] * 6,
        out_specs=[vmem] * 10 + [anywhere] * 3,
        scratch_shapes=[pltpu.VMEM(a.shape, BF) for a in last_grads]
        + [pltpu.VMEM(a.shape, F32) for a in last_grads]
        + [pltpu.SemaphoreType.DMA((3,)), pltpu.SemaphoreType.DMA((3,))],
        input_output_aliases={12: 10, 13: 11, 14: 12},
        compiler_params=pltpu.CompilerParams(vmem_limit_bytes=VMEM_LIMIT),
        name="outputs",
    )(*arrays, *last_grads, *grads)


def norm_back(grad, values, inverse, gain):
    scaled = grad * gain
    inner = jnp.mean(scaled * values, -1, keepdims=True)
    return inverse * scaled - values * inverse**3 * inner


def body(
    tokens, cotangent, attn_gain, ffn_gain, w_query, w_key, w_value, w_output, router,
    shared_gate, shared_up, shared_down, expert_gate, expert_up, expert_down, expert_ids,
):
    ranks = lax.axis_size("expert")
    me = lax.axis_index("expert")
    seqs, own_pos, width = tokens.shape
    length = own_pos * ranks
    total = seqs * length
    own = seqs * own_pos
    rows = w_query.shape[0]
    heads = width // HEAD_DIM
    slots = -(-heads // ranks)
    span = slots * HEAD_DIM
    share = shared_gate.shape[1] // ranks
    names = router.shape[1]
    count = expert_gate.shape[0]

    groups = lax.axis_size("dp")

    def in_order(a):
        return a.reshape(ranks, seqs, own_pos, -1).transpose(1, 0, 2, 3).reshape(total, -1)

    def by_rank(a):
        return a.reshape(seqs, ranks, own_pos, -1).transpose(1, 0, 2, 3).reshape(total, -1)

    rest = jnp.concatenate([router, attn_gain[:, None], ffn_gain[:, None]], -1)
    edges = [0, share, 2 * share, 2 * share + names, 2 * share + names + 1]
    gain_at = edges[3] - (slots - 1) * LANES
    top = expert_ids.shape[-1]
    cosine, sine = rotary_tables(length)
    (
        group_x, group_c, w_q, w_k, w_v, w_pack, small, half_out, inverse_one, q, k, v, mixed, lse,
    ) = front(
        ranks, groups, heads, seqs, slots, gain_at, tokens.reshape(own, width), cotangent.reshape(own, width),
        expert_ids.reshape(own, top), w_query, w_key, w_value, shared_gate, shared_up, rest, w_output,
        cosine, sine,
    )
    group_c = group_c.reshape(total, -1)
    gain_two = small[gain_at + 1 : gain_at + 2]
    units = width // LANES
    c_last = max(units // 5, 1) * LANES
    c_first = width - c_last
    resid, normed_two, all_mixed, all_out, packed, turned, all_ca = project(
        ranks, groups, heads, slots, count, top, edges[2], c_first, group_x, by_rank(mixed), half_out, small, w_pack, group_c
    )
    layer_part, d_normed_part, d_pack, d_s_down, all_n, all_cb, all_w, *own_grads = experts(
        ranks, c_last, normed_two, group_c, packed, turned, expert_gate, expert_up, expert_down, w_pack, shared_down
    )
    every = ((normed_two, group_c, packed), (all_n, all_ca, all_cb, all_w))
    banks = (expert_gate, expert_up, expert_down)
    hidden = expert_gate.shape[-1]
    cut = hidden * 4 // 7 if hidden % (7 * LANES) == 0 else hidden // 2

    def after(late, *earlier):
        return lax.optimization_barrier((late, earlier))[0]

    def scatter(partial):
        return lax.psum_scatter(partial, "expert", scatter_dimension=0, tiled=True)

    grads = expert_weights(0, 0, cut, every, banks)
    d_normed_two, grads = lax.optimization_barrier((scatter(d_normed_part), grads))
    d_normed_two = d_normed_two.astype(F32)
    inverse_two = lax.rsqrt(jnp.mean(resid * resid, -1, keepdims=True) + EPS)
    ffn_gain_part = jnp.sum(d_normed_two * resid * inverse_two, 0)
    d_out = cotangent.reshape(own, width).astype(F32)
    d_resid = d_out + norm_back(d_normed_two, resid, inverse_two, gain_two)
    own_att = d_resid.astype(BF)
    d_att = lax.all_gather(own_att, "expert", axis=0, tiled=True)
    grads = expert_weights(0, cut, hidden - cut, after(every, own_att), banks, grads)
    d_att, grads = lax.optimization_barrier((d_att, grads))

    d_normed_part, d_wq, d_wk, d_wv, attn_gain_part = attend_back(
        ranks, heads, seqs, slots, gain_at, in_order(d_att), in_order(group_x), inverse_one, small,
        (w_q, w_k, w_v), all_out, cosine, sine, q, k, v, lse
    )
    column = jnp.arange(span)[None, :]
    d_pack = jnp.where(column == edges[3], attn_gain_part.reshape(width, 1), d_pack)
    d_pack = jnp.where(column == edges[4], ffn_gain_part[:, None], d_pack).astype(BF)
    own_mixed = lax.dynamic_slice_in_dim(all_mixed, me * rows, rows, 1)
    d_wo_rows = dot_tn(own_mixed, d_att).astype(BF)
    d_wo_rows, d_sd_rows = lax.psum((d_wo_rows, d_s_down.astype(BF)), "dp")
    dn_sum, all_grads, *last_grads = tail(
        ranks, groups, heads, slots, 1, by_rank(d_normed_part), (d_wq, d_wk, d_wv, d_pack), every[1], banks, own_grads
    )
    layer_output, input_grad, g_q, g_k, g_v, g_o, g_sg, g_su, g_sd, small, g_gate, g_up, g_down = outputs(
        heads, slots, 1, gain_at, ranks * share,
        (dn_sum, scatter(after(layer_part, d_att)), resid, d_resid, tokens.reshape(own, width), small, all_grads, d_wo_rows, d_sd_rows),
        last_grads, grads,
    )
    g_r = small[:, edges[2] : edges[3]]
    g_one = small[:, edges[3]]
    g_two = small[:, edges[4]]
    return (
        layer_output.reshape(tokens.shape), input_grad.reshape(tokens.shape),
        g_one, g_two, g_q, g_k, g_v, g_o, g_r, g_sg, g_su, g_sd, g_gate, g_up, g_down,
    )


def solution(mesh):
    row = P("expert", None)
    experts_spec = P("expert", None, None)
    tokens_spec = P("dp", "expert", None)
    return jax.shard_map(
        body,
        mesh=mesh,
        in_specs=(tokens_spec, tokens_spec, P("expert"), P("expert"))
        + (row,) * 8
        + (experts_spec,) * 3
        + (P(("dp", "expert"), None, None),),
        out_specs=(tokens_spec, tokens_spec, P("expert"), P("expert")) + (row,) * 8 + (experts_spec,) * 3,
        check_vma=False,
    )
```
